32 devices in a mesh: dp: 4 (over y, x), row: 4 (over z), col: 2 (over core).
Axes of the slice: x: 2, y: 2, z: 4, core: 2. Of those that a mesh axis runs over, the one named last changes fastest.
Arguments:
- inputs: bfloat16 [8192, 1024], P(('dp', 'col'), 'row'), may hold values from -6 to 6
- segments: int32 [4, 2048], P('dp'), may hold values from 0 to 7, never falling along the last dimension, each value on 1 to 1537 neighbouring positions
- ln_gain: bfloat16 [1024], P('row'), may hold values from 0.099609375 to 1.8984375
- ln_bias: bfloat16 [1024], P('row'), may hold values from -1.75 to 1.75
- w_qkv: bfloat16 [1024, 3, 1024], P('row', None, 'col'), may hold values from -0.1875 to 0.1875
- b_qkv: bfloat16 [3, 1024], P(None, 'col'), may hold values from -0.3125 to 0.3125
- w_out: bfloat16 [1024, 1024], P('col', 'row'), may hold values from -0.75 to 0.75
- w_up: bfloat16 [1024, 4096], P('row', 'col'), may hold values from -0.1875 to 0.1875
- b_up: bfloat16 [4096], P('col'), may hold values from -1.75 to 1.75
- w_down: bfloat16 [4096, 1024], P('col', 'row'), may hold values from -0.09375 to 0.09375
- out_bias: bfloat16 [1024], P('row'), may hold values from -1.75 to 1.75
- cotangent: bfloat16 [8192, 1024], P(('dp', 'col'), 'row'), may hold values from -8 to 8
Outputs:
- layer_out: bfloat16 [8192, 1024], P(('dp', 'col'), 'row')
- grad_inputs: float32 [8192, 1024], P(('dp', 'col'), 'row')
- grad_ln_gain: float32 [1024], P('row')
- grad_ln_bias: float32 [1024], P('row')
- grad_w_qkv: float32 [1024, 3, 1024], P('row', None, 'col')
- grad_b_qkv: float32 [3, 1024], P(None, 'col')
- grad_w_out: float32 [1024, 1024], P('col', 'row')
- grad_w_up: float32 [1024, 4096], P('row', 'col')
- grad_b_up: float32 [4096], P('col')
- grad_w_down: float32 [4096, 1024], P('col', 'row')
- grad_out_bias: float32 [1024], P('row')
The draws below stay inside these ranges and needn't reach their ends.
Inputs may be any that keep to these rules, and one draw needn't show every extreme that they name: `segments`: in each sequence the document numbers start at 0 and never fall; every document holds 1 to 1537 tokens and one holds exactly 1537.
All inputs are finite; a program needn't handle non-finite values.
Results may differ from the reference program's by a relative error of at most 0.03.
Values may be sent and summed in bfloat16 or wider, within the bound.
A program may use at most 128 MiB of HBM per device.

```python
import math
import jax
import jax.numpy as jnp
import numpy as np
from jax import lax

D = 1024
H = 16
HD = 64
ROT = 16
FF = 4096
SEQ_LEN = 2048
NSEG = 8
SEQS = 4
TOKENS = 8192


def spiked(array, rng, source, target, shards_of, factor):
    owner, partner = [(jnp.arange(array.shape[axis_at]) // (array.shape[axis_at] // shards_of)).reshape([-1 if axis == axis_at else 1 for axis in range(array.ndim)]) for axis_at in (source, target)]
    chosen = jax.random.permutation(rng, shards_of)[partner]
    strong = (owner == chosen) | (owner == (partner + shards_of // 2) % shards_of)
    return jnp.where(strong, factor * array, array)


def shard_levels(own_key, shape, cuts, smallest, top_value):
    def one(dim, shards_of):
        steps = jax.random.uniform(jax.random.fold_in(jax.random.fold_in(own_key, 6), dim), (shards_of,), jnp.float32, smallest / len(cuts), top_value / len(cuts))
        return jnp.repeat(jnp.exp(steps), shape[dim] // shards_of).reshape((-1,) + (1,) * (len(shape) - dim - 1))

    level = one(*cuts[0])
    for cut in cuts[1:]:
        level = level * one(*cut)
    return level


def split_up(amount, total, reach, slope):
    portions = [(1 << 20) // math.isqrt(grade ** slope) + 1 for grade in range(2, amount + 1)]
    rest, counts = total - reach - (amount - 1), [1] * (amount - 1)
    while rest > 0:
        candidates = [i for i in range(amount - 1) if counts[i] < reach]
        pool, left = sum([portions[i] for i in candidates]), rest
        for i in candidates:
            extra = min(reach - counts[i], max(1, left * portions[i] // pool), rest)
            counts[i] = counts[i] + extra
            rest = rest - extra
    return np.array([reach] + counts)


def uneven_parts(stream_key, number_of, total, reach, lean):
    if number_of == 2:
        one = jax.random.randint(stream_key, (), max(1, total - reach), min(reach, total - 1) + 1)
        return jnp.stack([one, total - one])
    tallies = jnp.asarray(split_up(number_of, total, reach, lean), jnp.int32)
    twos = (number_of - 1) // 2
    source_of, sink = tallies[1:1 + 2 * twos:2], tallies[2:2 + 2 * twos:2]
    room = jnp.minimum(source_of - 1, reach - sink)
    moved = jax.random.randint(jax.random.fold_in(stream_key, 1), (twos,), 0, 1 << 20) % (room + 1)
    tallies = tallies.at[1:1 + 2 * twos:2].set(source_of - moved).at[2:2 + 2 * twos:2].set(sink + moved)
    return tallies[jax.random.permutation(jax.random.fold_in(stream_key, 2), number_of)]


def scatter_about(rng, extent, width, bound, pieces=(), kind=jnp.bfloat16):
    factor_of = shard_levels(rng, extent, pieces, -0.22, 0.18) if pieces else 1.0
    entries = jax.random.normal(rng, extent, jnp.float32) * width * factor_of
    return jnp.minimum(jnp.maximum(entries, -bound), bound).astype(kind)


def bell_draw_with(rng, extent, scale, most, split, heavy, held_as=jnp.bfloat16):
    array = scale * jax.random.normal(rng, extent, jnp.float32)
    if split:
        array = array * shard_levels(rng, extent, split, -0.22, 0.18)
    return jnp.clip(spiked(array, jax.random.fold_in(rng, 3), *heavy), -most, most).astype(held_as)


def setup_inputs(seed: int = 0) -> dict:
    key_of = jax.random.split(jax.random.key(seed), 13)
    inputs = scatter_about(key_of[0], (TOKENS, D), 1.0, 6.0, ((0, 8), (1, 4)))
    segments = jax.vmap(lambda own: jnp.searchsorted(jnp.cumsum(uneven_parts(own, NSEG, SEQ_LEN, 3 * SEQ_LEN // 4 + 1, 2)), jnp.arange(SEQ_LEN), side="right"))(jax.random.split(key_of[1], SEQS)).reshape((SEQS, SEQ_LEN)).astype(jnp.int32)
    ln_gain = jnp.clip(1.0 + 0.18 * jax.random.normal(key_of[2], (D,), jnp.float32), 0.099609375, 1.8984375).astype(jnp.bfloat16)
    ln_bias = scatter_about(key_of[3], (D,), 0.3, 1.75, ((0, 4),))
    w_qkv = scatter_about(key_of[4], (D, 3, D), D ** -0.5, 0.1875, ((0, 4), (2, 2)))
    b_qkv = scatter_about(key_of[5], (3, D), 0.05, 0.3125, ((1, 2),))
    w_out = scatter_about(key_of[6], (D, D), (D // 16) ** -0.5, 0.75, ((0, 2), (1, 4)))
    w_up = scatter_about(key_of[7], (D, FF), D ** -0.5, 0.1875, ((0, 4), (1, 2)))
    b_up = scatter_about(key_of[8], (FF,), 0.3, 1.75, ((0, 2),))
    w_down = scatter_about(key_of[9], (FF, D), FF ** -0.5, 0.09375, ((0, 2), (1, 4)))
    out_bias = scatter_about(key_of[10], (D,), 0.3, 1.75, ((0, 4),))
    cotangent = bell_draw_with(key_of[11], (TOKENS, D), 1.0, 8.0, ((0, 8), (1, 4)), (0, 1, 8, 2.0))
    return {"inputs": inputs, "segments": segments, "ln_gain": ln_gain, "ln_bias": ln_bias, "w_qkv": w_qkv, "b_qkv": b_qkv, "w_out": w_out, "w_up": w_up, "b_up": b_up, "w_down": w_down, "out_bias": out_bias, "cotangent": cotangent}


EPSILON = 1e-05
MASKED = -1000000000.0

@jax.custom_vjp
def low(v):
    return lax.optimization_barrier(v.astype(jnp.bfloat16)).astype(jnp.float32)

@jax.custom_vjp
def low_back(v):
    return v

def low_keep(v):
    return (low(v), None)

def low_pass(kept, grad):
    return (grad,)

def back_keep(v):
    return (v, None)

def back_low(kept, grad):
    return (low(grad),)
low.defvjp(low_keep, low_pass)
low_back.defvjp(back_keep, back_low)

def doc_positions(labels):
    token_index = jnp.arange(labels.shape[1], dtype=jnp.int32)
    flags = jnp.concatenate([jnp.ones((labels.shape[0], 1), dtype=jnp.bool_), labels[:, 1:] != labels[:, :-1]], 1)
    starts = lax.cummax(jnp.where(flags, token_index[None, :], 0), axis=1)
    return token_index[None, :] - starts

def rotate(tensor_in, positions):
    half_rot = ROT // 2
    inverse = 10000.0 ** (-(jnp.arange(half_rot, dtype=jnp.float32) * 2.0 / ROT))
    angles = positions.astype(jnp.float32)[:, None] * inverse[None, :]
    cosines = jnp.cos(angles)[:, None, :]
    sine_vals = jnp.sin(angles)[:, None, :]
    first_half = tensor_in[..., :half_rot]
    second_half = tensor_in[..., half_rot:ROT]
    rest_dims = tensor_in[..., ROT:]
    return jnp.concatenate([first_half * cosines - second_half * sine_vals, second_half * cosines + first_half * sine_vals, rest_dims], -1)

def attend(query, key_rows, value_rows, segments, score_scale):
    seq_count = segments.shape[0]
    query_size = min(512, SEQ_LEN)
    block_count = SEQ_LEN // query_size
    token_index = jnp.arange(SEQ_LEN, dtype=jnp.int32)
    shaped = (seq_count, SEQ_LEN, H, HD)

    def one_sequence(packed):
        seq_query, seq_keys, seq_values, seq_labels = packed

        def one_block(block_start):
            q_rows = lax.dynamic_slice_in_dim(seq_query, block_start, query_size, 0)
            q_labels = lax.dynamic_slice_in_dim(seq_labels, block_start, query_size, 0)
            q_index = block_start + jnp.arange(query_size, dtype=jnp.int32)
            scores = jnp.einsum('qhd,khd->hqk', q_rows, seq_keys, precision=lax.Precision.HIGHEST) * score_scale
            scores = low_back(scores)
            allowed = (q_labels[:, None] == seq_labels[None, :]) & (token_index[None, :] <= q_index[:, None])
            scores = jnp.where(allowed[None], scores, MASKED)
            row_max = lax.optimization_barrier(jnp.max(scores, -1, keepdims=True))
            log_total = row_max + jnp.log(lax.optimization_barrier(jnp.sum(jnp.exp(scores - row_max), -1, keepdims=True)))
            weights = jnp.exp(scores - log_total)
            return jnp.einsum('hqk,khd->qhd', low(weights), seq_values, precision=lax.Precision.HIGHEST)
        starts = jnp.arange(block_count, dtype=jnp.int32) * query_size
        return lax.map(jax.checkpoint(one_block), starts).reshape(SEQ_LEN, H, HD)
    return lax.map(jax.checkpoint(one_sequence), (query.reshape(shaped), key_rows.reshape(shaped), value_rows.reshape(shaped), segments))

def reference(inputs, segments, ln_gain, ln_bias, w_qkv, b_qkv, w_out, w_up, b_up, w_down, out_bias, cotangent):
    positions = doc_positions(segments).reshape(-1)
    row_count = inputs.shape[0]
    score_scale = 1.0 / math.sqrt(HD)
    highest = lax.Precision.HIGHEST

    def forward(tokens_in, gain_in, bias_in, qkv_w, qkv_b, proj_w, up_w, up_b, down_w, final_b):
        row_mean = lax.optimization_barrier(jnp.mean(tokens_in, -1, keepdims=True))
        row_var = lax.optimization_barrier(jnp.mean(tokens_in * tokens_in, -1, keepdims=True)) - row_mean * row_mean
        centred = (tokens_in - row_mean) * lax.rsqrt(row_var + EPSILON)
        normed = low(centred * gain_in + bias_in)
        projected = jnp.dot(normed, qkv_w.reshape(D, 3 * D), precision=highest) + qkv_b.reshape(3 * D)
        query_lin = low_back(projected[:, :D]).reshape(row_count, H, HD)
        key_lin = low_back(projected[:, D:2 * D]).reshape(row_count, H, HD)
        value_rows = low_back(low(projected[:, 2 * D:])).reshape(row_count, H, HD)
        query = low(rotate(query_lin, positions))
        key_rows = low(rotate(key_lin, positions))
        up_lin = low_back(jnp.dot(normed, up_w, precision=highest) + up_b)
        activated = low(jax.nn.gelu(up_lin, approximate=False))
        attended = attend(query, key_rows, value_rows, segments, score_scale).reshape(row_count, D)
        attended = low_back(low(attended))
        return tokens_in + jnp.dot(attended, proj_w, precision=highest) + jnp.dot(activated, down_w, precision=highest) + final_b
    layer_out, pullback = jax.vjp(forward, inputs.astype(jnp.float32), ln_gain.astype(jnp.float32), ln_bias.astype(jnp.float32), w_qkv.astype(jnp.float32), b_qkv.astype(jnp.float32), w_out.astype(jnp.float32), w_up.astype(jnp.float32), b_up.astype(jnp.float32), w_down.astype(jnp.float32), out_bias.astype(jnp.float32))
    grads = pullback(cotangent.astype(jnp.float32))
    return (layer_out.astype(jnp.bfloat16), grads[0], grads[1], grads[2], grads[3], grads[4], grads[5], grads[6], grads[7], grads[8], grads[9])
```

```python
import math

import jax
import jax.numpy as jnp
from jax import lax
from jax.experimental import pallas as pl
from jax.experimental.pallas import tpu as pltpu
from jax.sharding import PartitionSpec as P

D = 1024
HD = 64
ROT = 16
SEQ_LEN = 2048
EPSILON = 1e-05
MASKED = -1000000000.0
BF = jnp.bfloat16
F32 = jnp.float32
NT = (((1,), (1,)), ((), ()))
NN = (((1,), (0,)), ((), ()))
TN = (((0,), (0,)), ((), ()))


def dot(a, b, dims=NN):
    return lax.dot_general(a, b, dims, preferred_element_type=F32)


BQ = 512
BK = 256


def lane_mask(head, rows):
    lane = lax.broadcasted_iota(jnp.int32, (rows, 128), 1)
    return (lane >= head * HD) & (lane < (head + 1) * HD)


def attend_forward_kernel(first_ref, q_ref, k_ref, v_ref, rng_ref, out_ref, raw_ref, lse_ref, vt_ref):
    vt_ref[...] = v_ref[...].astype(F32).T.astype(BF)

    def q_step(qb, _):
        q0 = pl.multiple_of(qb * BQ, BQ)
        qs = q_ref[pl.ds(q0, BQ), :] * BF(1.0 / math.sqrt(HD))
        heads = [jnp.where(lane_mask(h, BQ), qs, BF(0)) for h in range(2)]
        start = rng_ref[0:1, pl.ds(q0, BQ)]
        span = rng_ref[1:2, pl.ds(q0, BQ)]

        def k_step(kb, carry):
            k0 = pl.multiple_of(kb * BK, BK)
            kk = k_ref[pl.ds(k0, BK), :]
            kidx = lax.broadcasted_iota(jnp.int32, (BK, BQ), 0) + k0 - start
            ok = (kidx >= 0) & (kidx <= span)
            new = []
            for h in range(2):
                m, l, acc = carry[h]
                s = jnp.where(ok, dot(kk, heads[h], NT), MASKED)
                m2 = jnp.maximum(m, jnp.max(s, 0, keepdims=True))
                p = jnp.exp(s - m2)
                c = jnp.exp(m - m2)
                l = l * c + jnp.sum(p, 0, keepdims=True)
                vt = vt_ref[h * HD : (h + 1) * HD, pl.ds(k0, BK)]
                acc = acc * c + dot(vt, p.astype(BF))
                new.append((m2, l, acc))
            return tuple(new)

        init = tuple(
            (jnp.full((1, BQ), -1e30, F32), jnp.zeros((1, BQ), F32), jnp.zeros((HD, BQ), F32))
            for _ in range(2)
        )
        last = (qb + 1) * (BQ // BK)
        res = lax.fori_loop(first_ref[qb], last, k_step, init)
        for h in range(2):
            m, l, acc = res[h]
            raw_ref[h * HD : (h + 1) * HD, pl.ds(q0, BQ)] = acc / l
            lse_ref[h : h + 1, pl.ds(q0, BQ)] = m + jnp.log(l)
        out_ref[pl.ds(q0, BQ), :] = raw_ref[:, pl.ds(q0, BQ)].T.astype(BF)
        return 0

    lax.fori_loop(0, SEQ_LEN // BQ, q_step, 0)


def vmem():
    return pl.BlockSpec(memory_space=pltpu.VMEM)


def smem():
    return pl.BlockSpec(memory_space=pltpu.SMEM)


def attend_forward(first, q, k, v, rng):
    n = q.shape[0]
    return pl.pallas_call(
        attend_forward_kernel,
        name="attend_forward",
        out_shape=(
            jax.ShapeDtypeStruct((n, 128), BF),
            jax.ShapeDtypeStruct((128, n), F32),
            jax.ShapeDtypeStruct((8, n), F32),
        ),
        in_specs=[smem()] + [vmem()] * 4,
        out_specs=(vmem(),) * 3,
        scratch_shapes=[pltpu.VMEM((128, n), BF)],
        compiler_params=pltpu.CompilerParams(vmem_limit_bytes=48 * 2**20),
    )(first, q, k, v, rng)


def rope(x, c, s1, s2):
    return x * c + pltpu.roll(x, 120, 1) * s1 + pltpu.roll(x, 8, 1) * s2


def rope_back(g, c, s1, s2):
    return g * c - pltpu.roll(g, 120, 1) * s1 - pltpu.roll(g, 8, 1) * s2


def attend_backward_kernel(
    last_ref, q_ref, k_ref, v_ref, do_ref, raw_ref, lse_ref, rng_ref, c_ref, s1_ref, s2_ref,
    out_ref, kt_ref, dqt_ref, delta_ref,
):
    n = q_ref.shape[0]
    kt_ref[...] = k_ref[...].astype(F32).T.astype(BF)
    dqt_ref[...] = jnp.zeros_like(dqt_ref)

    def delta_step(i, _):
        at = pl.ds(pl.multiple_of(i * BQ, BQ), BQ)
        prod = do_ref[at, :].astype(F32).T * raw_ref[:, at]
        for h in range(2):
            delta_ref[h : h + 1, at] = jnp.sum(prod[h * HD : (h + 1) * HD], 0, keepdims=True)
        return 0

    lax.fori_loop(0, n // BQ, delta_step, 0)

    def k_step(kb, _):
        k0 = pl.multiple_of(kb * BK, BK)
        kk = k_ref[pl.ds(k0, BK), :]
        vv = v_ref[pl.ds(k0, BK), :]

        def q_step(qb, carry):
            dk, dv = carry
            q0 = pl.multiple_of(qb * BQ, BQ)
            at = pl.ds(q0, BQ)
            qs = q_ref[at, :] * BF(1.0 / math.sqrt(HD))
            do = do_ref[at, :]
            kidx = lax.broadcasted_iota(jnp.int32, (BK, BQ), 0) + k0 - rng_ref[0:1, at]
            ok = (kidx >= 0) & (kidx <= rng_ref[1:2, at])
            for h in range(2):
                qh = jnp.where(lane_mask(h, BQ), qs, BF(0))
                doh = jnp.where(lane_mask(h, BQ), do, BF(0))
                s = jnp.where(ok, dot(kk, qh, NT), MASKED)
                p = jnp.exp(s - lse_ref[h : h + 1, at])
                ds = (p * (dot(vv, doh, NT) - delta_ref[h : h + 1, at])).astype(BF)
                dv = dv + dot(p.astype(BF), doh)
                dk = dk + dot(ds, qh)
                rows = slice(h * HD, (h + 1) * HD)
                dqt_ref[rows, at] += dot(kt_ref[rows, pl.ds(k0, BK)], ds)
            return dk, dv

        zero = jnp.zeros((BK, 128), F32)
        dk, dv = lax.fori_loop(k0 // BQ, last_ref[kb], q_step, (zero, zero))
        at = pl.ds(k0, BK)
        out_ref[at, 128:256] = rope_back(dk, c_ref[at, :], s1_ref[at, :], s2_ref[at, :]).astype(BF)
        out_ref[at, 256:384] = dv.astype(BF)
        return 0

    lax.fori_loop(0, n // BK, k_step, 0)

    def finish(i, _):
        at = pl.ds(pl.multiple_of(i * BQ, BQ), BQ)
        dq = dqt_ref[:, at].T * (1.0 / math.sqrt(HD))
        out_ref[at, 0:128] = rope_back(dq, c_ref[at, :], s1_ref[at, :], s2_ref[at, :]).astype(BF)
        return 0

    lax.fori_loop(0, n // BQ, finish, 0)


def attend_backward(last, q, k, v, do, raw, lse, rng, c, s1, s2):
    n = q.shape[0]
    return pl.pallas_call(
        attend_backward_kernel,
        name="attend_backward",
        out_shape=jax.ShapeDtypeStruct((n, 384), BF),
        in_specs=[smem()] + [vmem()] * 10,
        out_specs=vmem(),
        scratch_shapes=[
            pltpu.VMEM((128, n), BF),
            pltpu.VMEM((128, n), F32),
            pltpu.VMEM((8, n), F32),
        ],
        compiler_params=pltpu.CompilerParams(vmem_limit_bytes=56 * 2**20),
    )(last, q, k, v, do, raw, lse, rng, c, s1, s2)


def rope_tables(pos):
    half = ROT // 2
    freq = 10000.0 ** (-(jnp.arange(half, dtype=F32) * 2.0 / ROT))
    ang = pos.astype(F32)[None, :] * freq[:, None]
    cs, sn = lax.optimization_barrier((jnp.cos(ang), jnp.sin(ang)))
    cs, sn = cs.T, sn.T
    n = pos.shape[0]
    one = jnp.ones((n, HD - ROT), F32)
    zero = jnp.zeros((n, HD - ROT), F32)
    z8 = jnp.zeros((n, half), F32)
    c = jnp.concatenate([cs, cs, one] * 2, 1)
    s1 = jnp.concatenate([-sn, z8, zero] * 2, 1)
    s2 = jnp.concatenate([z8, sn, zero] * 2, 1)
    return c, s1, s2


def per_device_sliced(
    inputs, segments, ln_gain, ln_bias, w_qkv, b_qkv, w_out, w_up, b_up, w_down, out_bias, cotangent
):
    nrow = lax.axis_size("row")
    row = lax.axis_index("row")
    dpart = inputs.shape[1]
    hcols = w_qkv.shape[2] // nrow
    fcols = w_up.shape[1] // nrow
    toks = segments.shape[1]
    half = inputs.shape[0]

    seg = segments[0]
    idx = jnp.arange(toks, dtype=jnp.int32)
    start = jnp.sum(
        jnp.where(seg[None, :] < seg[:, None], 1, 0), 1, dtype=jnp.int32
    )
    pos = idx - start
    c, s1, s2 = rope_tables(pos)
    rng = jnp.concatenate([start[None], pos[None], jnp.zeros((6, toks), jnp.int32)], 0)
    first = start[::BQ] // BK
    ends = jnp.sum(jnp.where(start[None, :] <= idx[BK - 1 :: BK, None], 1, 0), 1, dtype=jnp.int32)
    last = (ends + BQ - 1) // BQ

    xg = lax.all_gather(lax.all_gather(inputs, "row"), "col", axis=1, tiled=True)
    cg = lax.all_gather(lax.all_gather(cotangent, "row"), "col", axis=1, tiled=True)
    gb = lax.all_gather(jnp.stack([ln_gain, ln_bias]).astype(F32), "row")
    w1s = jnp.concatenate(
        [
            w_qkv.reshape(dpart, 3, nrow, hcols).transpose(2, 0, 1, 3).reshape(nrow, dpart, 3 * hcols),
            w_up.reshape(dpart, nrow, fcols).transpose(1, 0, 2),
        ],
        2,
    )
    w2s = jnp.concatenate(
        [w_out.reshape(nrow, hcols, dpart), w_down.reshape(nrow, fcols, dpart)], 1
    )
    w1 = lax.all_to_all(w1s, "row", 0, 0)
    w2 = lax.all_to_all(w2s, "row", 0, 0)
    b1 = jnp.concatenate(
        [
            lax.dynamic_slice_in_dim(b_qkv, row * hcols, hcols, 1).reshape(-1),
            lax.dynamic_slice_in_dim(b_up, row * fcols, fcols, 0),
        ]
    ).astype(F32)

    xf = xg.astype(F32)
    mean = jnp.sum(xf, (0, 2)) / D
    var = jnp.sum(xf * xf, (0, 2)) / D - mean * mean
    inv = lax.rsqrt(var + EPSILON)
    xhat = (xf - mean[None, :, None]) * inv[None, :, None]
    normed = (xhat * gb[:, 0:1] + gb[:, 1:2]).astype(BF)
    nd = normed.transpose(1, 0, 2).reshape(toks, D)
    proj = dot(nd, w1.reshape(D, -1)) + b1
    h3 = 3 * hcols

    def rp(x):
        return (
            x * c + jnp.roll(x, -8, 1) * s1 + jnp.roll(x, 8, 1) * s2
        ).astype(BF)

    q, k, v = rp(proj[:, :hcols]), rp(proj[:, hcols : 2 * hcols]), proj[:, 2 * hcols : h3].astype(BF)
    up = proj[:, h3:]
    phi = 0.5 * (1.0 + lax.erf(up * (1.0 / math.sqrt(2.0))))
    act = (up * phi).astype(BF)
    gp = phi + up * jnp.exp(-0.5 * up * up) * (1.0 / math.sqrt(2.0 * math.pi))
    attended, raw, lse = attend_forward(first, q, k, v, rng)

    joined = jnp.concatenate([attended, act], 1)
    col = lax.axis_index("col")
    outp = jnp.einsum("tk,bkn->btn", joined, w2, preferred_element_type=F32).astype(BF)
    outp = lax.psum_scatter(outp, "row", scatter_dimension=0)
    outp = lax.psum_scatter(outp, "col", scatter_dimension=0, tiled=True)
    layer_out = (inputs.astype(F32) + outp.astype(F32) + out_bias.astype(F32)).astype(BF)
    gob = jnp.sum(cotangent.astype(F32), 0)
    cgd = cg.transpose(1, 0, 2).reshape(toks, D)
    w2d = w2.transpose(1, 0, 2).reshape(-1, D)
    g2 = dot(joined, cgd, TN)
    dj = dot(cgd, w2d, NT)
    datt = dj[:, :hcols].astype(BF)
    dup = (dj[:, hcols:] * gp).astype(BF)
    dproj = attend_backward(last, q, k, v, datt, raw, lse, rng, c, s1, s2)
    d1 = jnp.concatenate([dproj, dup], 1)
    g1 = dot(nd, d1, TN)
    gb1 = jnp.sum(d1.astype(F32), 0)
    dn = jnp.einsum("tn,bkn->btk", d1, w1, preferred_element_type=F32).astype(BF)
    dn = lax.psum_scatter(dn, "row", scatter_dimension=0)
    dn = lax.psum_scatter(dn, "col", scatter_dimension=0, tiled=True).astype(F32)
    myx = lax.dynamic_slice_in_dim(mean, col * half, half), lax.dynamic_slice_in_dim(inv, col * half, half)
    xh = (inputs.astype(F32) - myx[0][:, None]) * myx[1][:, None]
    dc = dn * ln_gain.astype(F32)
    st = lax.psum((jnp.sum(dc, 1), jnp.sum(dc * xh, 1)), "row")
    grad_inputs = myx[1][:, None] * (
        dc - st[0][:, None] / D - xh * st[1][:, None] / D
    ) + cotangent.astype(F32)
    ng = lax.psum((jnp.sum(dn * xh, 0), jnp.sum(dn, 0), gob), ("dp", "col"))

    g1 = lax.psum(g1.astype(BF), "dp").reshape(nrow, dpart, -1)
    g2 = lax.psum(g2.astype(BF), "dp").reshape(-1, nrow, dpart).transpose(1, 0, 2)
    g1 = lax.all_to_all(g1, "row", 0, 0).astype(F32)
    g2 = lax.all_to_all(g2, "row", 0, 0).astype(F32)
    gb1 = lax.all_gather(lax.psum(gb1, "dp"), "row")
    grad_w_qkv = g1[:, :, :h3].reshape(nrow, dpart, 3, hcols).transpose(1, 2, 0, 3).reshape(dpart, 3, -1)
    grad_w_up = g1[:, :, h3:].transpose(1, 0, 2).reshape(dpart, -1)
    grad_w_out = g2[:, :hcols].reshape(-1, dpart)
    grad_w_down = g2[:, hcols:].reshape(-1, dpart)
    grad_b_qkv = gb1[:, :h3].reshape(nrow, 3, hcols).transpose(1, 0, 2).reshape(3, -1)
    grad_b_up = gb1[:, h3:].reshape(-1)
    return (
        layer_out, grad_inputs, ng[0], ng[1], grad_w_qkv, grad_b_qkv,
        grad_w_out, grad_w_up, grad_b_up, grad_w_down, ng[2],
    )


FLOOR_INIT = -1e30


def doc_positions(labels):
    token_index = jnp.arange(labels.shape[1], dtype=jnp.int32)
    flags = jnp.concatenate(
        [jnp.ones((labels.shape[0], 1), dtype=jnp.bool_), labels[:, 1:] != labels[:, :-1]], 1
    )
    starts = lax.cummax(jnp.where(flags, token_index[None, :], 0), axis=1)
    return token_index[None, :] - starts


def rotate(tensor_in, positions):
    half_rot = ROT // 2
    inverse = 10000.0 ** (-(jnp.arange(half_rot, dtype=jnp.float32) * 2.0 / ROT))
    angles = positions.astype(jnp.float32)[:, None] * inverse[None, :]
    cosines = jnp.cos(angles)[:, None, :]
    sine_vals = jnp.sin(angles)[:, None, :]
    first_half = tensor_in[..., :half_rot]
    second_half = tensor_in[..., half_rot:ROT]
    rest_dims = tensor_in[..., ROT:]
    return jnp.concatenate(
        [
            first_half * cosines - second_half * sine_vals,
            second_half * cosines + first_half * sine_vals,
            rest_dims,
        ],
        -1,
    )


def slice_rows(array_in, first_row, row_count, axis_num=0):
    return lax.dynamic_slice_in_dim(array_in, first_row, row_count, axis_num)


def put_rows(array_in, update, first_row, axis_num=0):
    return lax.dynamic_update_slice_in_dim(array_in, update, first_row, axis_num)


def block_pairs(query_blocks, key_blocks):
    q_list = jnp.repeat(jnp.arange(query_blocks, dtype=jnp.int32), key_blocks)
    k_list = jnp.tile(jnp.arange(key_blocks, dtype=jnp.int32), query_blocks)
    return (q_list, k_list)


def per_device_general(
    inputs, segments, ln_gain, ln_bias, w_qkv, b_qkv, w_out, w_up, b_up, w_down, out_bias, cotangent
):
    local_rows, feature_cols = inputs.shape
    part_count = lax.axis_size("row")
    row_index = lax.axis_index("row")
    head_cols = w_qkv.shape[2]
    head_count = head_cols // HD
    group_seqs = segments.shape[0]
    all_rows = group_seqs * SEQ_LEN
    span = all_rows // part_count
    query_blocks = span // span
    score_scale = 1.0 / math.sqrt(HD)
    labels = (segments + (jnp.arange(group_seqs, dtype=jnp.int32) * SEQ_LEN)[:, None]).reshape(-1)
    positions = doc_positions(segments).reshape(-1)
    token_index = jnp.arange(all_rows, dtype=jnp.int32)
    my_labels = slice_rows(labels, row_index * span, span)
    my_index = slice_rows(token_index, row_index * span, span)
    my_positions = slice_rows(positions, row_index * span, span)
    float_in = inputs.astype(jnp.float32)
    ln_sums = lax.psum((jnp.sum(float_in, 1), jnp.sum(float_in * float_in, 1)), "row")
    row_mean = ln_sums[0] / D
    row_var = ln_sums[1] / D - row_mean * row_mean
    inv_std = lax.rsqrt(row_var + EPSILON)
    centred = (float_in - row_mean[:, None]) * inv_std[:, None]
    normed = (centred * ln_gain.astype(jnp.float32) + ln_bias.astype(jnp.float32)).astype(
        jnp.bfloat16
    )
    gathered_hidden = lax.all_gather(normed, "col", axis=0, tiled=True)
    first_weights = jnp.concatenate([w_qkv.reshape(feature_cols, 3 * head_cols), w_up], 1)
    first_bias = jnp.concatenate(
        [b_qkv.reshape(3 * head_cols).astype(jnp.float32), b_up.astype(jnp.float32)]
    )
    first_out = (
        lax.psum_scatter(
            jnp.dot(
                slice_rows(gathered_hidden, jnp.int32(0), lax.axis_size("row") * span),
                first_weights,
                preferred_element_type=jnp.float32,
            ).astype(jnp.bfloat16),
            "row",
            scatter_dimension=0,
            tiled=True,
        ).astype(jnp.float32)
        + first_bias
    )

    def rotate_mine(tensor_in):
        return rotate(tensor_in, my_positions)

    query_lin = first_out[:, :head_cols].reshape(span, head_count, HD)
    key_lin = first_out[:, head_cols : 2 * head_cols].reshape(span, head_count, HD)
    query = rotate_mine(query_lin).astype(jnp.bfloat16)
    key_rows = rotate_mine(key_lin).astype(jnp.bfloat16)
    value_rows = (
        first_out[:, 2 * head_cols : 3 * head_cols]
        .reshape(span, head_count, HD)
        .astype(jnp.bfloat16)
    )
    up_lin = first_out[:, 3 * head_cols :]
    activated = jax.nn.gelu(up_lin, approximate=False).astype(jnp.bfloat16)

    def over_keys(fold_step, initial):
        return fold_step(
            initial,
            (
                lax.all_gather(key_rows, "row", axis=0, tiled=True),
                lax.all_gather(value_rows, "row", axis=0, tiled=True),
            ),
            jnp.int32(0),
        )

    def key_setup(pieces, first_row):
        row_count = pieces[0].shape[0]
        piece_labels = slice_rows(labels, first_row, row_count)
        piece_index = slice_rows(token_index, first_row, row_count)
        return (row_count, span, piece_labels, piece_index)

    def block_live(piece_labels, piece_index, key_size, q_block, k_block):
        q_labels = slice_rows(my_labels, q_block * span, span)
        q_index = slice_rows(my_index, q_block * span, span)
        k_labels = slice_rows(piece_labels, k_block * key_size, key_size)
        k_index = slice_rows(piece_index, k_block * key_size, key_size)
        return (
            (jnp.max(q_index) >= jnp.min(k_index))
            & (jnp.min(q_labels) <= jnp.max(k_labels))
            & (jnp.min(k_labels) <= jnp.max(q_labels))
        )

    def block_scores(pieces, piece_labels, piece_index, key_size, q_block, k_block):
        q_start = q_block * span
        k_start = k_block * key_size
        q_labels = slice_rows(my_labels, q_start, span)
        q_index = slice_rows(my_index, q_start, span)
        k_labels = slice_rows(piece_labels, k_start, key_size)
        k_index = slice_rows(piece_index, k_start, key_size)
        q_block_rows = slice_rows(query, q_start, span)
        k_block_rows = slice_rows(pieces[0], k_start, key_size)
        v_block_rows = slice_rows(pieces[1], k_start, key_size)
        scores = (
            jnp.einsum(
                "qhd,khd->hqk", q_block_rows, k_block_rows, preferred_element_type=jnp.float32
            )
            * score_scale
        )
        allowed = (q_labels[:, None] == k_labels[None, :]) & (k_index[None, :] <= q_index[:, None])
        scores = jnp.where(allowed[None], scores, MASKED)
        return (q_start, k_start, scores, q_block_rows, k_block_rows, v_block_rows)

    def forward_piece(running, pieces, first_row):
        row_count, key_size, piece_labels, piece_index = key_setup(pieces, first_row)
        q_list, k_list = block_pairs(query_blocks, row_count // key_size)

        def forward_pair_step(current, pair_ids):
            q_block, k_block = pair_ids

            def update(inner_state):
                row_max, row_sum, row_acc = inner_state
                q_start, k_start, scores, q_block_rows, k_block_rows, v_block_rows = block_scores(
                    pieces, piece_labels, piece_index, key_size, q_block, k_block
                )
                old_max = slice_rows(row_max, q_start, span, 1)
                new_max = jnp.maximum(old_max, jnp.max(scores, -1))
                weights = jnp.exp(scores - new_max[..., None])
                keep_part = jnp.exp(old_max - new_max)
                new_sum = slice_rows(row_sum, q_start, span, 1) * keep_part + jnp.sum(weights, -1)
                added = jnp.einsum(
                    "hqk,khd->hqd",
                    weights.astype(jnp.bfloat16),
                    v_block_rows,
                    preferred_element_type=jnp.float32,
                )
                new_acc = slice_rows(row_acc, q_start, span, 1) * keep_part[..., None] + added
                return (
                    put_rows(row_max, new_max, q_start, 1),
                    put_rows(row_sum, new_sum, q_start, 1),
                    put_rows(row_acc, new_acc, q_start, 1),
                )

            def forward_unchanged(inner_state):
                return inner_state

            is_live = block_live(piece_labels, piece_index, key_size, q_block, k_block)
            return (lax.cond(is_live, update, forward_unchanged, current), None)

        result, _ = lax.scan(forward_pair_step, running, (q_list, k_list))
        return result

    forward_init = (
        jnp.full((head_count, span), FLOOR_INIT, jnp.float32),
        jnp.zeros((head_count, span), jnp.float32),
        jnp.zeros((head_count, span, HD), jnp.float32),
    )
    row_max, row_sum, row_acc = over_keys(forward_piece, forward_init)
    log_total = row_max + jnp.log(row_sum)
    attention_raw = jnp.transpose(row_acc / row_sum[..., None], (1, 0, 2)).reshape(span, head_cols)
    attended = attention_raw.astype(jnp.bfloat16)
    joined = jnp.concatenate(
        (
            lax.all_gather(attended, "row", axis=0, tiled=True),
            lax.all_gather(activated, "row", axis=0, tiled=True),
        ),
        1,
    )
    second_weights = jnp.concatenate([w_out, w_down], 0)
    partial_out = lax.psum_scatter(
        jnp.dot(
            slice_rows(joined, jnp.int32(0), lax.axis_size("col") * local_rows),
            second_weights,
            preferred_element_type=jnp.float32,
        ).astype(jnp.bfloat16),
        "col",
        scatter_dimension=0,
        tiled=True,
    ).astype(jnp.float32)
    layer_out = (float_in + partial_out + out_bias.astype(jnp.float32)).astype(jnp.bfloat16)
    grad_full = lax.all_gather(cotangent, "col", axis=0, tiled=True)
    grad_out_bias = jnp.sum(grad_full, 0, dtype=jnp.float32)
    grad_second = lax.dot_general(
        joined, grad_full, (((0,), (0,)), ((), ())), preferred_element_type=jnp.float32
    )
    branch_back = lax.psum_scatter(
        lax.dot_general(
            slice_rows(grad_full, jnp.int32(0), lax.axis_size("row") * span),
            second_weights,
            (((1,), (1,)), ((), ())),
            preferred_element_type=jnp.float32,
        ).astype(jnp.bfloat16),
        "row",
        scatter_dimension=0,
        tiled=True,
    ).astype(jnp.float32)
    d_attended = branch_back[:, :head_cols].astype(jnp.bfloat16)
    d_activated = branch_back[:, head_cols:]
    _, gelu_back = jax.vjp(lambda tensor_in: jax.nn.gelu(tensor_in, approximate=False), up_lin)
    d_up = gelu_back(d_activated)[0].astype(jnp.bfloat16)
    d_out_heads = d_attended.reshape(span, head_count, HD)
    row_delta = jnp.transpose(
        jnp.sum((d_attended.astype(jnp.float32) * attention_raw).reshape(span, head_count, HD), -1)
    )

    def backward_piece(running, pieces, first_row):
        d_query_acc, d_key_all, d_value_all = running
        row_count, key_size, piece_labels, piece_index = key_setup(pieces, first_row)
        q_list, k_list = block_pairs(query_blocks, row_count // key_size)
        zero_keys = jnp.zeros((row_count, head_count, HD), jnp.float32)

        def backward_pair_step(current, pair_ids):
            q_block, k_block = pair_ids

            def update(inner_state):
                d_query_run, d_key_run, d_value_run = inner_state
                q_start, k_start, scores, q_block_rows, k_block_rows, v_block_rows = block_scores(
                    pieces, piece_labels, piece_index, key_size, q_block, k_block
                )
                probs_full = jnp.exp(scores - slice_rows(log_total, q_start, span, 1)[..., None])
                d_out_block = slice_rows(d_out_heads, q_start, span)
                d_probs = jnp.einsum(
                    "qhd,khd->hqk", d_out_block, v_block_rows, preferred_element_type=jnp.float32
                )
                d_scores = (
                    probs_full * (d_probs - slice_rows(row_delta, q_start, span, 1)[..., None])
                ).astype(jnp.bfloat16)
                q_added = (
                    jnp.einsum(
                        "hqk,khd->qhd", d_scores, k_block_rows, preferred_element_type=jnp.float32
                    )
                    * score_scale
                )
                k_added = (
                    jnp.einsum(
                        "hqk,qhd->khd", d_scores, q_block_rows, preferred_element_type=jnp.float32
                    )
                    * score_scale
                )
                v_added = jnp.einsum(
                    "hqk,qhd->khd",
                    probs_full.astype(jnp.bfloat16),
                    d_out_block,
                    preferred_element_type=jnp.float32,
                )
                return (
                    put_rows(
                        d_query_run, slice_rows(d_query_run, q_start, span) + q_added, q_start
                    ),
                    put_rows(
                        d_key_run, slice_rows(d_key_run, k_start, key_size) + k_added, k_start
                    ),
                    put_rows(
                        d_value_run, slice_rows(d_value_run, k_start, key_size) + v_added, k_start
                    ),
                )

            def backward_unchanged(inner_state):
                return inner_state

            is_live = block_live(piece_labels, piece_index, key_size, q_block, k_block)
            return (lax.cond(is_live, update, backward_unchanged, current), None)

        scanned, _ = lax.scan(
            backward_pair_step, (d_query_acc, zero_keys, zero_keys), (q_list, k_list)
        )
        d_query_acc, key_part, value_part = scanned
        d_key_all = put_rows(d_key_all, key_part, first_row)
        d_value_all = put_rows(d_value_all, value_part, first_row)
        return (d_query_acc, d_key_all, d_value_all)

    backward_init = (
        jnp.zeros((span, head_count, HD), jnp.float32),
        jnp.zeros((all_rows, head_count, HD), jnp.float32),
        jnp.zeros((all_rows, head_count, HD), jnp.float32),
    )
    d_query_rot, d_key_total, d_value_total = over_keys(backward_piece, backward_init)
    d_key_rot, d_value_mine = (
        lax.psum_scatter(
            d_key_total.reshape(all_rows, head_cols).astype(jnp.bfloat16),
            "row",
            scatter_dimension=0,
            tiled=True,
        ).astype(jnp.float32),
        lax.psum_scatter(
            d_value_total.reshape(all_rows, head_cols).astype(jnp.bfloat16),
            "row",
            scatter_dimension=0,
            tiled=True,
        ).astype(jnp.float32),
    )
    _, query_back = jax.vjp(rotate_mine, query_lin)
    _, key_back = jax.vjp(rotate_mine, key_lin)
    d_query_lin = query_back(d_query_rot)[0].reshape(span, head_cols).astype(jnp.bfloat16)
    d_key_lin = (
        key_back(d_key_rot.reshape(span, head_count, HD))[0]
        .reshape(span, head_cols)
        .astype(jnp.bfloat16)
    )
    d_first = jnp.concatenate([d_query_lin, d_key_lin, d_value_mine.astype(jnp.bfloat16), d_up], 1)
    d_first_full = lax.all_gather(d_first, "row", axis=0, tiled=True)
    grad_first_bias = jnp.sum(d_first_full, 0, dtype=jnp.float32)
    grad_first = lax.dot_general(
        gathered_hidden, d_first_full, (((0,), (0,)), ((), ())), preferred_element_type=jnp.float32
    )
    d_normed = lax.psum_scatter(
        lax.dot_general(
            slice_rows(d_first_full, jnp.int32(0), lax.axis_size("col") * local_rows),
            first_weights,
            (((1,), (1,)), ((), ())),
            preferred_element_type=jnp.float32,
        ).astype(jnp.bfloat16),
        "col",
        scatter_dimension=0,
        tiled=True,
    ).astype(jnp.float32)
    d_centred = d_normed * ln_gain.astype(jnp.float32)
    grad_stats = lax.psum((jnp.sum(d_centred, 1), jnp.sum(d_centred * centred, 1)), "row")
    grad_inputs = inv_std[:, None] * (
        d_centred - grad_stats[0][:, None] / D - centred * grad_stats[1][:, None] / D
    ) + cotangent.astype(jnp.float32)
    summed = (
        lax.psum(grad_first.astype(jnp.bfloat16), "dp").astype(jnp.float32),
        lax.psum(grad_second.astype(jnp.bfloat16), "dp").astype(jnp.float32),
        lax.psum(grad_first_bias.astype(jnp.bfloat16), "dp").astype(jnp.float32),
        lax.psum(grad_out_bias.astype(jnp.bfloat16), "dp").astype(jnp.float32),
    )
    norm_grads = lax.psum((jnp.sum(d_normed * centred, 0), jnp.sum(d_normed, 0)), ("dp", "col"))
    grad_w_qkv = summed[0][:, : 3 * head_cols].reshape(feature_cols, 3, head_cols)
    grad_w_up = summed[0][:, 3 * head_cols :]
    grad_w_out = summed[1][:head_cols]
    grad_w_down = summed[1][head_cols:]
    grad_b_qkv = summed[2][: 3 * head_cols].reshape(3, head_cols)
    grad_b_up = summed[2][3 * head_cols :]
    return (
        layer_out,
        grad_inputs,
        norm_grads[0],
        norm_grads[1],
        grad_w_qkv,
        grad_b_qkv,
        grad_w_out,
        grad_w_up,
        grad_b_up,
        grad_w_down,
        summed[3],
    )


def solution(mesh):
    placed = (
        P(("dp", "col"), "row"),
        P("dp", None),
        P("row"),
        P("row"),
        P("row", None, "col"),
        P(None, "col"),
        P("col", "row"),
        P("row", "col"),
        P("col"),
        P("col", "row"),
        P("row"),
        P(("dp", "col"), "row"),
    )
    size = dict(mesh.shape)
    sliced = (size["dp"], size["row"], size["col"]) == (4, 4, 2)
    return jax.shard_map(
        per_device_sliced if sliced else per_device_general,
        mesh=mesh,
        in_specs=placed,
        out_specs=(
            P(("dp", "col"), "row"),
            P(("dp", "col"), "row"),
            P("row"),
            P("row"),
            P("row", None, "col"),
            P(None, "col"),
            P("col", "row"),
            P("row", "col"),
            P("col"),
            P("col", "row"),
            P("row"),
        ),
        check_vma=False,
    )
```

```python
import math

import jax
import jax.numpy as jnp
from jax import lax
from jax.experimental import pallas as pl
from jax.experimental.pallas import tpu as pltpu
from jax.sharding import PartitionSpec as P

D = 1024
HD = 64
ROT = 16
SEQ_LEN = 2048
EPSILON = 1e-05
MASKED = -1000000000.0
BF = jnp.bfloat16
F32 = jnp.float32
NT = (((1,), (1,)), ((), ()))
NN = (((1,), (0,)), ((), ()))
TN = (((0,), (0,)), ((), ()))


def dot(a, b, dims=NN):
    return lax.dot_general(a, b, dims, preferred_element_type=F32)


BQ = 512
BK = 256


def lane_mask(head, rows):
    lane = lax.broadcasted_iota(jnp.int32, (rows, 128), 1)
    return (lane >= head * HD) & (lane < (head + 1) * HD)


def attend_forward_kernel(first_ref, q_ref, k_ref, v_ref, rng_ref, out_ref, raw_ref, lse_ref, vt_ref):
    vt_ref[...] = v_ref[...].astype(F32).T.astype(BF)

    def q_step(qb, _):
        q0 = pl.multiple_of(qb * BQ, BQ)
        qs = q_ref[pl.ds(q0, BQ), :] * BF(1.0 / math.sqrt(HD))
        heads = [jnp.where(lane_mask(h, BQ), qs, BF(0)) for h in range(2)]
        start = rng_ref[0:1, pl.ds(q0, BQ)]
        span = rng_ref[1:2, pl.ds(q0, BQ)]

        def k_step(kb, carry):
            k0 = pl.multiple_of(kb * BK, BK)
            kk = k_ref[pl.ds(k0, BK), :]
            kidx = lax.broadcasted_iota(jnp.int32, (BK, BQ), 0) + k0 - start
            ok = (kidx >= 0) & (kidx <= span)
            new = []
            for h in range(2):
                m, l, acc = carry[h]
                s = jnp.where(ok, dot(kk, heads[h], NT), MASKED)
                m2 = jnp.maximum(m, jnp.max(s, 0, keepdims=True))
                p = jnp.exp(s - m2)
                c = jnp.exp(m - m2)
                l = l * c + jnp.sum(p, 0, keepdims=True)
                vt = vt_ref[h * HD : (h + 1) * HD, pl.ds(k0, BK)]
                acc = acc * c + dot(vt, p.astype(BF))
                new.append((m2, l, acc))
            return tuple(new)

        init = tuple(
            (jnp.full((1, BQ), -1e30, F32), jnp.zeros((1, BQ), F32), jnp.zeros((HD, BQ), F32))
            for _ in range(2)
        )
        last = (qb + 1) * (BQ // BK)
        res = lax.fori_loop(first_ref[qb], last, k_step, init)
        for h in range(2):
            m, l, acc = res[h]
            raw_ref[h * HD : (h + 1) * HD, pl.ds(q0, BQ)] = acc / l
            lse_ref[h : h + 1, pl.ds(q0, BQ)] = m + jnp.log(l)
        out_ref[pl.ds(q0, BQ), :] = raw_ref[:, pl.ds(q0, BQ)].T.astype(BF)
        return 0

    lax.fori_loop(0, SEQ_LEN // BQ, q_step, 0)


def vmem():
    return pl.BlockSpec(memory_space=pltpu.VMEM)


def smem():
    return pl.BlockSpec(memory_space=pltpu.SMEM)


def attend_forward(first, q, k, v, rng):
    n = q.shape[0]
    return pl.pallas_call(
        attend_forward_kernel,
        name="attend_forward",
        out_shape=(
            jax.ShapeDtypeStruct((n, 128), BF),
            jax.ShapeDtypeStruct((128, n), F32),
            jax.ShapeDtypeStruct((8, n), F32),
        ),
        in_specs=[smem()] + [vmem()] * 4,
        out_specs=(vmem(),) * 3,
        scratch_shapes=[pltpu.VMEM((128, n), BF)],
        compiler_params=pltpu.CompilerParams(vmem_limit_bytes=48 * 2**20),
    )(first, q, k, v, rng)


def rope(x, c, s1, s2):
    return x * c + pltpu.roll(x, 120, 1) * s1 + pltpu.roll(x, 8, 1) * s2


def unrope(gt, cosv, sinv):
    rows = []
    for h in range(2):
        o = h * HD
        a, b = gt[o : o + 8], gt[o + 8 : o + 16]
        rows += [a * cosv + b * sinv, b * cosv - a * sinv, gt[o + 16 : o + HD]]
    return jnp.concatenate(rows, 0)


def attend_backward_kernel(
    last_ref, q_ref, k_ref, v_ref, do_ref, raw_ref, lse_ref, rng_ref, cs_ref,
    out_ref, kt_ref, dqt_ref, delta_ref,
):
    n = q_ref.shape[0]
    kt_ref[...] = k_ref[...].astype(F32).T.astype(BF)
    dqt_ref[...] = jnp.zeros_like(dqt_ref)

    def delta_step(i, _):
        at = pl.ds(pl.multiple_of(i * BQ, BQ), BQ)
        prod = do_ref[at, :].astype(F32).T * raw_ref[:, at]
        for h in range(2):
            delta_ref[h : h + 1, at] = jnp.sum(prod[h * HD : (h + 1) * HD], 0, keepdims=True)
        return 0

    lax.fori_loop(0, n // BQ, delta_step, 0)

    def k_step(kb, _):
        k0 = pl.multiple_of(kb * BK, BK)
        kk = k_ref[pl.ds(k0, BK), :]
        vv = v_ref[pl.ds(k0, BK), :]

        def q_step(qb, carry):
            dk, dv = carry
            q0 = pl.multiple_of(qb * BQ, BQ)
            at = pl.ds(q0, BQ)
            qs = q_ref[at, :] * BF(1.0 / math.sqrt(HD))
            do = do_ref[at, :]
            kidx = lax.broadcasted_iota(jnp.int32, (BK, BQ), 0) + k0 - rng_ref[0:1, at]
            ok = (kidx >= 0) & (kidx <= rng_ref[1:2, at])
            for h in range(2):
                qh = jnp.where(lane_mask(h, BQ), qs, BF(0))
                doh = jnp.where(lane_mask(h, BQ), do, BF(0))
                s = jnp.where(ok, dot(kk, qh, NT), MASKED)
                p = jnp.exp(s - lse_ref[h : h + 1, at])
                ds = (p * (dot(vv, doh, NT) - delta_ref[h : h + 1, at])).astype(BF)
                dv = dv + dot(p.astype(BF), doh)
                dk = dk + dot(ds, qh)
                rows = slice(h * HD, (h + 1) * HD)
                dqt_ref[rows, at] += dot(kt_ref[rows, pl.ds(k0, BK)], ds)
            return dk, dv

        zero = jnp.zeros((BK, 128), F32)
        dk, dv = lax.fori_loop(k0 // BQ, last_ref[kb], q_step, (zero, zero))
        at = pl.ds(k0, BK)
        out_ref[at, 128:256] = unrope(dk.T, cs_ref[0:8, at], cs_ref[8:16, at]).T.astype(BF)
        out_ref[at, 256:384] = dv.astype(BF)
        return 0

    lax.fori_loop(0, n // BK, k_step, 0)

    def finish(i, _):
        at = pl.ds(pl.multiple_of(i * BQ, BQ), BQ)
        dq = dqt_ref[:, at] * (1.0 / math.sqrt(HD))
        out_ref[at, 0:128] = unrope(dq, cs_ref[0:8, at], cs_ref[8:16, at]).T.astype(BF)
        return 0

    lax.fori_loop(0, n // BQ, finish, 0)


def attend_backward(last, q, k, v, do, raw, lse, rng, cs):
    n = q.shape[0]
    return pl.pallas_call(
        attend_backward_kernel,
        name="attend_backward",
        out_shape=jax.ShapeDtypeStruct((n, 384), BF),
        in_specs=[smem()] + [vmem()] * 8,
        out_specs=vmem(),
        scratch_shapes=[
            pltpu.VMEM((128, n), BF),
            pltpu.VMEM((128, n), F32),
            pltpu.VMEM((8, n), F32),
        ],
        compiler_params=pltpu.CompilerParams(vmem_limit_bytes=56 * 2**20),
    )(last, q, k, v, do, raw, lse, rng, cs)


MESH = pl.DeviceIdType.MESH
TC = 256
XC = 2


def hbm():
    return pl.BlockSpec(memory_space=pl.ANY)


def remote(src, dst, send, recv, dev):
    return pltpu.make_async_remote_copy(
        src_ref=src, dst_ref=dst, send_sem=send, recv_sem=recv, device_id=dev, device_id_type=MESH
    )


def where():
    return lax.axis_index("dp"), lax.axis_index("row"), lax.axis_index("col")


def greet(dp, row, col, rows=4, dps=4):
    bar = pltpu.get_barrier_semaphore()
    count = 0
    for d in range(1, dps):
        pl.semaphore_signal(bar, inc=1, device_id=(dp ^ d, row, col), device_id_type=MESH)
        count += 1
    for d in range(1, rows):
        pl.semaphore_signal(bar, inc=1, device_id=(dp, lax.rem(row + d, rows), col), device_id_type=MESH)
        count += 1
    pl.semaphore_signal(bar, inc=1, device_id=(dp, row, 1 - col), device_id_type=MESH)
    pl.semaphore_wait(bar, count + 1)


class LineGather:
    def __init__(self, own, full, sems, pos, half):
        self.own, self.full, self.pos, self.half = own, full, pos, half
        (self.su, self.sd, self.ru, self.rd, self.ss, self.rs, self.loc) = sems
        self.piece = half // XC

    def at(self, block, k):
        dp, row, col = self.pos
        start = pl.multiple_of(col * self.half + k * self.piece, self.piece)
        return self.full.at[block, pl.ds(start, self.piece)]

    def sib_at(self, block, k):
        dp, row, col = self.pos
        start = pl.multiple_of((1 - col) * self.half + k * self.piece, self.piece)
        return self.full.at[block, pl.ds(start, self.piece)]

    def src(self, step, block, k):
        return self.own.at[pl.ds(k * self.piece, self.piece)] if step == 0 else self.at(block, k)

    def up(self, step, k):
        dp, row, col = self.pos
        return remote(
            self.src(step, row - step, k), self.at(row - step, k),
            self.su.at[step, k], self.ru.at[step, k], (dp, row + 1, col),
        )

    def down(self, step, k):
        dp, row, col = self.pos
        return remote(
            self.src(step, row + step, k), self.at(row + step, k),
            self.sd.at[step, k], self.rd.at[step, k], (dp, row - 1, col),
        )

    def sib(self, step, sign, k):
        dp, row, col = self.pos
        i = step + 3 * (sign < 0)
        block = row - sign * step
        return remote(
            self.src(step, block, k), self.at(block, k),
            self.ss.at[i, k], self.rs.at[i, k], (dp, row, 1 - col),
        )

    def local(self):
        dp, row, col = self.pos
        start = pl.multiple_of(col * self.half, self.half)
        return pltpu.make_async_copy(self.own, self.full.at[row, pl.ds(start, self.half)], self.loc)

    def start(self):
        dp, row, col = self.pos
        for k in range(XC):
            @pl.when(row < 3)
            def _():
                self.up(0, k).start()

            @pl.when(row > 0)
            def _():
                self.down(0, k).start()
        for k in range(XC):
            self.sib(0, 1, k).start()
        self.local().start()

    def step(self, s):
        dp, row, col = self.pos
        for k in range(XC):
            @pl.when(row >= s)
            def _():
                pltpu.make_async_copy(self.at(row - s, k), self.at(row - s, k), self.ru.at[s - 1, k]).wait()

                @pl.when(row < 3)
                def _():
                    self.up(s, k).start()

                self.sib(s, 1, k).start()

            @pl.when(row + s <= 3)
            def _():
                pltpu.make_async_copy(self.at(row + s, k), self.at(row + s, k), self.rd.at[s - 1, k]).wait()

                @pl.when(row > 0)
                def _():
                    self.down(s, k).start()

                self.sib(s, -1, k).start()

    def sib_wait(self, s, sign):
        dp, row, col = self.pos
        block = row - sign * s
        i = s + 3 * (sign < 0)
        for k in range(XC):
            pltpu.make_async_copy(self.sib_at(block, k), self.sib_at(block, k), self.rs.at[i, k]).wait()

    def arrived(self):
        dp, row, col = self.pos
        self.local().wait()
        self.sib_wait(0, 1)
        for s in range(1, 4):
            @pl.when(row >= s)
            def _():
                self.sib_wait(s, 1)

            @pl.when(row + s <= 3)
            def _():
                self.sib_wait(s, -1)

    def drain(self):
        dp, row, col = self.pos
        for k in range(XC):
            self.sib(0, 1, k).wait_send()
            for s in range(0, 3):
                @pl.when((row >= s) & (row < 3))
                def _():
                    self.up(s, k).wait_send()

                @pl.when((row + s <= 3) & (row > 0))
                def _():
                    self.down(s, k).wait_send()
            for s in range(1, 4):
                @pl.when(row >= s)
                def _():
                    self.sib(s, 1, k).wait_send()

                @pl.when(row + s <= 3)
                def _():
                    self.sib(s, -1, k).wait_send()


def line_sems():
    dma = pltpu.SemaphoreType.DMA
    return [dma((4, XC))] * 4 + [dma((7, XC))] * 2 + [dma]


class WeightGather:
    def __init__(self, packed, full, sems, pos):
        self.packed, self.full, self.pos = packed, full, pos
        self.sz, self.rz, self.sp, self.rp, self.loc = sems
        self.rows = packed.shape[1] // 4

    def part(self, ref, block, quarter):
        return ref.at[block, pl.ds(pl.multiple_of(quarter * self.rows, self.rows), self.rows)]

    def along(self, d):
        dp, row, col = self.pos
        target = lax.rem(row + d, 4)
        return remote(
            self.part(self.packed, target, dp), self.part(self.full, row, dp),
            self.sz.at[d], self.rz.at[d], (dp, target, col),
        )

    def across(self, d, e):
        dp, row, col = self.pos
        block = lax.rem(row + 4 - d, 4)
        return remote(
            self.part(self.full, block, dp), self.part(self.full, block, dp),
            self.sp.at[d, e], self.rp.at[d, e], (dp ^ e, row, col),
        )

    def local(self):
        dp, row, col = self.pos
        return pltpu.make_async_copy(self.packed.at[row], self.full.at[row], self.loc)

    def start(self):
        for d in (2, 1, 3):
            self.along(d).start()
        self.local().start()

    def forward(self):
        dp, row, col = self.pos
        for d in (1, 3, 2):
            block = lax.rem(row + 4 - d, 4)
            part = self.part(self.full, block, dp)
            pltpu.make_async_copy(part, part, self.rz.at[d]).wait()
            for e in (3, 1, 2):
                self.across(d, e).start()

    def arrived(self):
        dp, row, col = self.pos
        self.local().wait()
        for d in (1, 3, 2):
            block = lax.rem(row + 4 - d, 4)
            for e in (1, 2, 3):
                part = self.part(self.full, block, dp ^ e)
                pltpu.make_async_copy(part, part, self.rp.at[d, e]).wait()

    def drain(self):
        for d in (1, 2, 3):
            self.along(d).wait_send()
            for e in (1, 2, 3):
                self.across(d, e).wait_send()


def weight_sems():
    dma = pltpu.SemaphoreType.DMA
    return [dma((4,))] * 2 + [dma((4, 4))] * 2 + [dma]


def project_kernel(
    x, w1s, w2s, gb, seg, b1,
    q_o, k_o, v_o, act_o, gp_o, nrm_o, w1_o, w2_o, stat_o, cs_o, rng_o,
    xf, w1, w2, gbs, q_v, k_v, v_v, act_v, gp_v, nrm_v, stat_v, cs_v, rng_v, c_v, s1_v, s2_v,
    *sems,
):
    pos = where()
    dp, row, col = pos
    toks = seg.shape[1]
    half = toks // 2
    line = LineGather(x, xf, sems[:7], pos, half)
    g1 = WeightGather(w1s, w1, sems[7:12], pos)
    g2 = WeightGather(w2s, w2, sems[12:17], pos)
    gs, gr, out_sem = sems[17:20]
    greet(dp, row, col)
    g1.start()
    line.start()

    def gain_copy(d):
        return remote(gb, gbs.at[row], gs.at[d], gr.at[d], (dp, lax.rem(row + d, 4), col))

    for d in (1, 2, 3):
        gain_copy(d).start()
    own_gain = pltpu.make_async_copy(gb, gbs.at[row], gr.at[0])
    own_gain.start()
    g2.start()

    labels = seg[...]
    start = jnp.zeros_like(labels)
    for d in range(1, 8):
        below = jnp.sum((labels == d - 1).astype(F32), 1, keepdims=True).astype(jnp.int32)
        start = start + jnp.where(labels >= d, below, 0)
    index = lax.broadcasted_iota(jnp.int32, labels.shape, 1)
    place = index - start
    rng_v[0:1, :] = start
    rng_v[1:2, :] = place
    rng_v[2:8, :] = jnp.zeros((6, toks), jnp.int32)
    power = lax.broadcasted_iota(jnp.int32, (8, 1), 0).astype(F32) * (-2.0 * math.log(10000.0) / ROT)
    ang = place.astype(F32) * jnp.exp(power)
    cs_v[0:8, :] = jnp.cos(ang)
    cs_v[8:16, :] = jnp.sin(ang)

    def table_step(i, _):
        at = pl.ds(pl.multiple_of(i * TC, TC), TC)
        cosv, sinv = cs_v[0:8, at], cs_v[8:16, at]
        one = jnp.ones((HD - ROT, TC), F32)
        zero = jnp.zeros((HD - ROT, TC), F32)
        z8 = jnp.zeros((8, TC), F32)
        c_v[at, :] = jnp.concatenate([cosv, cosv, one] * 2, 0).T
        s1_v[at, :] = jnp.concatenate([-sinv, z8, zero] * 2, 0).T
        s2_v[at, :] = jnp.concatenate([z8, sinv, zero] * 2, 0).T
        return 0

    lax.fori_loop(0, toks // TC, table_step, 0)

    line.step(1)
    g1.forward()
    line.step(2)
    line.step(3)
    g2.forward()
    own_gain.wait()
    for d in (1, 2, 3):
        src = gbs.at[lax.rem(row + 4 - d, 4)]
        pltpu.make_async_copy(src, src, gr.at[d]).wait()
    line.arrived()
    g1.arrived()

    def out(i, src, dst):
        return pltpu.make_async_copy(src, dst, out_sem.at[i])

    out(7, w1, w1_o).start()
    bias = b1[...]

    def token_step(i, _):
        at = pl.ds(pl.multiple_of(i * TC, TC), TC)
        blocks = [xf[b, at, :].astype(F32) for b in range(4)]
        total = (blocks[0] + blocks[1]) + (blocks[2] + blocks[3])
        square = (blocks[0] * blocks[0] + blocks[1] * blocks[1]) + (
            blocks[2] * blocks[2] + blocks[3] * blocks[3]
        )
        mean = jnp.sum(total, 1, keepdims=True) * (1.0 / D)
        var = jnp.sum(square, 1, keepdims=True) * (1.0 / D) - mean * mean
        inv = lax.rsqrt(var + EPSILON)
        lane = lax.broadcasted_iota(jnp.int32, (TC, 128), 1)
        stat_v[at, :] = jnp.where(lane == 0, mean, inv)
        acc = None
        for b in range(4):
            gain = gbs[b, 0:1, :]
            shift = gbs[b, 1:2, :]
            n = ((blocks[b] - mean) * inv * gain + shift).astype(BF)
            nrm_v[b, at, :] = n
            part = dot(n, w1[b])
            acc = part if acc is None else acc + part
        acc = acc + bias
        c, s1, s2 = c_v[at, :], s1_v[at, :], s2_v[at, :]
        q_v[at, :] = rope(acc[:, 0:128], c, s1, s2).astype(BF)
        k_v[at, :] = rope(acc[:, 128:256], c, s1, s2).astype(BF)
        v_v[at, :] = acc[:, 256:384].astype(BF)
        up = acc[:, 384:]
        phi = 0.5 * (1.0 + lax.erf(up * (1.0 / math.sqrt(2.0))))
        act_v[at, :] = (up * phi).astype(BF)
        gp_v[at, :] = (phi + up * jnp.exp(-0.5 * up * up) * (1.0 / math.sqrt(2.0 * math.pi))).astype(BF)
        return 0

    lax.fori_loop(0, toks // TC, token_step, 0)
    own = stat_v.at[pl.ds(pl.multiple_of(col * half, half), half)]
    pairs = [
        (q_v, q_o), (k_v, k_o), (v_v, v_o), (act_v, act_o), (gp_v, gp_o), (nrm_v, nrm_o),
        (own, stat_o), (w1, w1_o), (cs_v, cs_o), (rng_v, rng_o),
    ]
    for i, (s, d) in enumerate(pairs):
        if i != 7:
            out(i, s, d).start()
    g2.arrived()
    out(10, w2, w2_o).start()
    line.drain()
    g1.drain()
    g2.drain()
    for d in (1, 2, 3):
        gain_copy(d).wait_send()
    for i, (s, d) in enumerate(pairs):
        out(i, s, d).wait()
    out(10, w2, w2_o).wait()


def project(x, w1s, w2s, gb, seg, b1):
    toks = seg.shape[1]
    nw1, nw2 = w1s.shape, w2s.shape
    fc = nw1[2] - 384
    dma = pltpu.SemaphoreType.DMA
    sd = jax.ShapeDtypeStruct
    return pl.pallas_call(
        project_kernel,
        name="project",
        out_shape=(
            sd((toks, 128), BF), sd((toks, 128), BF), sd((toks, 128), BF), sd((toks, fc), BF),
            sd((toks, fc), BF), sd((4, toks, 256), BF), sd(nw1, BF), sd(nw2, BF),
            sd((toks // 2, 128), F32), sd((16, toks), F32), sd((8, toks), jnp.int32),
        ),
        in_specs=[hbm()] * 3 + [vmem()] * 3,
        out_specs=(hbm(),) * 11,
        scratch_shapes=[
            pltpu.VMEM((4, toks, 256), BF), pltpu.VMEM(nw1, BF), pltpu.VMEM(nw2, BF),
            pltpu.VMEM((4, 8, 256), F32),
            pltpu.VMEM((toks, 128), BF), pltpu.VMEM((toks, 128), BF), pltpu.VMEM((toks, 128), BF),
            pltpu.VMEM((toks, fc), BF), pltpu.VMEM((toks, fc), BF), pltpu.VMEM((4, toks, 256), BF),
            pltpu.VMEM((toks, 128), F32), pltpu.VMEM((16, toks), F32), pltpu.VMEM((8, toks), jnp.int32),
            pltpu.VMEM((toks, 128), F32), pltpu.VMEM((toks, 128), F32), pltpu.VMEM((toks, 128), F32),
            *line_sems(), *weight_sems(), *weight_sems(), dma((4,)), dma((4,)), dma((11,)),
        ],
        compiler_params=pltpu.CompilerParams(
            collective_id=0, has_side_effects=True, vmem_limit_bytes=56 * 2**20
        ),
    )(x, w1s, w2s, gb, seg, b1)


def per_device_sliced(
    inputs, segments, ln_gain, ln_bias, w_qkv, b_qkv, w_out, w_up, b_up, w_down, out_bias, cotangent
):
    nrow = lax.axis_size("row")
    row = lax.axis_index("row")
    dpart = inputs.shape[1]
    hcols = w_qkv.shape[2] // nrow
    fcols = w_up.shape[1] // nrow
    toks = segments.shape[1]
    half = inputs.shape[0]

    seg = segments[0]
    first = jnp.sum((seg[None, :] < seg[::BQ, None]).astype(jnp.int32), 1) // BK
    ends = jnp.sum((seg[None, :] <= seg[BK - 1 :: BK, None]).astype(jnp.int32), 1)
    last = (ends + BQ - 1) // BQ

    cg = lax.all_gather(lax.all_gather(cotangent, "row"), "col", axis=1, tiled=True)
    gb = jnp.concatenate([ln_gain[None], ln_bias[None], jnp.zeros((6, dpart), BF)]).astype(F32)
    w1s = jnp.concatenate(
        [
            w_qkv.reshape(dpart, 3, nrow, hcols).transpose(2, 0, 1, 3).reshape(nrow, dpart, 3 * hcols),
            w_up.reshape(dpart, nrow, fcols).transpose(1, 0, 2),
        ],
        2,
    )
    w2s = jnp.concatenate(
        [w_out.reshape(nrow, hcols, dpart), w_down.reshape(nrow, fcols, dpart)], 1
    )
    b1 = jnp.concatenate(
        [
            lax.dynamic_slice_in_dim(b_qkv, row * hcols, hcols, 1).reshape(-1),
            lax.dynamic_slice_in_dim(b_up, row * fcols, fcols, 0),
        ]
    ).astype(F32)

    h3 = 3 * hcols
    q, k, v, act, gp, nrm, w1, w2, stat, cs, rng = project(
        inputs, w1s, w2s, gb, segments, b1[None]
    )
    attended, raw, lse = attend_forward(first, q, k, v, rng)

    joined = jnp.concatenate([attended, act], 1)
    col = lax.axis_index("col")
    outp = jnp.einsum("tk,bkn->btn", joined, w2, preferred_element_type=F32).astype(BF)
    outp = lax.psum_scatter(outp, "row", scatter_dimension=0)
    outp = lax.psum_scatter(outp, "col", scatter_dimension=0, tiled=True)
    layer_out = (inputs.astype(F32) + outp.astype(F32) + out_bias.astype(F32)).astype(BF)
    gob = jnp.sum(cotangent.astype(F32), 0)
    cgd = cg.transpose(1, 0, 2).reshape(toks, D)
    w2d = w2.transpose(1, 0, 2).reshape(-1, D)
    g2 = dot(joined, cgd, TN)
    dj = dot(cgd, w2d, NT)
    datt = dj[:, :hcols].astype(BF)
    dup = (dj[:, hcols:] * gp).astype(BF)
    dproj = attend_backward(last, q, k, v, datt, raw, lse, rng, cs)
    d1 = jnp.concatenate([dproj, dup], 1)
    nd = nrm.transpose(1, 0, 2).reshape(toks, D)
    g1 = dot(nd, d1, TN)
    gb1 = jnp.sum(d1.astype(F32), 0)
    dn = jnp.einsum("tn,bkn->btk", d1, w1, preferred_element_type=F32).astype(BF)
    dn = lax.psum_scatter(dn, "row", scatter_dimension=0)
    dn = lax.psum_scatter(dn, "col", scatter_dimension=0, tiled=True).astype(F32)
    myx = stat[:, 0], stat[:, 1]
    xh = (inputs.astype(F32) - myx[0][:, None]) * myx[1][:, None]
    dc = dn * ln_gain.astype(F32)
    st = lax.psum((jnp.sum(dc, 1), jnp.sum(dc * xh, 1)), "row")
    grad_inputs = myx[1][:, None] * (
        dc - st[0][:, None] / D - xh * st[1][:, None] / D
    ) + cotangent.astype(F32)
    ng = lax.psum((jnp.sum(dn * xh, 0), jnp.sum(dn, 0), gob), ("dp", "col"))

    g1 = lax.psum(g1.astype(BF), "dp").reshape(nrow, dpart, -1)
    g2 = lax.psum(g2.astype(BF), "dp").reshape(-1, nrow, dpart).transpose(1, 0, 2)
    g1 = lax.all_to_all(g1, "row", 0, 0).astype(F32)
    g2 = lax.all_to_all(g2, "row", 0, 0).astype(F32)
    gb1 = lax.all_gather(lax.psum(gb1, "dp"), "row")
    grad_w_qkv = g1[:, :, :h3].reshape(nrow, dpart, 3, hcols).transpose(1, 2, 0, 3).reshape(dpart, 3, -1)
    grad_w_up = g1[:, :, h3:].transpose(1, 0, 2).reshape(dpart, -1)
    grad_w_out = g2[:, :hcols].reshape(-1, dpart)
    grad_w_down = g2[:, hcols:].reshape(-1, dpart)
    grad_b_qkv = gb1[:, :h3].reshape(nrow, 3, hcols).transpose(1, 0, 2).reshape(3, -1)
    grad_b_up = gb1[:, h3:].reshape(-1)
    return (
        layer_out, grad_inputs, ng[0], ng[1], grad_w_qkv, grad_b_qkv,
        grad_w_out, grad_w_up, grad_b_up, grad_w_down, ng[2],
    )


FLOOR_INIT = -1e30


def doc_positions(labels):
    token_index = jnp.arange(labels.shape[1], dtype=jnp.int32)
    flags = jnp.concatenate(
        [jnp.ones((labels.shape[0], 1), dtype=jnp.bool_), labels[:, 1:] != labels[:, :-1]], 1
    )
    starts = lax.cummax(jnp.where(flags, token_index[None, :], 0), axis=1)
    return token_index[None, :] - starts


def rotate(tensor_in, positions):
    half_rot = ROT // 2
    inverse = 10000.0 ** (-(jnp.arange(half_rot, dtype=jnp.float32) * 2.0 / ROT))
    angles = positions.astype(jnp.float32)[:, None] * inverse[None, :]
    cosines = jnp.cos(angles)[:, None, :]
    sine_vals = jnp.sin(angles)[:, None, :]
    first_half = tensor_in[..., :half_rot]
    second_half = tensor_in[..., half_rot:ROT]
    rest_dims = tensor_in[..., ROT:]
    return jnp.concatenate(
        [
            first_half * cosines - second_half * sine_vals,
            second_half * cosines + first_half * sine_vals,
            rest_dims,
        ],
        -1,
    )


def slice_rows(array_in, first_row, row_count, axis_num=0):
    return lax.dynamic_slice_in_dim(array_in, first_row, row_count, axis_num)


def put_rows(array_in, update, first_row, axis_num=0):
    return lax.dynamic_update_slice_in_dim(array_in, update, first_row, axis_num)


def block_pairs(query_blocks, key_blocks):
    q_list = jnp.repeat(jnp.arange(query_blocks, dtype=jnp.int32), key_blocks)
    k_list = jnp.tile(jnp.arange(key_blocks, dtype=jnp.int32), query_blocks)
    return (q_list, k_list)


def per_device_general(
    inputs, segments, ln_gain, ln_bias, w_qkv, b_qkv, w_out, w_up, b_up, w_down, out_bias, cotangent
):
    local_rows, feature_cols = inputs.shape
    part_count = lax.axis_size("row")
    row_index = lax.axis_index("row")
    head_cols = w_qkv.shape[2]
    head_count = head_cols // HD
    group_seqs = segments.shape[0]
    all_rows = group_seqs * SEQ_LEN
    span = all_rows // part_count
    query_blocks = span // span
    score_scale = 1.0 / math.sqrt(HD)
    labels = (segments + (jnp.arange(group_seqs, dtype=jnp.int32) * SEQ_LEN)[:, None]).reshape(-1)
    positions = doc_positions(segments).reshape(-1)
    token_index = jnp.arange(all_rows, dtype=jnp.int32)
    my_labels = slice_rows(labels, row_index * span, span)
    my_index = slice_rows(token_index, row_index * span, span)
    my_positions = slice_rows(positions, row_index * span, span)
    float_in = inputs.astype(jnp.float32)
    ln_sums = lax.psum((jnp.sum(float_in, 1), jnp.sum(float_in * float_in, 1)), "row")
    row_mean = ln_sums[0] / D
    row_var = ln_sums[1] / D - row_mean * row_mean
    inv_std = lax.rsqrt(row_var + EPSILON)
    centred = (float_in - row_mean[:, None]) * inv_std[:, None]
    normed = (centred * ln_gain.astype(jnp.float32) + ln_bias.astype(jnp.float32)).astype(
        jnp.bfloat16
    )
    gathered_hidden = lax.all_gather(normed, "col", axis=0, tiled=True)
    first_weights = jnp.concatenate([w_qkv.reshape(feature_cols, 3 * head_cols), w_up], 1)
    first_bias = jnp.concatenate(
        [b_qkv.reshape(3 * head_cols).astype(jnp.float32), b_up.astype(jnp.float32)]
    )
    first_out = (
        lax.psum_scatter(
            jnp.dot(
                slice_rows(gathered_hidden, jnp.int32(0), lax.axis_size("row") * span),
                first_weights,
                preferred_element_type=jnp.float32,
            ).astype(jnp.bfloat16),
            "row",
            scatter_dimension=0,
            tiled=True,
        ).astype(jnp.float32)
        + first_bias
    )

    def rotate_mine(tensor_in):
        return rotate(tensor_in, my_positions)

    query_lin = first_out[:, :head_cols].reshape(span, head_count, HD)
    key_lin = first_out[:, head_cols : 2 * head_cols].reshape(span, head_count, HD)
    query = rotate_mine(query_lin).astype(jnp.bfloat16)
    key_rows = rotate_mine(key_lin).astype(jnp.bfloat16)
    value_rows = (
        first_out[:, 2 * head_cols : 3 * head_cols]
        .reshape(span, head_count, HD)
        .astype(jnp.bfloat16)
    )
    up_lin = first_out[:, 3 * head_cols :]
    activated = jax.nn.gelu(up_lin, approximate=False).astype(jnp.bfloat16)

    def over_keys(fold_step, initial):
        return fold_step(
            initial,
            (
                lax.all_gather(key_rows, "row", axis=0, tiled=True),
                lax.all_gather(value_rows, "row", axis=0, tiled=True),
            ),
            jnp.int32(0),
        )

    def key_setup(pieces, first_row):
        row_count = pieces[0].shape[0]
        piece_labels = slice_rows(labels, first_row, row_count)
        piece_index = slice_rows(token_index, first_row, row_count)
        return (row_count, span, piece_labels, piece_index)

    def block_live(piece_labels, piece_index, key_size, q_block, k_block):
        q_labels = slice_rows(my_labels, q_block * span, span)
        q_index = slice_rows(my_index, q_block * span, span)
        k_labels = slice_rows(piece_labels, k_block * key_size, key_size)
        k_index = slice_rows(piece_index, k_block * key_size, key_size)
        return (
            (jnp.max(q_index) >= jnp.min(k_index))
            & (jnp.min(q_labels) <= jnp.max(k_labels))
            & (jnp.min(k_labels) <= jnp.max(q_labels))
        )

    def block_scores(pieces, piece_labels, piece_index, key_size, q_block, k_block):
        q_start = q_block * span
        k_start = k_block * key_size
        q_labels = slice_rows(my_labels, q_start, span)
        q_index = slice_rows(my_index, q_start, span)
        k_labels = slice_rows(piece_labels, k_start, key_size)
        k_index = slice_rows(piece_index, k_start, key_size)
        q_block_rows = slice_rows(query, q_start, span)
        k_block_rows = slice_rows(pieces[0], k_start, key_size)
        v_block_rows = slice_rows(pieces[1], k_start, key_size)
        scores = (
            jnp.einsum(
                "qhd,khd->hqk", q_block_rows, k_block_rows, preferred_element_type=jnp.float32
            )
            * score_scale
        )
        allowed = (q_labels[:, None] == k_labels[None, :]) & (k_index[None, :] <= q_index[:, None])
        scores = jnp.where(allowed[None], scores, MASKED)
        return (q_start, k_start, scores, q_block_rows, k_block_rows, v_block_rows)

    def forward_piece(running, pieces, first_row):
        row_count, key_size, piece_labels, piece_index = key_setup(pieces, first_row)
        q_list, k_list = block_pairs(query_blocks, row_count // key_size)

        def forward_pair_step(current, pair_ids):
            q_block, k_block = pair_ids

            def update(inner_state):
                row_max, row_sum, row_acc = inner_state
                q_start, k_start, scores, q_block_rows, k_block_rows, v_block_rows = block_scores(
                    pieces, piece_labels, piece_index, key_size, q_block, k_block
                )
                old_max = slice_rows(row_max, q_start, span, 1)
                new_max = jnp.maximum(old_max, jnp.max(scores, -1))
                weights = jnp.exp(scores - new_max[..., None])
                keep_part = jnp.exp(old_max - new_max)
                new_sum = slice_rows(row_sum, q_start, span, 1) * keep_part + jnp.sum(weights, -1)
                added = jnp.einsum(
                    "hqk,khd->hqd",
                    weights.astype(jnp.bfloat16),
                    v_block_rows,
                    preferred_element_type=jnp.float32,
                )
                new_acc = slice_rows(row_acc, q_start, span, 1) * keep_part[..., None] + added
                return (
                    put_rows(row_max, new_max, q_start, 1),
                    put_rows(row_sum, new_sum, q_start, 1),
                    put_rows(row_acc, new_acc, q_start, 1),
                )

            def forward_unchanged(inner_state):
                return inner_state

            is_live = block_live(piece_labels, piece_index, key_size, q_block, k_block)
            return (lax.cond(is_live, update, forward_unchanged, current), None)

        result, _ = lax.scan(forward_pair_step, running, (q_list, k_list))
        return result

    forward_init = (
        jnp.full((head_count, span), FLOOR_INIT, jnp.float32),
        jnp.zeros((head_count, span), jnp.float32),
        jnp.zeros((head_count, span, HD), jnp.float32),
    )
    row_max, row_sum, row_acc = over_keys(forward_piece, forward_init)
    log_total = row_max + jnp.log(row_sum)
    attention_raw = jnp.transpose(row_acc / row_sum[..., None], (1, 0, 2)).reshape(span, head_cols)
    attended = attention_raw.astype(jnp.bfloat16)
    joined = jnp.concatenate(
        (
            lax.all_gather(attended, "row", axis=0, tiled=True),
            lax.all_gather(activated, "row", axis=0, tiled=True),
        ),
        1,
    )
    second_weights = jnp.concatenate([w_out, w_down], 0)
    partial_out = lax.psum_scatter(
        jnp.dot(
            slice_rows(joined, jnp.int32(0), lax.axis_size("col") * local_rows),
            second_weights,
            preferred_element_type=jnp.float32,
        ).astype(jnp.bfloat16),
        "col",
        scatter_dimension=0,
        tiled=True,
    ).astype(jnp.float32)
    layer_out = (float_in + partial_out + out_bias.astype(jnp.float32)).astype(jnp.bfloat16)
    grad_full = lax.all_gather(cotangent, "col", axis=0, tiled=True)
    grad_out_bias = jnp.sum(grad_full, 0, dtype=jnp.float32)
    grad_second = lax.dot_general(
        joined, grad_full, (((0,), (0,)), ((), ())), preferred_element_type=jnp.float32
    )
    branch_back = lax.psum_scatter(
        lax.dot_general(
            slice_rows(grad_full, jnp.int32(0), lax.axis_size("row") * span),
            second_weights,
            (((1,), (1,)), ((), ())),
            preferred_element_type=jnp.float32,
        ).astype(jnp.bfloat16),
        "row",
        scatter_dimension=0,
        tiled=True,
    ).astype(jnp.float32)
    d_attended = branch_back[:, :head_cols].astype(jnp.bfloat16)
    d_activated = branch_back[:, head_cols:]
    _, gelu_back = jax.vjp(lambda tensor_in: jax.nn.gelu(tensor_in, approximate=False), up_lin)
    d_up = gelu_back(d_activated)[0].astype(jnp.bfloat16)
    d_out_heads = d_attended.reshape(span, head_count, HD)
    row_delta = jnp.transpose(
        jnp.sum((d_attended.astype(jnp.float32) * attention_raw).reshape(span, head_count, HD), -1)
    )

    def backward_piece(running, pieces, first_row):
        d_query_acc, d_key_all, d_value_all = running
        row_count, key_size, piece_labels, piece_index = key_setup(pieces, first_row)
        q_list, k_list = block_pairs(query_blocks, row_count // key_size)
        zero_keys = jnp.zeros((row_count, head_count, HD), jnp.float32)

        def backward_pair_step(current, pair_ids):
            q_block, k_block = pair_ids

            def update(inner_state):
                d_query_run, d_key_run, d_value_run = inner_state
                q_start, k_start, scores, q_block_rows, k_block_rows, v_block_rows = block_scores(
                    pieces, piece_labels, piece_index, key_size, q_block, k_block
                )
                probs_full = jnp.exp(scores - slice_rows(log_total, q_start, span, 1)[..., None])
                d_out_block = slice_rows(d_out_heads, q_start, span)
                d_probs = jnp.einsum(
                    "qhd,khd->hqk", d_out_block, v_block_rows, preferred_element_type=jnp.float32
                )
                d_scores = (
                    probs_full * (d_probs - slice_rows(row_delta, q_start, span, 1)[..., None])
                ).astype(jnp.bfloat16)
                q_added = (
                    jnp.einsum(
                        "hqk,khd->qhd", d_scores, k_block_rows, preferred_element_type=jnp.float32
                    )
                    * score_scale
                )
                k_added = (
                    jnp.einsum(
                        "hqk,qhd->khd", d_scores, q_block_rows, preferred_element_type=jnp.float32
                    )
                    * score_scale
                )
                v_added = jnp.einsum(
                    "hqk,qhd->khd",
                    probs_full.astype(jnp.bfloat16),
                    d_out_block,
                    preferred_element_type=jnp.float32,
                )
                return (
                    put_rows(
                        d_query_run, slice_rows(d_query_run, q_start, span) + q_added, q_start
                    ),
                    put_rows(
                        d_key_run, slice_rows(d_key_run, k_start, key_size) + k_added, k_start
                    ),
                    put_rows(
                        d_value_run, slice_rows(d_value_run, k_start, key_size) + v_added, k_start
                    ),
                )

            def backward_unchanged(inner_state):
                return inner_state

            is_live = block_live(piece_labels, piece_index, key_size, q_block, k_block)
            return (lax.cond(is_live, update, backward_unchanged, current), None)

        scanned, _ = lax.scan(
            backward_pair_step, (d_query_acc, zero_keys, zero_keys), (q_list, k_list)
        )
        d_query_acc, key_part, value_part = scanned
        d_key_all = put_rows(d_key_all, key_part, first_row)
        d_value_all = put_rows(d_value_all, value_part, first_row)
        return (d_query_acc, d_key_all, d_value_all)

    backward_init = (
        jnp.zeros((span, head_count, HD), jnp.float32),
        jnp.zeros((all_rows, head_count, HD), jnp.float32),
        jnp.zeros((all_rows, head_count, HD), jnp.float32),
    )
    d_query_rot, d_key_total, d_value_total = over_keys(backward_piece, backward_init)
    d_key_rot, d_value_mine = (
        lax.psum_scatter(
            d_key_total.reshape(all_rows, head_cols).astype(jnp.bfloat16),
            "row",
            scatter_dimension=0,
            tiled=True,
        ).astype(jnp.float32),
        lax.psum_scatter(
            d_value_total.reshape(all_rows, head_cols).astype(jnp.bfloat16),
            "row",
            scatter_dimension=0,
            tiled=True,
        ).astype(jnp.float32),
    )
    _, query_back = jax.vjp(rotate_mine, query_lin)
    _, key_back = jax.vjp(rotate_mine, key_lin)
    d_query_lin = query_back(d_query_rot)[0].reshape(span, head_cols).astype(jnp.bfloat16)
    d_key_lin = (
        key_back(d_key_rot.reshape(span, head_count, HD))[0]
        .reshape(span, head_cols)
        .astype(jnp.bfloat16)
    )
    d_first = jnp.concatenate([d_query_lin, d_key_lin, d_value_mine.astype(jnp.bfloat16), d_up], 1)
    d_first_full = lax.all_gather(d_first, "row", axis=0, tiled=True)
    grad_first_bias = jnp.sum(d_first_full, 0, dtype=jnp.float32)
    grad_first = lax.dot_general(
        gathered_hidden, d_first_full, (((0,), (0,)), ((), ())), preferred_element_type=jnp.float32
    )
    d_normed = lax.psum_scatter(
        lax.dot_general(
            slice_rows(d_first_full, jnp.int32(0), lax.axis_size("col") * local_rows),
            first_weights,
            (((1,), (1,)), ((), ())),
            preferred_element_type=jnp.float32,
        ).astype(jnp.bfloat16),
        "col",
        scatter_dimension=0,
        tiled=True,
    ).astype(jnp.float32)
    d_centred = d_normed * ln_gain.astype(jnp.float32)
    grad_stats = lax.psum((jnp.sum(d_centred, 1), jnp.sum(d_centred * centred, 1)), "row")
    grad_inputs = inv_std[:, None] * (
        d_centred - grad_stats[0][:, None] / D - centred * grad_stats[1][:, None] / D
    ) + cotangent.astype(jnp.float32)
    summed = (
        lax.psum(grad_first.astype(jnp.bfloat16), "dp").astype(jnp.float32),
        lax.psum(grad_second.astype(jnp.bfloat16), "dp").astype(jnp.float32),
        lax.psum(grad_first_bias.astype(jnp.bfloat16), "dp").astype(jnp.float32),
        lax.psum(grad_out_bias.astype(jnp.bfloat16), "dp").astype(jnp.float32),
    )
    norm_grads = lax.psum((jnp.sum(d_normed * centred, 0), jnp.sum(d_normed, 0)), ("dp", "col"))
    grad_w_qkv = summed[0][:, : 3 * head_cols].reshape(feature_cols, 3, head_cols)
    grad_w_up = summed[0][:, 3 * head_cols :]
    grad_w_out = summed[1][:head_cols]
    grad_w_down = summed[1][head_cols:]
    grad_b_qkv = summed[2][: 3 * head_cols].reshape(3, head_cols)
    grad_b_up = summed[2][3 * head_cols :]
    return (
        layer_out,
        grad_inputs,
        norm_grads[0],
        norm_grads[1],
        grad_w_qkv,
        grad_b_qkv,
        grad_w_out,
        grad_w_up,
        grad_b_up,
        grad_w_down,
        summed[3],
    )


def solution(mesh):
    placed = (
        P(("dp", "col"), "row"),
        P("dp", None),
        P("row"),
        P("row"),
        P("row", None, "col"),
        P(None, "col"),
        P("col", "row"),
        P("row", "col"),
        P("col"),
        P("col", "row"),
        P("row"),
        P(("dp", "col"), "row"),
    )
    size = dict(mesh.shape)
    sliced = (size["dp"], size["row"], size["col"]) == (4, 4, 2)
    return jax.shard_map(
        per_device_sliced if sliced else per_device_general,
        mesh=mesh,
        in_specs=placed,
        out_specs=(
            P(("dp", "col"), "row"),
            P(("dp", "col"), "row"),
            P("row"),
            P("row"),
            P("row", None, "col"),
            P(None, "col"),
            P("col", "row"),
            P("row", "col"),
            P("col"),
            P("col", "row"),
            P("row"),
        ),
        check_vma=False,
    )
```

```python
import math

import jax
import jax.numpy as jnp
from jax import lax
from jax.experimental import pallas as pl
from jax.experimental.pallas import tpu as pltpu
from jax.sharding import PartitionSpec as P

D = 1024
HD = 64
ROT = 16
SEQ_LEN = 2048
EPSILON = 1e-05
MASKED = -1000000000.0
BF = jnp.bfloat16
F32 = jnp.float32
NT = (((1,), (1,)), ((), ()))
NN = (((1,), (0,)), ((), ()))
TN = (((0,), (0,)), ((), ()))


def dot(a, b, dims=NN):
    return lax.dot_general(a, b, dims, preferred_element_type=F32)


BQ = 512
BK = 256


def lane_mask(head, rows):
    lane = lax.broadcasted_iota(jnp.int32, (rows, 128), 1)
    return (lane >= head * HD) & (lane < (head + 1) * HD)


def vmem():
    return pl.BlockSpec(memory_space=pltpu.VMEM)


def rope(x, c, s1, s2):
    return x * c + pltpu.roll(x, 120, 1) * s1 + pltpu.roll(x, 8, 1) * s2


def unrope(gt, cosv, sinv):
    rows = []
    for h in range(2):
        o = h * HD
        a, b = gt[o : o + 8], gt[o + 8 : o + 16]
        rows += [a * cosv + b * sinv, b * cosv - a * sinv, gt[o + 16 : o + HD]]
    return jnp.concatenate(rows, 0)


MESH = pl.DeviceIdType.MESH
TC = 256
XC = 2


def hbm():
    return pl.BlockSpec(memory_space=pl.ANY)


def remote(src, dst, send, recv, dev):
    return pltpu.make_async_remote_copy(
        src_ref=src, dst_ref=dst, send_sem=send, recv_sem=recv, device_id=dev, device_id_type=MESH
    )


def where():
    return lax.axis_index("dp"), lax.axis_index("row"), lax.axis_index("col")


def greet(dp, row, col, rows=4, dps=4):
    bar = pltpu.get_barrier_semaphore()
    count = 0
    for d in range(1, dps):
        pl.semaphore_signal(bar, inc=1, device_id=(dp ^ d, row, col), device_id_type=MESH)
        count += 1
    for d in range(1, rows):
        pl.semaphore_signal(bar, inc=1, device_id=(dp, lax.rem(row + d, rows), col), device_id_type=MESH)
        count += 1
    pl.semaphore_signal(bar, inc=1, device_id=(dp, row, 1 - col), device_id_type=MESH)
    pl.semaphore_wait(bar, count + 1)


class LineGather:
    def __init__(self, own, full, sems, pos, half):
        self.own, self.full, self.pos, self.half = own, full, pos, half
        (self.su, self.sd, self.ru, self.rd, self.ss, self.rs, self.loc) = sems
        self.piece = half // XC

    def at(self, block, k):
        dp, row, col = self.pos
        start = pl.multiple_of(col * self.half + k * self.piece, self.piece)
        return self.full.at[block, pl.ds(start, self.piece)]

    def sib_at(self, block, k):
        dp, row, col = self.pos
        start = pl.multiple_of((1 - col) * self.half + k * self.piece, self.piece)
        return self.full.at[block, pl.ds(start, self.piece)]

    def src(self, step, block, k):
        return self.own.at[pl.ds(k * self.piece, self.piece)] if step == 0 else self.at(block, k)

    def up(self, step, k):
        dp, row, col = self.pos
        return remote(
            self.src(step, row - step, k), self.at(row - step, k),
            self.su.at[step, k], self.ru.at[step, k], (dp, row + 1, col),
        )

    def down(self, step, k):
        dp, row, col = self.pos
        return remote(
            self.src(step, row + step, k), self.at(row + step, k),
            self.sd.at[step, k], self.rd.at[step, k], (dp, row - 1, col),
        )

    def sib(self, step, sign, k):
        dp, row, col = self.pos
        i = step + 3 * (sign < 0)
        block = row - sign * step
        return remote(
            self.src(step, block, k), self.at(block, k),
            self.ss.at[i, k], self.rs.at[i, k], (dp, row, 1 - col),
        )

    def local(self):
        dp, row, col = self.pos
        start = pl.multiple_of(col * self.half, self.half)
        return pltpu.make_async_copy(self.own, self.full.at[row, pl.ds(start, self.half)], self.loc)

    def start(self):
        dp, row, col = self.pos
        for k in range(XC):
            @pl.when(row < 3)
            def _():
                self.up(0, k).start()

            @pl.when(row > 0)
            def _():
                self.down(0, k).start()
        for k in range(XC):
            self.sib(0, 1, k).start()
        self.local().start()

    def step(self, s):
        dp, row, col = self.pos
        for k in range(XC):
            @pl.when(row >= s)
            def _():
                pltpu.make_async_copy(self.at(row - s, k), self.at(row - s, k), self.ru.at[s - 1, k]).wait()

                @pl.when(row < 3)
                def _():
                    self.up(s, k).start()

                self.sib(s, 1, k).start()

            @pl.when(row + s <= 3)
            def _():
                pltpu.make_async_copy(self.at(row + s, k), self.at(row + s, k), self.rd.at[s - 1, k]).wait()

                @pl.when(row > 0)
                def _():
                    self.down(s, k).start()

                self.sib(s, -1, k).start()

    def sib_wait(self, s, sign):
        dp, row, col = self.pos
        block = row - sign * s
        i = s + 3 * (sign < 0)
        for k in range(XC):
            pltpu.make_async_copy(self.sib_at(block, k), self.sib_at(block, k), self.rs.at[i, k]).wait()

    def arrived(self):
        dp, row, col = self.pos
        self.local().wait()
        self.sib_wait(0, 1)
        for s in range(1, 4):
            @pl.when(row >= s)
            def _():
                self.sib_wait(s, 1)

            @pl.when(row + s <= 3)
            def _():
                self.sib_wait(s, -1)

    def drain(self):
        dp, row, col = self.pos
        for k in range(XC):
            self.sib(0, 1, k).wait_send()
            for s in range(0, 3):
                @pl.when((row >= s) & (row < 3))
                def _():
                    self.up(s, k).wait_send()

                @pl.when((row + s <= 3) & (row > 0))
                def _():
                    self.down(s, k).wait_send()
            for s in range(1, 4):
                @pl.when(row >= s)
                def _():
                    self.sib(s, 1, k).wait_send()

                @pl.when(row + s <= 3)
                def _():
                    self.sib(s, -1, k).wait_send()


def line_sems():
    dma = pltpu.SemaphoreType.DMA
    return [dma((4, XC))] * 4 + [dma((7, XC))] * 2 + [dma]


class WeightGather:
    def __init__(self, packed, full, sems, pos):
        self.packed, self.full, self.pos = packed, full, pos
        self.sz, self.rz, self.sp, self.rp, self.loc = sems
        self.rows = packed.shape[1] // 4

    def part(self, ref, block, quarter):
        return ref.at[block, pl.ds(pl.multiple_of(quarter * self.rows, self.rows), self.rows)]

    def along(self, d):
        dp, row, col = self.pos
        target = lax.rem(row + d, 4)
        return remote(
            self.part(self.packed, target, dp), self.part(self.full, row, dp),
            self.sz.at[d], self.rz.at[d], (dp, target, col),
        )

    def across(self, d, e):
        dp, row, col = self.pos
        block = lax.rem(row + 4 - d, 4)
        return remote(
            self.part(self.full, block, dp), self.part(self.full, block, dp),
            self.sp.at[d, e], self.rp.at[d, e], (dp ^ e, row, col),
        )

    def local(self):
        dp, row, col = self.pos
        return pltpu.make_async_copy(self.packed.at[row], self.full.at[row], self.loc)

    def start(self):
        for d in (2, 1, 3):
            self.along(d).start()
        self.local().start()

    def forward(self):
        dp, row, col = self.pos
        for d in (1, 3, 2):
            block = lax.rem(row + 4 - d, 4)
            part = self.part(self.full, block, dp)
            pltpu.make_async_copy(part, part, self.rz.at[d]).wait()
            for e in (3, 1, 2):
                self.across(d, e).start()

    def arrived(self):
        dp, row, col = self.pos
        self.local().wait()
        for d in (1, 3, 2):
            block = lax.rem(row + 4 - d, 4)
            for e in (1, 2, 3):
                part = self.part(self.full, block, dp ^ e)
                pltpu.make_async_copy(part, part, self.rp.at[d, e]).wait()

    def drain(self):
        for d in (1, 2, 3):
            self.along(d).wait_send()
            for e in (1, 2, 3):
                self.across(d, e).wait_send()


def weight_sems():
    dma = pltpu.SemaphoreType.DMA
    return [dma((4,))] * 2 + [dma((4, 4))] * 2 + [dma]


def attend_rows(qb, q_v, k_v, vt_v, rng_v, raw_v, lse_v, att_v):
    q0 = qb * BQ
    at = pl.ds(q0, BQ)
    qs = q_v[at, :] * BF(1.0 / math.sqrt(HD))
    heads = [jnp.where(lane_mask(h, BQ), qs, BF(0)) for h in range(2)]
    start, span = rng_v[0:1, at], rng_v[1:2, at]

    def k_step(kb, carry):
        k0 = pl.multiple_of(kb * BK, BK)
        kk = k_v[pl.ds(k0, BK), :]
        kidx = lax.broadcasted_iota(jnp.int32, (BK, BQ), 0) + k0 - start
        ok = (kidx >= 0) & (kidx <= span)
        new = []
        for h in range(2):
            m, l, acc = carry[h]
            s = jnp.where(ok, dot(kk, heads[h], NT), MASKED)
            m2 = jnp.maximum(m, jnp.max(s, 0, keepdims=True))
            p = jnp.exp(s - m2)
            c = jnp.exp(m - m2)
            l = l * c + jnp.sum(p, 0, keepdims=True)
            vt = vt_v[h * HD : (h + 1) * HD, pl.ds(k0, BK)]
            acc = acc * c + dot(vt, p.astype(BF))
            new.append((m2, l, acc))
        return tuple(new)

    init = tuple(
        (jnp.full((1, BQ), -1e30, F32), jnp.zeros((1, BQ), F32), jnp.zeros((HD, BQ), F32))
        for _ in range(2)
    )
    res = lax.fori_loop(0, (qb + 1) * (BQ // BK), k_step, init)
    for h in range(2):
        m, l, acc = res[h]
        raw_v[h * HD : (h + 1) * HD, at] = acc / l
        lse_v[h : h + 1, at] = m + jnp.log(l)
    att_v[at, :] = raw_v[:, at].T.astype(BF)


def forward_kernel(
    x, w1s, w2s, cot, gb, seg, b1,
    q_o, k_o, v_o, act_o, gp_o, nrm_o, w1_o, w2_o, stat_o, cs_o, rng_o, att_o, raw_o, lse_o, cot_o,
    xf, cf, w1, w2, gbs, q_v, k_v, v_v, act_v, gp_v, nrm_v, stat_v, cs_v, rng_v, c_v, s1_v, s2_v,
    vt_v, att_v, raw_v, lse_v,
    *sems,
):
    pos = where()
    dp, row, col = pos
    toks = seg.shape[1]
    half = toks // 2
    line = LineGather(x, xf, sems[0:7], pos, half)
    cline = LineGather(cot, cf, sems[7:14], pos, half)
    g1 = WeightGather(w1s, w1, sems[14:19], pos)
    g2 = WeightGather(w2s, w2, sems[19:24], pos)
    gs, gr, out_sem = sems[24:27]
    greet(dp, row, col)
    g1.start()
    line.start()

    def gain_copy(d):
        return remote(gb, gbs.at[row], gs.at[d], gr.at[d], (dp, lax.rem(row + d, 4), col))

    for d in (1, 2, 3):
        gain_copy(d).start()
    own_gain = pltpu.make_async_copy(gb, gbs.at[row], gr.at[0])
    own_gain.start()
    g2.start()

    labels = seg[...]
    start = jnp.zeros_like(labels)
    for d in range(1, 8):
        below = jnp.sum((labels == d - 1).astype(F32), 1, keepdims=True).astype(jnp.int32)
        start = start + jnp.where(labels >= d, below, 0)
    index = lax.broadcasted_iota(jnp.int32, labels.shape, 1)
    place = index - start
    rng_v[0:1, :] = start
    rng_v[1:2, :] = place
    rng_v[2:8, :] = jnp.zeros((6, toks), jnp.int32)
    power = lax.broadcasted_iota(jnp.int32, (8, 1), 0).astype(F32) * (-2.0 * math.log(10000.0) / ROT)
    ang = place.astype(F32) * jnp.exp(power)
    cs_v[0:8, :] = jnp.cos(ang)
    cs_v[8:16, :] = jnp.sin(ang)
    lse_v[...] = jnp.zeros_like(lse_v)

    def table_step(i, _):
        at = pl.ds(pl.multiple_of(i * TC, TC), TC)
        cosv, sinv = cs_v[0:8, at], cs_v[8:16, at]
        one = jnp.ones((HD - ROT, TC), F32)
        zero = jnp.zeros((HD - ROT, TC), F32)
        z8 = jnp.zeros((8, TC), F32)
        c_v[at, :] = jnp.concatenate([cosv, cosv, one] * 2, 0).T
        s1_v[at, :] = jnp.concatenate([-sinv, z8, zero] * 2, 0).T
        s2_v[at, :] = jnp.concatenate([z8, sinv, zero] * 2, 0).T
        return 0

    lax.fori_loop(0, toks // TC, table_step, 0)

    line.step(1)
    g1.forward()
    line.step(2)
    line.step(3)
    cline.start()
    g2.forward()
    own_gain.wait()
    for d in (1, 2, 3):
        src = gbs.at[lax.rem(row + 4 - d, 4)]
        pltpu.make_async_copy(src, src, gr.at[d]).wait()
    line.arrived()
    g1.arrived()
    own = stat_v.at[pl.ds(pl.multiple_of(col * half, half), half)]
    outs = [
        (q_v, q_o), (k_v, k_o), (v_v, v_o), (act_v, act_o), (gp_v, gp_o), (nrm_v, nrm_o),
        (w1, w1_o), (w2, w2_o), (own, stat_o), (cs_v, cs_o), (rng_v, rng_o), (att_v, att_o),
        (raw_v, raw_o), (lse_v, lse_o), (cf, cot_o),
    ]

    def out(i):
        return pltpu.make_async_copy(outs[i][0], outs[i][1], out_sem.at[i])

    out(6).start()
    out(9).start()
    out(10).start()
    bias = b1[...]
    weights = w1.reshape(w1.shape[0] * w1.shape[1], w1.shape[2])

    def token_step(i, _):
        at = pl.ds(pl.multiple_of(i * TC, TC), TC)
        blocks = [xf[b, at, :].astype(F32) for b in range(4)]
        total = (blocks[0] + blocks[1]) + (blocks[2] + blocks[3])
        square = (blocks[0] * blocks[0] + blocks[1] * blocks[1]) + (
            blocks[2] * blocks[2] + blocks[3] * blocks[3]
        )
        mean = jnp.sum(total, 1, keepdims=True) * (1.0 / D)
        var = jnp.sum(square, 1, keepdims=True) * (1.0 / D) - mean * mean
        inv = lax.rsqrt(var + EPSILON)
        lane = lax.broadcasted_iota(jnp.int32, (TC, 128), 1)
        stat_v[at, :] = jnp.where(lane == 0, mean, inv)
        parts = []
        for b in range(4):
            gain = gbs[b, 0:1, :]
            shift = gbs[b, 1:2, :]
            n = ((blocks[b] - mean) * inv * gain + shift).astype(BF)
            nrm_v[b, at, :] = n
            parts.append(n)
        acc = dot(jnp.concatenate(parts, 1), weights[...]) + bias
        c, s1, s2 = c_v[at, :], s1_v[at, :], s2_v[at, :]
        q_v[at, :] = rope(acc[:, 0:128], c, s1, s2).astype(BF)
        k_v[at, :] = rope(acc[:, 128:256], c, s1, s2).astype(BF)
        v_v[at, :] = acc[:, 256:384].astype(BF)
        vt_v[:, at] = acc[:, 256:384].T.astype(BF)
        up = acc[:, 384:]
        phi = 0.5 * (1.0 + lax.erf(up * (1.0 / math.sqrt(2.0))))
        act_v[at, :] = (up * phi).astype(BF)
        gp_v[at, :] = (phi + up * jnp.exp(-0.5 * up * up) * (1.0 / math.sqrt(2.0 * math.pi))).astype(BF)
        return 0

    steps = toks // TC
    lax.fori_loop(0, steps // 2, token_step, 0)
    cline.step(1)
    lax.fori_loop(steps // 2, steps, token_step, 0)
    for i in (0, 1, 2, 3, 4, 5, 8):
        out(i).start()
    blocks = toks // BQ
    for qb in range(blocks):
        if qb == 1:
            cline.step(2)
        if qb == blocks - 1:
            cline.step(3)
        attend_rows(qb, q_v, k_v, vt_v, rng_v, raw_v, lse_v, att_v)
    for i in (11, 12, 13):
        out(i).start()
    g2.arrived()
    out(7).start()
    cline.arrived()
    out(14).start()
    line.drain()
    cline.drain()
    g1.drain()
    g2.drain()
    for d in (1, 2, 3):
        gain_copy(d).wait_send()
    for i in range(len(outs)):
        out(i).wait()


def forward(x, w1s, w2s, cot, gb, seg, b1):
    toks = seg.shape[1]
    nw1, nw2 = w1s.shape, w2s.shape
    fc = nw1[2] - 384
    dma = pltpu.SemaphoreType.DMA
    sd = jax.ShapeDtypeStruct
    i32 = jnp.int32
    return pl.pallas_call(
        forward_kernel,
        name="forward",
        out_shape=(
            sd((toks, 128), BF), sd((toks, 128), BF), sd((toks, 128), BF), sd((toks, fc), BF),
            sd((toks, fc), BF), sd((4, toks, 256), BF), sd(nw1, BF), sd(nw2, BF),
            sd((toks // 2, 128), F32), sd((16, toks), F32), sd((8, toks), i32),
            sd((toks, 128), BF), sd((128, toks), F32), sd((8, toks), F32), sd((4, toks, 256), BF),
        ),
        in_specs=[hbm()] * 4 + [vmem()] * 3,
        out_specs=(hbm(),) * 15,
        scratch_shapes=[
            pltpu.VMEM((4, toks, 256), BF), pltpu.VMEM((4, toks, 256), BF),
            pltpu.VMEM(nw1, BF), pltpu.VMEM(nw2, BF), pltpu.VMEM((4, 8, 256), F32),
            pltpu.VMEM((toks, 128), BF), pltpu.VMEM((toks, 128), BF), pltpu.VMEM((toks, 128), BF),
            pltpu.VMEM((toks, fc), BF), pltpu.VMEM((toks, fc), BF), pltpu.VMEM((4, toks, 256), BF),
            pltpu.VMEM((toks, 128), F32), pltpu.VMEM((16, toks), F32), pltpu.VMEM((8, toks), i32),
            pltpu.VMEM((toks, 128), F32), pltpu.VMEM((toks, 128), F32), pltpu.VMEM((toks, 128), F32),
            pltpu.VMEM((128, toks), BF), pltpu.VMEM((toks, 128), BF), pltpu.VMEM((128, toks), F32),
            pltpu.VMEM((8, toks), F32),
            *line_sems(), *line_sems(), *weight_sems(), *weight_sems(), dma((4,)), dma((4,)), dma((15,)),
        ],
        compiler_params=pltpu.CompilerParams(
            collective_id=0, has_side_effects=True, vmem_limit_bytes=56 * 2**20
        ),
    )(x, w1s, w2s, cot, gb, seg, b1)


class LineReduce:
    def __init__(self, own, stage, sib, line, sems, pos, half):
        self.own, self.stage, self.sib_in, self.line_in = own, stage, sib, line
        self.s_sib, self.r_sib, self.s_line, self.r_line = sems
        self.pos, self.half, self.piece = pos, half, half // 2

    def at(self, ref, b, k):
        start = k * self.piece
        if not isinstance(k, int):
            start = pl.multiple_of(start, self.piece)
        return ref.at[b, pl.ds(start, self.piece)]

    def sib(self, b, k):
        dp, row, col = self.pos
        return remote(
            self.at(self.stage, b, k), self.at(self.sib_in, b, k),
            self.s_sib.at[b, k], self.r_sib.at[b, k], (dp, row, 1 - col),
        )

    def up(self, b, k):
        dp, row, col = self.pos
        return remote(
            self.at(self.own, b, k), self.at(self.line_in, b, k),
            self.s_line.at[b, k], self.r_line.at[b, k], (dp, row + 1, col),
        )

    def down(self, b, k):
        dp, row, col = self.pos
        slot = jnp.where(b == row - 1, 4, b)
        return remote(
            self.at(self.own, b, k), self.at(self.line_in, slot, k),
            self.s_line.at[b, k], self.r_line.at[slot, k], (dp, row - 1, col),
        )

    def produce(self, b, fn):
        dp, row, col = self.pos
        for k in range(2):
            first = pl.multiple_of((1 - col) * self.half + k * self.piece, self.piece)
            self.at(self.stage, b, k)[...] = fn(first, self.piece).astype(BF)
            self.sib(b, k).start()
        for k in range(2):
            first = pl.multiple_of(col * self.half + k * self.piece, self.piece)
            self.at(self.own, b, k)[...] = fn(first, self.piece).astype(BF)

    def wait_line(self, slot, k):
        pltpu.make_async_copy(self.at(self.line_in, slot, k), self.at(self.line_in, slot, k), self.r_line.at[slot, k]).wait()

    def wait_sib(self, b, k):
        pltpu.make_async_copy(self.at(self.sib_in, b, k), self.at(self.sib_in, b, k), self.r_sib.at[b, k]).wait()

    def hop(self, b, k):
        dp, row, col = self.pos
        self.wait_sib(b, k)
        own, sib, line = (self.at(r, b, k) for r in (self.own, self.sib_in, self.line_in))
        inner = (row > 0) & (row < 3)

        @pl.when(inner)
        def _():
            self.wait_line(b, k)
            own[...] = (own[...].astype(F32) + sib[...].astype(F32) + line[...].astype(F32)).astype(BF)

        @pl.when(jnp.logical_not(inner))
        def _():
            own[...] = (own[...].astype(F32) + sib[...].astype(F32)).astype(BF)

        @pl.when(row < b)
        def _():
            self.up(b, k).start()

        @pl.when(row > b)
        def _():
            self.down(b, k).start()

    def edge(self, b):
        dp, row, col = self.pos

        @pl.when(((row == 0) & (b > 0)) | ((row == 3) & (b < 3)))
        def _():
            for k in range(2):
                self.hop(b, k)

    def slot(self, j):
        dp, row, col = self.pos

        @pl.when((row == 1) | (row == 2))
        def _():
            self.hop(jnp.where(row == 1, 3 - j // 2, j // 2), j % 2)
            if j in (1, 2):
                self.hop(jnp.where(row == 1, 0, 3), j - 1)

    def final(self, k, total):
        dp, row, col = self.pos
        self.wait_sib(row, k)
        total[...] = self.at(self.own, row, k)[...].astype(F32) + self.at(self.sib_in, row, k)[...].astype(F32)

        @pl.when(row > 0)
        def _():
            self.wait_line(row, k)
            total[...] += self.at(self.line_in, row, k)[...].astype(F32)

        @pl.when(row < 3)
        def _():
            self.wait_line(4, k)
            total[...] += self.at(self.line_in, 4, k)[...].astype(F32)

    def drain_sib(self):
        for b in range(4):
            for k in range(2):
                self.sib(b, k).wait_send()

    def drain_line(self):
        dp, row, col = self.pos
        for b in range(4):
            for k in range(2):
                @pl.when(row < b)
                def _():
                    self.up(b, k).wait_send()

                @pl.when(row > b)
                def _():
                    self.down(b, k).wait_send()


def reduce_sems():
    dma = pltpu.SemaphoreType.DMA
    return [dma((4, 2))] * 3 + [dma((5, 2))]


class GradReduce:
    def __init__(self, grad, peers, part, final, sems, pos):
        self.grad, self.peers, self.part, self.out = grad, peers, part, final
        self.s1, self.r1, self.s2, self.r2, self.s3, self.r3 = sems
        self.pos = pos
        self.rows = grad.shape[1] // 4

    def quarter(self, ref, q):
        return ref.at[:, pl.ds(pl.multiple_of(q * self.rows, self.rows), self.rows)]

    def one(self, ref, b, q):
        return ref.at[b, pl.ds(pl.multiple_of(q * self.rows, self.rows), self.rows)]

    def first(self, e):
        dp, row, col = self.pos
        return remote(
            self.quarter(self.grad, dp ^ e), self.peers.at[e - 1], self.s1.at[e], self.r1.at[e],
            (dp ^ e, row, col),
        )

    def second(self, d):
        dp, row, col = self.pos
        target = lax.rem(row + d, 4)
        return remote(
            self.part.at[target], self.one(self.out, row, dp), self.s2.at[d], self.r2.at[d],
            (dp, target, col),
        )

    def third(self, e):
        dp, row, col = self.pos
        return remote(
            self.quarter(self.out, dp), self.quarter(self.out, dp), self.s3.at[e], self.r3.at[e],
            (dp ^ e, row, col),
        )

    def start(self):
        for e in (3, 1, 2):
            self.first(e).start()

    def sum_and_spread(self):
        dp, row, col = self.pos
        for e in (1, 2, 3):
            pltpu.make_async_copy(self.peers.at[e - 1], self.peers.at[e - 1], self.r1.at[e]).wait()

        def add(d, _):
            b = lax.rem(row + d, 4)
            total = self.one(self.grad, b, dp)[...].astype(F32)
            for e in range(3):
                total = total + self.peers[e, b].astype(F32)
            self.part[b] = total.astype(BF)
            return 0

        for d in (2, 1, 3):
            add(d, 0)
            self.second(d).start()
        add(0, 0)
        self.one(self.out, row, dp)[...] = self.part[row]

    def share(self):
        dp, row, col = self.pos
        for d in (1, 2, 3):
            src = lax.rem(row + 4 - d, 4)
            ref = self.one(self.out, src, dp)
            pltpu.make_async_copy(ref, ref, self.r2.at[d]).wait()
        for e in (3, 1, 2):
            self.third(e).start()

    def finish(self):
        dp, row, col = self.pos
        for e in (1, 2, 3):
            ref = self.quarter(self.out, dp ^ e)
            pltpu.make_async_copy(ref, ref, self.r3.at[e]).wait()
        for e in (1, 2, 3):
            self.first(e).wait_send()
            self.second(e).wait_send()
            self.third(e).wait_send()


def grad_sems():
    dma = pltpu.SemaphoreType.DMA
    return [dma((4,))] * 6


def backward_kernel(
    att, act, w2, cf, gp, raw, q, k, v, lse, cs, rng, nrm, w1, stat, x, cot, gain, obias,
    out_o, gin_o, dn_o, cols_o, f2_o, f1_o,
    att_v, act_v, w2_v, cf_v, gp_v, raw_v, q_v, k_v, v_v, lse_v, cs_v, rng_v, nrm_v, w1_v, stat_v, x_v, cot_v,
    own, stage, sib_a, line_a, sib_b, line_b, total, d1, da, delta, kt, dqt,
    g2, p2, t2, f2, gu, pu, tu, fu, gq, pq, tq, fq, send_st, st, out_v, gin_v,
    *sems,
):
    pos = where()
    dp, row, col = pos
    toks = q_v.shape[0]
    half = toks // 2
    piece = half // 2
    loads = [
        (att, att_v), (act, act_v), (w2, w2_v), (cf, cf_v), (gp, gp_v), (raw, raw_v), (q, q_v), (k, k_v),
        (v, v_v), (lse, lse_v), (cs, cs_v), (rng, rng_v), (nrm, nrm_v), (w1, w1_v), (stat, stat_v), (x, x_v),
        (cot, cot_v),
    ]
    load_sem, out_sem, s_st, r_st = sems[26:30]
    loads = [pltpu.make_async_copy(s, d, load_sem.at[i]) for i, (s, d) in enumerate(loads)]
    for c in loads:
        c.start()
    ra = LineReduce(own, stage, sib_a, line_a, sems[0:4], pos, half)
    rb = LineReduce(own, stage, sib_b, line_b, sems[4:8], pos, half)
    gr2 = GradReduce(g2, p2, t2, f2, sems[8:14], pos)
    gru = GradReduce(gu, pu, tu, fu, sems[14:20], pos)
    grq = GradReduce(gq, pq, tq, fq, sems[20:26], pos)
    greet(dp, row, col)
    order = (3, 0, 2, 1)

    for i in range(3):
        loads[i].wait()
    for i, b in enumerate(order):
        def out_part(first, count):
            at = pl.ds(first, count)
            return dot(jnp.concatenate([att_v[at, :], act_v[at, :]], 1), w2_v[b])

        ra.produce(b, out_part)
        if i > 0:
            ra.edge(order[i - 1])
    ra.edge(order[3])

    for i in (3, 4, 5):
        loads[i].wait()

    def joined_back(i, _):
        at = pl.ds(pl.multiple_of(i * TC, TC), TC)
        dj = dot(
            jnp.concatenate([cf_v[b, at, :] for b in range(4)], 1),
            jnp.concatenate([w2_v[b] for b in range(4)], 1),
            NT,
        )
        d_att = dj[:, 0:128].astype(BF)
        da[at, :] = d_att
        d1[at, 384:] = (dj[:, 128:] * gp_v[at, :].astype(F32)).astype(BF)
        prod = d_att.astype(F32).T * raw_v[:, at]
        for h in range(2):
            delta[h : h + 1, at] = jnp.sum(prod[h * HD : (h + 1) * HD], 0, keepdims=True)
        return 0

    lax.fori_loop(0, toks // TC, joined_back, 0)
    ra.slot(0)
    for b in range(4):
        g2[b, 0:128, :] = dot(att_v[...], cf_v[b], TN).astype(BF)
        g2[b, 128:, :] = dot(act_v[...], cf_v[b], TN).astype(BF)
    gr2.start()
    for i in range(6, 13):
        loads[i].wait()
    ra.slot(1)
    for b in range(4):
        gu[b] = dot(nrm_v[b], d1[:, 384:], TN).astype(BF)
    gru.start()
    ra.slot(2)

    kt[...] = k_v[...].astype(F32).T.astype(BF)
    dqt[...] = jnp.zeros_like(dqt)
    scale = 1.0 / math.sqrt(HD)

    def keys_back(kb):
        k0 = kb * BK
        kk = k_v[pl.ds(k0, BK), :]
        vv = v_v[pl.ds(k0, BK), :]

        def q_step(qb, carry):
            dk, dv = carry
            at = pl.ds(pl.multiple_of(qb * BQ, BQ), BQ)
            qs = q_v[at, :] * BF(scale)
            do = da[at, :]
            kidx = lax.broadcasted_iota(jnp.int32, (BK, BQ), 0) + k0 - rng_v[0:1, at]
            ok = (kidx >= 0) & (kidx <= rng_v[1:2, at])
            for h in range(2):
                qh = jnp.where(lane_mask(h, BQ), qs, BF(0))
                doh = jnp.where(lane_mask(h, BQ), do, BF(0))
                s = jnp.where(ok, dot(kk, qh, NT), MASKED)
                p = jnp.exp(s - lse_v[h : h + 1, at])
                ds = (p * (dot(vv, doh, NT) - delta[h : h + 1, at])).astype(BF)
                dv = dv + dot(p.astype(BF), doh)
                dk = dk + dot(ds, qh)
                rows = slice(h * HD, (h + 1) * HD)
                dqt[rows, at] += dot(kt[rows, pl.ds(k0, BK)], ds)
            return dk, dv

        zero = jnp.zeros((BK, 128), F32)
        dk, dv = lax.fori_loop(k0 // BQ, toks // BQ, q_step, (zero, zero))
        at = pl.ds(k0, BK)
        d1[at, 128:256] = unrope(dk.T, cs_v[0:8, at], cs_v[8:16, at]).T.astype(BF)
        d1[at, 256:384] = dv.astype(BF)

    for kb in range(toks // BK):
        keys_back(kb)
        if kb == 0:
            ra.slot(3)
        if kb == 1:
            gr2.sum_and_spread()
        if kb == 3:
            gru.sum_and_spread()
        if kb == 4:
            gr2.share()
        if kb == 6:
            gru.share()

    def queries_back(i, _):
        at = pl.ds(pl.multiple_of(i * BQ, BQ), BQ)
        d1[at, 0:128] = unrope(dqt[:, at] * scale, cs_v[0:8, at], cs_v[8:16, at]).T.astype(BF)
        return 0

    lax.fori_loop(0, toks // BQ, queries_back, 0)
    for i in range(13, len(loads)):
        loads[i].wait()
    ra.drain_sib()
    ra.drain_line()
    for kk in range(2):
        at = pl.ds(kk * piece, piece)
        ra.final(kk, total)
        out_v[at, :] = (x_v[at, :].astype(F32) + total[...] + obias[...]).astype(BF)
    pltpu.make_async_copy(out_v, out_o, out_sem.at[0]).start()

    for i, b in enumerate(order):
        def norm_part(first, count):
            return dot(d1[pl.ds(first, count), :], w1_v[b], NT)

        rb.produce(b, norm_part)
        if i > 0:
            rb.edge(order[i - 1])
    rb.edge(order[3])
    for b in range(4):
        gq[b] = dot(nrm_v[b], d1[:, 0:384], TN).astype(BF)
    grq.start()
    rb.slot(0)

    def column_sums(i, acc):
        at = pl.ds(pl.multiple_of(i * TC, TC), TC)
        return acc + jnp.sum(d1[at, :].astype(F32), 0, keepdims=True)

    cols_o[0:1, :] = lax.fori_loop(0, toks // TC, column_sums, jnp.zeros((1, d1.shape[1]), F32))
    cols_o[1:8, :] = jnp.zeros((7, d1.shape[1]), F32)
    rb.slot(1)
    grq.sum_and_spread()
    rb.slot(2)
    grq.share()
    rb.slot(3)
    scale_g = gain[...]
    dnsum = [jnp.zeros((1, 256), F32) for _ in range(3)]
    for kk in range(2):
        rb.final(kk, total)
        at = pl.ds(kk * piece, piece)
        dn = total[...]
        mean, inv = stat_v[at, 0:1], stat_v[at, 1:2]
        xh = (x_v[at, :].astype(F32) - mean) * inv
        ct = cot_v[at, :].astype(F32)
        dc = dn * scale_g
        s0 = jnp.sum(dc, 1, keepdims=True)
        s1 = jnp.sum(dc * xh, 1, keepdims=True)
        lane = lax.broadcasted_iota(jnp.int32, (piece, 128), 1)
        both = jnp.where(lane == 0, s0, jnp.where(lane == 1, s1, 0.0))
        send_st[:, at] = both.T[0:8, :]
        gin_v[at, :] = dc
        dnsum[0] += jnp.sum(dn * xh, 0, keepdims=True)
        dnsum[1] += jnp.sum(dn, 0, keepdims=True)
        dnsum[2] += jnp.sum(ct, 0, keepdims=True)

    def stat_copy(d):
        return remote(send_st, st.at[d - 1], s_st.at[d], r_st.at[d], (dp, lax.rem(row + d, 4), col))

    for d in (2, 1, 3):
        stat_copy(d).start()
    for i in range(3):
        dn_o[i : i + 1, :] = dnsum[i]
    dn_o[3:8, :] = jnp.zeros((5, 256), F32)
    gr2.finish()
    gru.finish()
    pltpu.make_async_copy(f2, f2_o, out_sem.at[1]).start()
    fuc = fu.shape[2]
    pltpu.make_async_copy(fu, f1_o.at[:, :, pl.ds(384, fuc)], out_sem.at[2]).start()
    sums = send_st[...]
    for d in (1, 2, 3):
        pltpu.make_async_copy(st.at[d - 1], st.at[d - 1], r_st.at[d]).wait()
        sums = sums + st[d - 1]
    for kk in range(2):
        at = pl.ds(kk * piece, piece)
        col2 = jnp.concatenate([sums[:, kk * piece : (kk + 1) * piece], jnp.zeros((120, piece), F32)], 0).T
        mean, inv = stat_v[at, 0:1], stat_v[at, 1:2]
        xh = (x_v[at, :].astype(F32) - mean) * inv
        gin_v[at, :] = inv * (gin_v[at, :] - col2[:, 0:1] * (1.0 / D) - xh * (col2[:, 1:2] * (1.0 / D))) + cot_v[
            at, :
        ].astype(F32)
    pltpu.make_async_copy(gin_v, gin_o, out_sem.at[3]).start()
    grq.finish()
    pltpu.make_async_copy(fq, f1_o.at[:, :, pl.ds(0, 384)], out_sem.at[4]).start()
    rb.drain_sib()
    rb.drain_line()
    for d in (1, 2, 3):
        stat_copy(d).wait_send()
    pltpu.make_async_copy(out_v, out_o, out_sem.at[0]).wait()
    pltpu.make_async_copy(f2, f2_o, out_sem.at[1]).wait()
    pltpu.make_async_copy(fu, f1_o.at[:, :, pl.ds(384, fuc)], out_sem.at[2]).wait()
    pltpu.make_async_copy(gin_v, gin_o, out_sem.at[3]).wait()
    pltpu.make_async_copy(fq, f1_o.at[:, :, pl.ds(0, 384)], out_sem.at[4]).wait()


def backward(att, act, w2, cf, gp, raw, q, k, v, lse, cs, rng, nrm, w1, stat, x, cot, gain, obias):
    toks = q.shape[0]
    half = toks // 2
    fc = act.shape[1]
    arrays = [att, act, w2, cf, gp, raw, q, k, v, lse, cs, rng, nrm, w1, stat, x, cot]
    dma = pltpu.SemaphoreType.DMA
    sd = jax.ShapeDtypeStruct
    V = pltpu.VMEM
    grads = []
    for r, c in ((128 + fc, 256), (256, fc), (256, 384)):
        grads += [V((4, r, c), BF), V((3, 4, r // 4, c), BF), V((4, r // 4, c), BF), V((4, r, c), BF)]
    return pl.pallas_call(
        backward_kernel,
        name="backward",
        out_shape=(
            sd((half, 256), BF), sd((half, 256), F32), sd((8, 256), F32), sd((8, 384 + fc), F32),
            sd((4, 128 + fc, 256), BF), sd((4, 256, 384 + fc), BF),
        ),
        in_specs=[hbm()] * 17 + [vmem()] * 2,
        out_specs=(hbm(), hbm(), vmem(), vmem(), hbm(), hbm()),
        scratch_shapes=[
            *[V(a.shape, a.dtype) for a in arrays],
            V((4, half, 256), BF), V((4, half, 256), BF), V((4, half, 256), BF), V((5, half, 256), BF),
            V((4, half, 256), BF), V((5, half, 256), BF), V((half // 2, 256), F32),
            V((toks, 384 + fc), BF), V((toks, 128), BF), V((8, toks), F32), V((128, toks), BF),
            V((128, toks), F32),
            *grads,
            V((8, half), F32), V((3, 8, half), F32), V((half, 256), BF), V((half, 256), F32),
            *reduce_sems(), *reduce_sems(), *grad_sems(), *grad_sems(), *grad_sems(),
            dma((17,)), dma((5,)), dma((4,)), dma((4,)),
        ],
        compiler_params=pltpu.CompilerParams(
            collective_id=1, has_side_effects=True, vmem_limit_bytes=60 * 2**20
        ),
    )(*arrays, gain, obias)


def per_device_sliced(
    inputs, segments, ln_gain, ln_bias, w_qkv, b_qkv, w_out, w_up, b_up, w_down, out_bias, cotangent
):
    nrow = lax.axis_size("row")
    row = lax.axis_index("row")
    dpart = inputs.shape[1]
    hcols = w_qkv.shape[2] // nrow
    fcols = w_up.shape[1] // nrow
    h3 = 3 * hcols
    gb = jnp.concatenate([ln_gain[None], ln_bias[None], jnp.zeros((6, dpart), BF)]).astype(F32)
    w1s = jnp.concatenate(
        [
            w_qkv.reshape(dpart, 3, nrow, hcols).transpose(2, 0, 1, 3).reshape(nrow, dpart, h3),
            w_up.reshape(dpart, nrow, fcols).transpose(1, 0, 2),
        ],
        2,
    )
    w2s = jnp.concatenate(
        [w_out.reshape(nrow, hcols, dpart), w_down.reshape(nrow, fcols, dpart)], 1
    )
    b1 = jnp.concatenate(
        [
            lax.dynamic_slice_in_dim(b_qkv, row * hcols, hcols, 1).reshape(-1),
            lax.dynamic_slice_in_dim(b_up, row * fcols, fcols, 0),
        ]
    ).astype(F32)
    q, k, v, act, gp, nrm, w1, w2, stat, cs, rng, att, raw, lse, cf = forward(
        inputs, w1s, w2s, cotangent, gb, segments, b1[None]
    )
    layer_out, grad_inputs, sums, cols, f2, f1 = backward(
        att, act, w2, cf, gp, raw, q, k, v, lse, cs, rng, nrm, w1, stat, inputs, cotangent,
        ln_gain.astype(F32)[None], out_bias.astype(F32)[None],
    )
    ng = lax.psum(sums[0:3], ("dp", "col"))
    gb1 = lax.all_gather(lax.psum(cols[0], "dp"), "row")
    g1 = f1.astype(F32)
    g2 = f2.astype(F32)
    grad_w_qkv = g1[:, :, :h3].reshape(nrow, dpart, 3, hcols).transpose(1, 2, 0, 3).reshape(dpart, 3, -1)
    grad_w_up = g1[:, :, h3:].transpose(1, 0, 2).reshape(dpart, -1)
    grad_w_out = g2[:, :hcols].reshape(-1, dpart)
    grad_w_down = g2[:, hcols:].reshape(-1, dpart)
    grad_b_qkv = gb1[:, :h3].reshape(nrow, 3, hcols).transpose(1, 0, 2).reshape(3, -1)
    grad_b_up = gb1[:, h3:].reshape(-1)
    return (
        layer_out, grad_inputs, ng[0], ng[1], grad_w_qkv, grad_b_qkv,
        grad_w_out, grad_w_up, grad_b_up, grad_w_down, ng[2],
    )


FLOOR_INIT = -1e30


def doc_positions(labels):
    token_index = jnp.arange(labels.shape[1], dtype=jnp.int32)
    flags = jnp.concatenate(
        [jnp.ones((labels.shape[0], 1), dtype=jnp.bool_), labels[:, 1:] != labels[:, :-1]], 1
    )
    starts = lax.cummax(jnp.where(flags, token_index[None, :], 0), axis=1)
    return token_index[None, :] - starts


def rotate(tensor_in, positions):
    half_rot = ROT // 2
    inverse = 10000.0 ** (-(jnp.arange(half_rot, dtype=jnp.float32) * 2.0 / ROT))
    angles = positions.astype(jnp.float32)[:, None] * inverse[None, :]
    cosines = jnp.cos(angles)[:, None, :]
    sine_vals = jnp.sin(angles)[:, None, :]
    first_half = tensor_in[..., :half_rot]
    second_half = tensor_in[..., half_rot:ROT]
    rest_dims = tensor_in[..., ROT:]
    return jnp.concatenate(
        [
            first_half * cosines - second_half * sine_vals,
            second_half * cosines + first_half * sine_vals,
            rest_dims,
        ],
        -1,
    )


def slice_rows(array_in, first_row, row_count, axis_num=0):
    return lax.dynamic_slice_in_dim(array_in, first_row, row_count, axis_num)


def put_rows(array_in, update, first_row, axis_num=0):
    return lax.dynamic_update_slice_in_dim(array_in, update, first_row, axis_num)


def block_pairs(query_blocks, key_blocks):
    q_list = jnp.repeat(jnp.arange(query_blocks, dtype=jnp.int32), key_blocks)
    k_list = jnp.tile(jnp.arange(key_blocks, dtype=jnp.int32), query_blocks)
    return (q_list, k_list)


def per_device_general(
    inputs, segments, ln_gain, ln_bias, w_qkv, b_qkv, w_out, w_up, b_up, w_down, out_bias, cotangent
):
    local_rows, feature_cols = inputs.shape
    part_count = lax.axis_size("row")
    row_index = lax.axis_index("row")
    head_cols = w_qkv.shape[2]
    head_count = head_cols // HD
    group_seqs = segments.shape[0]
    all_rows = group_seqs * SEQ_LEN
    span = all_rows // part_count
    query_blocks = span // span
    score_scale = 1.0 / math.sqrt(HD)
    labels = (segments + (jnp.arange(group_seqs, dtype=jnp.int32) * SEQ_LEN)[:, None]).reshape(-1)
    positions = doc_positions(segments).reshape(-1)
    token_index = jnp.arange(all_rows, dtype=jnp.int32)
    my_labels = slice_rows(labels, row_index * span, span)
    my_index = slice_rows(token_index, row_index * span, span)
    my_positions = slice_rows(positions, row_index * span, span)
    float_in = inputs.astype(jnp.float32)
    ln_sums = lax.psum((jnp.sum(float_in, 1), jnp.sum(float_in * float_in, 1)), "row")
    row_mean = ln_sums[0] / D
    row_var = ln_sums[1] / D - row_mean * row_mean
    inv_std = lax.rsqrt(row_var + EPSILON)
    centred = (float_in - row_mean[:, None]) * inv_std[:, None]
    normed = (centred * ln_gain.astype(jnp.float32) + ln_bias.astype(jnp.float32)).astype(
        jnp.bfloat16
    )
    gathered_hidden = lax.all_gather(normed, "col", axis=0, tiled=True)
    first_weights = jnp.concatenate([w_qkv.reshape(feature_cols, 3 * head_cols), w_up], 1)
    first_bias = jnp.concatenate(
        [b_qkv.reshape(3 * head_cols).astype(jnp.float32), b_up.astype(jnp.float32)]
    )
    first_out = (
        lax.psum_scatter(
            jnp.dot(
                slice_rows(gathered_hidden, jnp.int32(0), lax.axis_size("row") * span),
                first_weights,
                preferred_element_type=jnp.float32,
            ).astype(jnp.bfloat16),
            "row",
            scatter_dimension=0,
            tiled=True,
        ).astype(jnp.float32)
        + first_bias
    )

    def rotate_mine(tensor_in):
        return rotate(tensor_in, my_positions)

    query_lin = first_out[:, :head_cols].reshape(span, head_count, HD)
    key_lin = first_out[:, head_cols : 2 * head_cols].reshape(span, head_count, HD)
    query = rotate_mine(query_lin).astype(jnp.bfloat16)
    key_rows = rotate_mine(key_lin).astype(jnp.bfloat16)
    value_rows = (
        first_out[:, 2 * head_cols : 3 * head_cols]
        .reshape(span, head_count, HD)
        .astype(jnp.bfloat16)
    )
    up_lin = first_out[:, 3 * head_cols :]
    activated = jax.nn.gelu(up_lin, approximate=False).astype(jnp.bfloat16)

    def over_keys(fold_step, initial):
        return fold_step(
            initial,
            (
                lax.all_gather(key_rows, "row", axis=0, tiled=True),
                lax.all_gather(value_rows, "row", axis=0, tiled=True),
            ),
            jnp.int32(0),
        )

    def key_setup(pieces, first_row):
        row_count = pieces[0].shape[0]
        piece_labels = slice_rows(labels, first_row, row_count)
        piece_index = slice_rows(token_index, first_row, row_count)
        return (row_count, span, piece_labels, piece_index)

    def block_live(piece_labels, piece_index, key_size, q_block, k_block):
        q_labels = slice_rows(my_labels, q_block * span, span)
        q_index = slice_rows(my_index, q_block * span, span)
        k_labels = slice_rows(piece_labels, k_block * key_size, key_size)
        k_index = slice_rows(piece_index, k_block * key_size, key_size)
        return (
            (jnp.max(q_index) >= jnp.min(k_index))
            & (jnp.min(q_labels) <= jnp.max(k_labels))
            & (jnp.min(k_labels) <= jnp.max(q_labels))
        )

    def block_scores(pieces, piece_labels, piece_index, key_size, q_block, k_block):
        q_start = q_block * span
        k_start = k_block * key_size
        q_labels = slice_rows(my_labels, q_start, span)
        q_index = slice_rows(my_index, q_start, span)
        k_labels = slice_rows(piece_labels, k_start, key_size)
        k_index = slice_rows(piece_index, k_start, key_size)
        q_block_rows = slice_rows(query, q_start, span)
        k_block_rows = slice_rows(pieces[0], k_start, key_size)
        v_block_rows = slice_rows(pieces[1], k_start, key_size)
        scores = (
            jnp.einsum(
                "qhd,khd->hqk", q_block_rows, k_block_rows, preferred_element_type=jnp.float32
            )
            * score_scale
        )
        allowed = (q_labels[:, None] == k_labels[None, :]) & (k_index[None, :] <= q_index[:, None])
        scores = jnp.where(allowed[None], scores, MASKED)
        return (q_start, k_start, scores, q_block_rows, k_block_rows, v_block_rows)

    def forward_piece(running, pieces, first_row):
        row_count, key_size, piece_labels, piece_index = key_setup(pieces, first_row)
        q_list, k_list = block_pairs(query_blocks, row_count // key_size)

        def forward_pair_step(current, pair_ids):
            q_block, k_block = pair_ids

            def update(inner_state):
                row_max, row_sum, row_acc = inner_state
                q_start, k_start, scores, q_block_rows, k_block_rows, v_block_rows = block_scores(
                    pieces, piece_labels, piece_index, key_size, q_block, k_block
                )
                old_max = slice_rows(row_max, q_start, span, 1)
                new_max = jnp.maximum(old_max, jnp.max(scores, -1))
                weights = jnp.exp(scores - new_max[..., None])
                keep_part = jnp.exp(old_max - new_max)
                new_sum = slice_rows(row_sum, q_start, span, 1) * keep_part + jnp.sum(weights, -1)
                added = jnp.einsum(
                    "hqk,khd->hqd",
                    weights.astype(jnp.bfloat16),
                    v_block_rows,
                    preferred_element_type=jnp.float32,
                )
                new_acc = slice_rows(row_acc, q_start, span, 1) * keep_part[..., None] + added
                return (
                    put_rows(row_max, new_max, q_start, 1),
                    put_rows(row_sum, new_sum, q_start, 1),
                    put_rows(row_acc, new_acc, q_start, 1),
                )

            def forward_unchanged(inner_state):
                return inner_state

            is_live = block_live(piece_labels, piece_index, key_size, q_block, k_block)
            return (lax.cond(is_live, update, forward_unchanged, current), None)

        result, _ = lax.scan(forward_pair_step, running, (q_list, k_list))
        return result

    forward_init = (
        jnp.full((head_count, span), FLOOR_INIT, jnp.float32),
        jnp.zeros((head_count, span), jnp.float32),
        jnp.zeros((head_count, span, HD), jnp.float32),
    )
    row_max, row_sum, row_acc = over_keys(forward_piece, forward_init)
    log_total = row_max + jnp.log(row_sum)
    attention_raw = jnp.transpose(row_acc / row_sum[..., None], (1, 0, 2)).reshape(span, head_cols)
    attended = attention_raw.astype(jnp.bfloat16)
    joined = jnp.concatenate(
        (
            lax.all_gather(attended, "row", axis=0, tiled=True),
            lax.all_gather(activated, "row", axis=0, tiled=True),
        ),
        1,
    )
    second_weights = jnp.concatenate([w_out, w_down], 0)
    partial_out = lax.psum_scatter(
        jnp.dot(
            slice_rows(joined, jnp.int32(0), lax.axis_size("col") * local_rows),
            second_weights,
            preferred_element_type=jnp.float32,
        ).astype(jnp.bfloat16),
        "col",
        scatter_dimension=0,
        tiled=True,
    ).astype(jnp.float32)
    layer_out = (float_in + partial_out + out_bias.astype(jnp.float32)).astype(jnp.bfloat16)
    grad_full = lax.all_gather(cotangent, "col", axis=0, tiled=True)
    grad_out_bias = jnp.sum(grad_full, 0, dtype=jnp.float32)
    grad_second = lax.dot_general(
        joined, grad_full, (((0,), (0,)), ((), ())), preferred_element_type=jnp.float32
    )
    branch_back = lax.psum_scatter(
        lax.dot_general(
            slice_rows(grad_full, jnp.int32(0), lax.axis_size("row") * span),
            second_weights,
            (((1,), (1,)), ((), ())),
            preferred_element_type=jnp.float32,
        ).astype(jnp.bfloat16),
        "row",
        scatter_dimension=0,
        tiled=True,
    ).astype(jnp.float32)
    d_attended = branch_back[:, :head_cols].astype(jnp.bfloat16)
    d_activated = branch_back[:, head_cols:]
    _, gelu_back = jax.vjp(lambda tensor_in: jax.nn.gelu(tensor_in, approximate=False), up_lin)
    d_up = gelu_back(d_activated)[0].astype(jnp.bfloat16)
    d_out_heads = d_attended.reshape(span, head_count, HD)
    row_delta = jnp.transpose(
        jnp.sum((d_attended.astype(jnp.float32) * attention_raw).reshape(span, head_count, HD), -1)
    )

    def backward_piece(running, pieces, first_row):
        d_query_acc, d_key_all, d_value_all = running
        row_count, key_size, piece_labels, piece_index = key_setup(pieces, first_row)
        q_list, k_list = block_pairs(query_blocks, row_count // key_size)
        zero_keys = jnp.zeros((row_count, head_count, HD), jnp.float32)

        def backward_pair_step(current, pair_ids):
            q_block, k_block = pair_ids

            def update(inner_state):
                d_query_run, d_key_run, d_value_run = inner_state
                q_start, k_start, scores, q_block_rows, k_block_rows, v_block_rows = block_scores(
                    pieces, piece_labels, piece_index, key_size, q_block, k_block
                )
                probs_full = jnp.exp(scores - slice_rows(log_total, q_start, span, 1)[..., None])
                d_out_block = slice_rows(d_out_heads, q_start, span)
                d_probs = jnp.einsum(
                    "qhd,khd->hqk", d_out_block, v_block_rows, preferred_element_type=jnp.float32
                )
                d_scores = (
                    probs_full * (d_probs - slice_rows(row_delta, q_start, span, 1)[..., None])
                ).astype(jnp.bfloat16)
                q_added = (
                    jnp.einsum(
                        "hqk,khd->qhd", d_scores, k_block_rows, preferred_element_type=jnp.float32
                    )
                    * score_scale
                )
                k_added = (
                    jnp.einsum(
                        "hqk,qhd->khd", d_scores, q_block_rows, preferred_element_type=jnp.float32
                    )
                    * score_scale
                )
                v_added = jnp.einsum(
                    "hqk,qhd->khd",
                    probs_full.astype(jnp.bfloat16),
                    d_out_block,
                    preferred_element_type=jnp.float32,
                )
                return (
                    put_rows(
                        d_query_run, slice_rows(d_query_run, q_start, span) + q_added, q_start
                    ),
                    put_rows(
                        d_key_run, slice_rows(d_key_run, k_start, key_size) + k_added, k_start
                    ),
                    put_rows(
                        d_value_run, slice_rows(d_value_run, k_start, key_size) + v_added, k_start
                    ),
                )

            def backward_unchanged(inner_state):
                return inner_state

            is_live = block_live(piece_labels, piece_index, key_size, q_block, k_block)
            return (lax.cond(is_live, update, backward_unchanged, current), None)

        scanned, _ = lax.scan(
            backward_pair_step, (d_query_acc, zero_keys, zero_keys), (q_list, k_list)
        )
        d_query_acc, key_part, value_part = scanned
        d_key_all = put_rows(d_key_all, key_part, first_row)
        d_value_all = put_rows(d_value_all, value_part, first_row)
        return (d_query_acc, d_key_all, d_value_all)

    backward_init = (
        jnp.zeros((span, head_count, HD), jnp.float32),
        jnp.zeros((all_rows, head_count, HD), jnp.float32),
        jnp.zeros((all_rows, head_count, HD), jnp.float32),
    )
    d_query_rot, d_key_total, d_value_total = over_keys(backward_piece, backward_init)
    d_key_rot, d_value_mine = (
        lax.psum_scatter(
            d_key_total.reshape(all_rows, head_cols).astype(jnp.bfloat16),
            "row",
            scatter_dimension=0,
            tiled=True,
        ).astype(jnp.float32),
        lax.psum_scatter(
            d_value_total.reshape(all_rows, head_cols).astype(jnp.bfloat16),
            "row",
            scatter_dimension=0,
            tiled=True,
        ).astype(jnp.float32),
    )
    _, query_back = jax.vjp(rotate_mine, query_lin)
    _, key_back = jax.vjp(rotate_mine, key_lin)
    d_query_lin = query_back(d_query_rot)[0].reshape(span, head_cols).astype(jnp.bfloat16)
    d_key_lin = (
        key_back(d_key_rot.reshape(span, head_count, HD))[0]
        .reshape(span, head_cols)
        .astype(jnp.bfloat16)
    )
    d_first = jnp.concatenate([d_query_lin, d_key_lin, d_value_mine.astype(jnp.bfloat16), d_up], 1)
    d_first_full = lax.all_gather(d_first, "row", axis=0, tiled=True)
    grad_first_bias = jnp.sum(d_first_full, 0, dtype=jnp.float32)
    grad_first = lax.dot_general(
        gathered_hidden, d_first_full, (((0,), (0,)), ((), ())), preferred_element_type=jnp.float32
    )
    d_normed = lax.psum_scatter(
        lax.dot_general(
            slice_rows(d_first_full, jnp.int32(0), lax.axis_size("col") * local_rows),
            first_weights,
            (((1,), (1,)), ((), ())),
            preferred_element_type=jnp.float32,
        ).astype(jnp.bfloat16),
        "col",
        scatter_dimension=0,
        tiled=True,
    ).astype(jnp.float32)
    d_centred = d_normed * ln_gain.astype(jnp.float32)
    grad_stats = lax.psum((jnp.sum(d_centred, 1), jnp.sum(d_centred * centred, 1)), "row")
    grad_inputs = inv_std[:, None] * (
        d_centred - grad_stats[0][:, None] / D - centred * grad_stats[1][:, None] / D
    ) + cotangent.astype(jnp.float32)
    summed = (
        lax.psum(grad_first.astype(jnp.bfloat16), "dp").astype(jnp.float32),
        lax.psum(grad_second.astype(jnp.bfloat16), "dp").astype(jnp.float32),
        lax.psum(grad_first_bias.astype(jnp.bfloat16), "dp").astype(jnp.float32),
        lax.psum(grad_out_bias.astype(jnp.bfloat16), "dp").astype(jnp.float32),
    )
    norm_grads = lax.psum((jnp.sum(d_normed * centred, 0), jnp.sum(d_normed, 0)), ("dp", "col"))
    grad_w_qkv = summed[0][:, : 3 * head_cols].reshape(feature_cols, 3, head_cols)
    grad_w_up = summed[0][:, 3 * head_cols :]
    grad_w_out = summed[1][:head_cols]
    grad_w_down = summed[1][head_cols:]
    grad_b_qkv = summed[2][: 3 * head_cols].reshape(3, head_cols)
    grad_b_up = summed[2][3 * head_cols :]
    return (
        layer_out,
        grad_inputs,
        norm_grads[0],
        norm_grads[1],
        grad_w_qkv,
        grad_b_qkv,
        grad_w_out,
        grad_w_up,
        grad_b_up,
        grad_w_down,
        summed[3],
    )


def solution(mesh):
    placed = (
        P(("dp", "col"), "row"),
        P("dp", None),
        P("row"),
        P("row"),
        P("row", None, "col"),
        P(None, "col"),
        P("col", "row"),
        P("row", "col"),
        P("col"),
        P("col", "row"),
        P("row"),
        P(("dp", "col"), "row"),
    )
    size = dict(mesh.shape)
    sliced = (size["dp"], size["row"], size["col"]) == (4, 4, 2)
    return jax.shard_map(
        per_device_sliced if sliced else per_device_general,
        mesh=mesh,
        in_specs=placed,
        out_specs=(
            P(("dp", "col"), "row"),
            P(("dp", "col"), "row"),
            P("row"),
            P("row"),
            P("row", None, "col"),
            P(None, "col"),
            P("col", "row"),
            P("row", "col"),
            P("col"),
            P("col", "row"),
            P("row"),
        ),
        check_vma=False,
    )
```

```python
import math

import jax
import jax.numpy as jnp
from jax import lax
from jax.experimental import pallas as pl
from jax.experimental.pallas import tpu as pltpu
from jax.sharding import PartitionSpec as P

D = 1024
HD = 64
ROT = 16
SEQ_LEN = 2048
EPSILON = 1e-05
MASKED = -1000000000.0
BF = jnp.bfloat16
F32 = jnp.float32
NT = (((1,), (1,)), ((), ()))
NN = (((1,), (0,)), ((), ()))
TN = (((0,), (0,)), ((), ()))


def dot(a, b, dims=NN):
    return lax.dot_general(a, b, dims, preferred_element_type=F32)


BK = 256


def lane_mask(head, rows):
    lane = lax.broadcasted_iota(jnp.int32, (rows, 128), 1)
    return (lane >= head * HD) & (lane < (head + 1) * HD)


MESH = pl.DeviceIdType.MESH
TC = 256
BT = 512


def vmem():
    return pl.BlockSpec(memory_space=pltpu.VMEM)


def hbm():
    return pl.BlockSpec(memory_space=pl.ANY)


def span(first, count):
    if not isinstance(first, int):
        first = pl.multiple_of(first, count & -count)
    return pl.ds(first, count)


def remote(src, dst, send, recv, dev):
    return pltpu.make_async_remote_copy(
        src_ref=src, dst_ref=dst, send_sem=send, recv_sem=recv, device_id=dev, device_id_type=MESH
    )


def landed(ref, sem):
    pltpu.make_async_copy(ref, ref, sem).wait()


def left(ref, sem):
    pltpu.make_async_copy(ref, ref, sem).wait()


def where():
    return lax.axis_index("dp"), lax.axis_index("row"), lax.axis_index("col")


def greet(dp, row, col):
    bar = pltpu.get_barrier_semaphore()
    for d in range(1, 4):
        pl.semaphore_signal(bar, inc=1, device_id=(dp ^ d, row, col), device_id_type=MESH)
        pl.semaphore_signal(bar, inc=1, device_id=(dp, lax.rem(row + d, 4), col), device_id_type=MESH)
    pl.semaphore_signal(bar, inc=1, device_id=(dp, row, 1 - col), device_id_type=MESH)
    pl.semaphore_wait(bar, 7)


def dmas(*shapes):
    return [pltpu.SemaphoreType.DMA(s) for s in shapes]


class LineGather:
    SEMS = ((4, 2),) * 4 + ((7, 2),) * 2 + ((1,),)

    def __init__(self, own, full, sems, pos):
        self.own, self.full, self.pos = own, full, pos
        self.su, self.sd, self.ru, self.rd, self.ss, self.rs, self.loc = sems
        self.half = 2 * BT

    def at(self, block, k, other=False):
        dp, row, col = self.pos
        half = (1 - col) if other else col
        return self.full.at[block, span(half * self.half + k * BT, BT)]

    def src(self, step, block, k):
        return self.own.at[span(k * BT, BT)] if step == 0 else self.at(block, k)

    def up(self, step, k):
        dp, row, col = self.pos
        return remote(
            self.src(step, row - step, k), self.at(row - step, k),
            self.su.at[step, k], self.ru.at[step, k], (dp, row + 1, col),
        )

    def down(self, step, k):
        dp, row, col = self.pos
        return remote(
            self.src(step, row + step, k), self.at(row + step, k),
            self.sd.at[step, k], self.rd.at[step, k], (dp, row - 1, col),
        )

    def sib(self, step, sign, k):
        dp, row, col = self.pos
        i = step + 3 * (sign < 0)
        block = row - sign * step
        return remote(
            self.src(step, block, k), self.at(block, k),
            self.ss.at[i, k], self.rs.at[i, k], (dp, row, 1 - col),
        )

    def local(self):
        dp, row, col = self.pos
        return pltpu.make_async_copy(
            self.own, self.full.at[row, span(col * self.half, self.half)], self.loc.at[0]
        )

    def send_own(self, k):
        dp, row, col = self.pos

        @pl.when(row < 3)
        def _():
            self.up(0, k).start()

        @pl.when(row > 0)
        def _():
            self.down(0, k).start()

        self.sib(0, 1, k).start()

    def step(self, s, k):
        dp, row, col = self.pos

        @pl.when(row >= s)
        def _():
            landed(self.at(row - s, k), self.ru.at[s - 1, k])

            @pl.when(row < 3)
            def _():
                self.up(s, k).start()

            self.sib(s, 1, k).start()

        @pl.when(row + s <= 3)
        def _():
            landed(self.at(row + s, k), self.rd.at[s - 1, k])

            @pl.when(row > 0)
            def _():
                self.down(s, k).start()

            self.sib(s, -1, k).start()

    def ready(self, t):
        dp, row, col = self.pos
        k = t % 2

        @pl.when(col != t // 2)
        def _():
            landed(self.at(row, k, True), self.rs.at[0, k])
            for s in range(1, 4):
                @pl.when(row >= s)
                def _():
                    landed(self.at(row - s, k, True), self.rs.at[s, k])

                @pl.when(row + s <= 3)
                def _():
                    landed(self.at(row + s, k, True), self.rs.at[s + 3, k])

    def drain(self):
        dp, row, col = self.pos
        for k in range(2):
            self.sib(0, 1, k).wait_send()
            for s in range(0, 3):
                @pl.when((row >= s) & (row < 3))
                def _():
                    self.up(s, k).wait_send()

                @pl.when((row + s <= 3) & (row > 0))
                def _():
                    self.down(s, k).wait_send()
            for s in range(1, 4):
                @pl.when(row >= s)
                def _():
                    self.sib(s, 1, k).wait_send()

                @pl.when(row + s <= 3)
                def _():
                    self.sib(s, -1, k).wait_send()


class WeightGather:
    SEMS = ((4,), (4,), (4, 4), (4, 4), (4,))

    def __init__(self, full, pieces, sems, pos):
        self.full, self.pieces, self.pos = full, pieces, pos
        self.sz, self.rz, self.sp, self.rp, self.loc = sems
        self.quarter = full.shape[1] // 4

    def parts(self, block, q):
        seen = []
        for src, r0, rows, c0, cols, d0, e0 in self.pieces(0):
            seen.append((d0, rows))
        out = []
        for d0, rows in dict.fromkeys(seen):
            out.append(self.full.at[block, span(d0 + q * (rows // 4), rows // 4)])
        return out

    def bytes(self):
        return self.full.at[0, pl.ds(0, self.quarter)]

    def along(self, d):
        dp, row, col = self.pos
        target = lax.rem(row + d, 4)
        copies = []
        for src, r0, rows, c0, cols, d0, e0 in self.pieces(target):
            q = rows // 4
            copies.append(remote(
                src.at[span(r0 + dp * q, q), span(c0, cols)],
                self.full.at[row, span(d0 + dp * q, q), pl.ds(e0, cols)],
                self.sz.at[d], self.rz.at[d], (dp, target, col),
            ))
        return copies

    def across(self, d, e):
        dp, row, col = self.pos
        block = lax.rem(row + 4 - d, 4)
        return [
            remote(p, p, self.sp.at[d, e], self.rp.at[d, e], (dp ^ e, row, col)) for p in self.parts(block, dp)
        ]

    def local(self):
        dp, row, col = self.pos
        return [
            pltpu.make_async_copy(
                src.at[span(r0, rows), span(c0, cols)],
                self.full.at[row, pl.ds(d0, rows), pl.ds(e0, cols)], self.loc.at[i],
            )
            for i, (src, r0, rows, c0, cols, d0, e0) in enumerate(self.pieces(row))
        ]

    def start(self):
        for d in (2, 1, 3):
            for c in self.along(d):
                c.start()
        for c in self.local():
            c.start()

    def forward(self):
        for d in (1, 3, 2):
            landed(self.bytes(), self.rz.at[d])
            for e in (3, 1, 2):
                for c in self.across(d, e):
                    c.start()

    def arrived(self):
        for c in self.local():
            c.wait()
        for d in (1, 3, 2):
            for e in (1, 2, 3):
                landed(self.bytes(), self.rp.at[d, e])

    def drain(self):
        for d in (1, 2, 3):
            left(self.bytes(), self.sz.at[d])
            for e in (1, 2, 3):
                left(self.bytes(), self.sp.at[d, e])


class LineReduce:
    SEMS = ((4, 2),) * 3 + ((5, 2),)

    def __init__(self, own, sib, line, sems, pos):
        self.own, self.sib_in, self.line_in = own, sib, line
        self.s_sib, self.r_sib, self.s_line, self.r_line = sems
        self.pos = pos

    def at(self, ref, b, k):
        return ref.at[b, span(k * BT, BT)]

    def sib(self, stage, b, k):
        dp, row, col = self.pos
        return remote(
            stage.at[b], self.at(self.sib_in, b, k), self.s_sib.at[b, k], self.r_sib.at[b, k], (dp, row, 1 - col)
        )

    def up(self, b, k):
        dp, row, col = self.pos
        return remote(
            self.at(self.own, b, k), self.at(self.line_in, b, k),
            self.s_line.at[b, k], self.r_line.at[b, k], (dp, row + 1, col),
        )

    def down(self, b, k):
        dp, row, col = self.pos
        slot = jnp.where(b == row - 1, 4, b)
        return remote(
            self.at(self.own, b, k), self.at(self.line_in, slot, k),
            self.s_line.at[b, k], self.r_line.at[slot, k], (dp, row - 1, col),
        )

    def produce(self, t, stage, fn):
        dp, row, col = self.pos
        k = t % 2
        for b in (3, 0, 2, 1):
            part = fn(b).astype(BF)

            @pl.when(col == t // 2)
            def _():
                self.at(self.own, b, k)[...] = part

            @pl.when(col != t // 2)
            def _():
                stage[b] = part
                self.sib(stage, b, k).start()

    def wait_stage(self, t, stage):
        dp, row, col = self.pos

        @pl.when(col != t // 2)
        def _():
            for b in range(4):
                self.sib(stage, b, t % 2).wait_send()

    def hop(self, b, k, take):
        dp, row, col = self.pos
        landed(self.at(self.sib_in, b, k), self.r_sib.at[b, k])
        own, sib = self.at(self.own, b, k), self.at(self.sib_in, b, k)
        if take:
            landed(self.at(self.line_in, b, k), self.r_line.at[b, k])
            line = self.at(self.line_in, b, k)
            own[...] = (own[...].astype(F32) + sib[...].astype(F32) + line[...].astype(F32)).astype(BF)
        else:
            own[...] = (own[...].astype(F32) + sib[...].astype(F32)).astype(BF)

        @pl.when(row < b)
        def _():
            self.up(b, k).start()

        @pl.when(row > b)
        def _():
            self.down(b, k).start()

    def edge(self, t):
        dp, row, col = self.pos
        mine = col == t // 2

        @pl.when(((row == 0) | (row == 3)) & mine)
        def _():
            for i in range(3):
                self.hop(jnp.where(row == 0, 3 - i, i), t % 2, False)

    def slot(self, t, j):
        dp, row, col = self.pos
        mine = col == t // 2
        k = t % 2

        @pl.when(((row == 1) | (row == 2)) & mine)
        def _():
            self.hop(jnp.where(row == 1, 3 - j, j), k, True)
            if j == 1:
                self.hop(jnp.where(row == 1, 0, 3), k, True)

    def final(self, k, total):
        dp, row, col = self.pos
        landed(self.at(self.sib_in, row, k), self.r_sib.at[row, k])
        total[...] = self.at(self.own, row, k)[...].astype(F32) + self.at(self.sib_in, row, k)[...].astype(F32)

        @pl.when(row > 0)
        def _():
            landed(self.at(self.line_in, row, k), self.r_line.at[row, k])
            total[...] += self.at(self.line_in, row, k)[...].astype(F32)

        @pl.when(row < 3)
        def _():
            landed(self.at(self.line_in, 4, k), self.r_line.at[4, k])
            total[...] += self.at(self.line_in, 4, k)[...].astype(F32)

    def drain(self):
        dp, row, col = self.pos
        for b in range(4):
            for k in range(2):
                @pl.when(row < b)
                def _():
                    self.up(b, k).wait_send()

                @pl.when(row > b)
                def _():
                    self.down(b, k).wait_send()


class GradReduce:
    SEMS = ((4,),) * 6

    def __init__(self, grad, peers, part, place, shared, sems, pos):
        self.grad, self.peers, self.part, self.place, self.shared = grad, peers, part, place, shared
        self.s1, self.r1, self.s2, self.r2, self.s3, self.r3 = sems
        self.pos = pos
        self.rows = grad.shape[1] // 4

    def quarter(self, ref, q):
        return ref.at[:, span(q * self.rows, self.rows)]

    def first(self, e):
        dp, row, col = self.pos
        return remote(
            self.quarter(self.grad, dp ^ e), self.peers.at[e - 1], self.s1.at[e], self.r1.at[e],
            (dp ^ e, row, col),
        )

    def second(self, d):
        dp, row, col = self.pos
        target = lax.rem(row + d, 4)
        return [
            remote(
                self.part.at[target, :, pl.ds(c0, cols)], dst, self.s2.at[d], self.r2.at[d], (dp, target, col)
            )
            for dst, c0, cols in self.place(row, dp)
        ]

    def third(self, e):
        dp, row, col = self.pos
        return remote(self.shared(dp), self.shared(dp), self.s3.at[e], self.r3.at[e], (dp ^ e, row, col))

    def start(self):
        for e in (3, 1, 2):
            self.first(e).start()

    def own(self):
        dp, row, col = self.pos
        return [
            pltpu.make_async_copy(self.part.at[row, :, pl.ds(c0, cols)], dst, self.s2.at[0])
            for dst, c0, cols in self.place(row, dp)
        ]

    def sum_and_spread(self):
        dp, row, col = self.pos
        for e in (1, 2, 3):
            landed(self.peers.at[e - 1], self.r1.at[e])

        for d in (2, 1, 3, 0):
            b = lax.rem(row + d, 4)
            total = self.grad.at[b, span(dp * self.rows, self.rows)][...].astype(F32)
            for e in range(3):
                total = total + self.peers[e, b].astype(F32)
            self.part[b] = total.astype(BF)
            for c in self.own() if d == 0 else self.second(d):
                c.start()

    def share(self):
        pltpu.make_async_copy(self.part.at[0], self.part.at[0], self.s2.at[0]).wait()
        for d in (1, 2, 3):
            landed(self.part.at[0], self.r2.at[d])
        for e in (3, 1, 2):
            self.third(e).start()

    def finish(self):
        dp, row, col = self.pos
        for e in (1, 2, 3):
            landed(self.shared(dp), self.r3.at[e])
        for e in (1, 2, 3):
            self.first(e).wait_send()
            left(self.part.at[0], self.s2.at[e])
            self.third(e).wait_send()


def unrope(gt, cosv, sinv):
    rows = []
    for h in range(2):
        o = h * HD
        a, b = gt[o : o + 8], gt[o + 8 : o + 16]
        rows += [a * cosv + b * sinv, b * cosv - a * sinv, gt[o + 16 : o + HD]]
    return jnp.concatenate(rows, 0)


def layer_kernel(
    x, cot, wq, wu, wo, wd, seg, vec,
    out_o, gin_o, small_o, cols_o, fq_o, fu_o, fo_o, fd_o,
    xf, nrm, cf, w1, w2, q_v, k_v, v_v, tr_v, att_v, da, act_v, gp_v, raw, dqt, dka, dva,
    stat, lse, delta, cs, rng, gbs, d1,
    own_a, sib_a, line_a, own_b, sib_b, line_b, stage, total,
    gq, pq, tq, gu, pu, tu, go, po, to, gd, pd, td,
    x_v, out_v, gin_v, send_st, st, sums, sums_in, small, small_sib, small_in,
    *sems,
):
    pos = where()
    dp, row, col = pos
    toks = seg.shape[1]
    half = toks // 2
    hc = wq.shape[1] // 12
    fc = wu.shape[1] // 4
    h3 = 3 * hc
    depth = wq.shape[0]
    scale = 1.0 / math.sqrt(HD)
    taken = [0]

    def take(cls):
        first = taken[0]
        taken[0] = first + len(cls.SEMS)
        return sems[first : taken[0]]

    X = LineGather(x, xf, take(LineGather), pos)
    C = LineGather(cot, cf, take(LineGather), pos)

    def pieces1(t):
        return [(wq, 0, depth, (4 * j + t) * hc, hc, 0, j * hc) for j in range(3)] + [
            (wu, 0, depth, t * fc, fc, 0, h3)
        ]

    def pieces2(t):
        return [(wo, t * hc, hc, 0, depth, 0, 0), (wd, t * fc, fc, 0, depth, hc, 0)]

    W1 = WeightGather(w1, pieces1, take(WeightGather), pos)
    W2 = WeightGather(w2, pieces2, take(WeightGather), pos)
    A = LineReduce(own_a, sib_a, line_a, take(LineReduce), pos)
    B = LineReduce(own_b, sib_b, line_b, take(LineReduce), pos)

    def wide(ref, width):
        return lambda s, q: [
            (ref.at[span(q * (depth // 4), depth // 4), span((j * 4 + s) * width, width)], j * width, width)
            for j in range(ref.shape[1] // (4 * width))
        ]

    def wide_share(ref):
        return lambda q: ref.at[span(q * (depth // 4), depth // 4)]

    def tall(ref):
        n = ref.shape[1] // 4
        return lambda s, q: [(ref.at[s, span(q * n, n)], 0, depth)]

    def tall_share(ref):
        n = ref.shape[1] // 4
        return lambda q: ref.at[:, span(q * n, n)]

    GQ = GradReduce(gq, pq, tq, wide(fq_o, hc), wide_share(fq_o), take(GradReduce), pos)
    GU = GradReduce(gu, pu, tu, wide(fu_o, fc), wide_share(fu_o), take(GradReduce), pos)
    GO = GradReduce(go, po, to, tall(fo_o), tall_share(fo_o), take(GradReduce), pos)
    GD = GradReduce(gd, pd, td, tall(fd_o), tall_share(fd_o), take(GradReduce), pos)
    gs, gr, misc, s_st, r_st, s_sum, r_sum, s_row, r_row, s_small, r_small = sems[taken[0] :]

    greet(dp, row, col)
    W1.start()
    X.send_own(0)
    X.local().start()
    x_copy = pltpu.make_async_copy(x, x_v, misc.at[0])
    x_copy.start()
    at_gain = h3 * 4 + fc * 4
    gbs[pl.ds(row, 1)] = jnp.zeros((1, 8, depth), F32)
    gbs[pl.ds(row, 1), 0:1, :] = vec[0:1, at_gain : at_gain + depth][None]
    gbs[pl.ds(row, 1), 1:2, :] = vec[0:1, at_gain + depth : at_gain + 2 * depth][None]

    def gain_copy(d):
        return remote(gbs.at[row], gbs.at[row], gs.at[d], gr.at[d], (dp, lax.rem(row + d, 4), col))

    for d in (1, 2, 3):
        gain_copy(d).start()

    labels = seg[...]
    start = jnp.zeros_like(labels)
    for d in range(1, 8):
        below = jnp.sum((labels == d - 1).astype(F32), 1, keepdims=True).astype(jnp.int32)
        start = start + jnp.where(labels >= d, below, 0)
    index = lax.broadcasted_iota(jnp.int32, labels.shape, 1)
    place = index - start
    rng[0:1, :] = start
    rng[1:2, :] = place
    power = lax.broadcasted_iota(jnp.int32, (8, 1), 0).astype(F32) * (-2.0 * math.log(10000.0) / ROT)
    ang = place.astype(F32) * jnp.exp(power)
    cs[0:8, :] = jnp.cos(ang)
    cs[8:16, :] = jnp.sin(ang)
    bias = jnp.concatenate(
        [vec[0:1, span((4 * j + row) * hc, hc)] for j in range(3)] + [vec[0:1, span(12 * hc + row * fc, fc)]], 1
    )
    dka[...] = jnp.zeros_like(dka)
    dva[...] = jnp.zeros_like(dva)
    weights = w1.reshape(w1.shape[0] * w1.shape[1], w1.shape[2])

    def project(t):
        def token_step(i, _):
            at = span(t * BT + i * TC, TC)
            blocks = [xf[b, at, :].astype(F32) for b in range(4)]
            one = (blocks[0] + blocks[1]) + (blocks[2] + blocks[3])
            two = (blocks[0] * blocks[0] + blocks[1] * blocks[1]) + (
                blocks[2] * blocks[2] + blocks[3] * blocks[3]
            )
            mean = jnp.sum(one, 1, keepdims=True) * (1.0 / D)
            var = jnp.sum(two, 1, keepdims=True) * (1.0 / D) - mean * mean
            inv = lax.rsqrt(var + EPSILON)
            lane = lax.broadcasted_iota(jnp.int32, (TC, 128), 1)
            stat[at, :] = jnp.where(lane == 0, mean, inv)
            parts = []
            for b in range(4):
                n = ((blocks[b] - mean) * inv * gbs[b, 0:1, :] + gbs[b, 1:2, :]).astype(BF)
                nrm[b, at, :] = n
                parts.append(n)
            acc = dot(jnp.concatenate(parts, 1), weights[...]) + bias
            cosv, sinv = cs[0:8, at], cs[8:16, at]
            q_v[at, :] = unrope(acc[:, 0:128].T, cosv, -sinv).T.astype(BF)
            k_v[at, :] = unrope(acc[:, 128:256].T, cosv, -sinv).T.astype(BF)
            v_v[at, :] = acc[:, 256:384].astype(BF)
            tr_v[:, at] = acc[:, 256:384].T.astype(BF)
            up = acc[:, 384:]
            phi = 0.5 * (1.0 + lax.erf(up * (1.0 / math.sqrt(2.0))))
            act_v[at, :] = (up * phi).astype(BF)
            gp_v[at, :] = (phi + up * jnp.exp(-0.5 * up * up) * (1.0 / math.sqrt(2.0 * math.pi))).astype(BF)
            return 0

        lax.fori_loop(0, BT // TC, token_step, 0)

    def allowed(k0, at):
        kidx = lax.broadcasted_iota(jnp.int32, (BK, BT), 0) + k0 - rng[0:1, at]
        return (kidx >= 0) & (kidx <= rng[1:2, at])

    def attend(t):
        at = pl.ds(t * BT, BT)
        qs = q_v[at, :] * BF(scale)
        heads = [jnp.where(lane_mask(h, BT), qs, BF(0)) for h in range(2)]

        def k_step(kb, carry):
            k0 = pl.multiple_of(kb * BK, BK)
            kk = k_v[pl.ds(k0, BK), :]
            ok = allowed(k0, at)
            new = []
            for h in range(2):
                m, l, acc = carry[h]
                s = jnp.where(ok, dot(kk, heads[h], NT), MASKED)
                m2 = jnp.maximum(m, jnp.max(s, 0, keepdims=True))
                p = jnp.exp(s - m2)
                c = jnp.exp(m - m2)
                l = l * c + jnp.sum(p, 0, keepdims=True)
                vt = tr_v[h * HD : (h + 1) * HD, pl.ds(k0, BK)]
                acc = acc * c + dot(vt, p.astype(BF))
                new.append((m2, l, acc))
            return tuple(new)

        init = tuple(
            (jnp.full((1, BT), -1e30, F32), jnp.zeros((1, BT), F32), jnp.zeros((HD, BT), F32))
            for _ in range(2)
        )
        res = lax.fori_loop(0, (t + 1) * (BT // BK), k_step, init)
        for h in range(2):
            m, l, acc = res[h]
            raw[h * HD : (h + 1) * HD, at] = acc / l
            lse[h : h + 1, at] = m + jnp.log(l)
        att_v[at, :] = raw[:, at].T.astype(BF)

    def out_part(t):
        at = pl.ds(t * BT, BT)
        joined = jnp.concatenate([att_v[at, :], act_v[at, :]], 1)
        A.produce(t, stage, lambda b: dot(joined, w2[b]))
        A.edge(t)

    def joined_back(t):
        def chunk(i, _):
            at = span(t * BT + i * TC, TC)
            dj = dot(
                jnp.concatenate([cf[b, at, :] for b in range(4)], 1),
                jnp.concatenate([w2[b] for b in range(4)], 1),
                NT,
            )
            d_att = dj[:, 0:128].astype(BF)
            da[at, :] = d_att
            d1[at, 384:] = (dj[:, 128:] * gp_v[at, :].astype(F32)).astype(BF)
            prod = d_att.astype(F32).T * raw[:, at]
            for h in range(2):
                delta[h : h + 1, at] = jnp.sum(prod[h * HD : (h + 1) * HD], 0, keepdims=True)
            return 0

        lax.fori_loop(0, BT // TC, chunk, 0)

    def attend_back(t, lo, hi):
        at = pl.ds(t * BT, BT)
        qs = q_v[at, :] * BF(scale)
        do = da[at, :]
        qh = [jnp.where(lane_mask(h, BT), qs, BF(0)) for h in range(2)]
        doh = [jnp.where(lane_mask(h, BT), do, BF(0)) for h in range(2)]
        if lo == 0:
            dqt[...] = jnp.zeros_like(dqt)

        def k_step(kb, _):
            k0 = pl.multiple_of(kb * BK, BK)
            ka = pl.ds(k0, BK)
            kk = k_v[ka, :]
            vv = v_v[ka, :]
            ok = allowed(k0, at)
            dk, dv = dka[ka, :], dva[ka, :]
            for h in range(2):
                s = jnp.where(ok, dot(kk, qh[h], NT), MASKED)
                p = jnp.exp(s - lse[h : h + 1, at])
                ds = (p * (dot(vv, doh[h], NT) - delta[h : h + 1, at])).astype(BF)
                dv = dv + dot(p.astype(BF), doh[h])
                dk = dk + dot(ds, qh[h])
                rows = slice(h * HD, (h + 1) * HD)
                dqt[rows, :] += dot(tr_v[rows, ka], ds)
            dka[ka, :] = dk
            dva[ka, :] = dv
            return 0

        lax.fori_loop(lo, hi, k_step, 0)

    def finish_back(t):
        at = pl.ds(t * BT, BT)
        cosv, sinv = cs[0:8, at], cs[8:16, at]
        d1[at, 0:128] = unrope(dqt[...] * scale, cosv, sinv).T.astype(BF)
        d1[at, 128:256] = unrope(dka[at, :].T, cosv, sinv).T.astype(BF)
        d1[at, 256:384] = dva[at, :].astype(BF)

    def norm_part(t):
        rows = d1[pl.ds(t * BT, BT), :]
        B.produce(t, stage, lambda b: dot(rows, w1[b], NT))

    X.step(1, 0)
    W1.forward()
    X.step(2, 0)
    X.step(3, 0)
    X.send_own(1)
    W2.start()
    for d in (1, 2, 3):
        landed(gbs.at[0], gr.at[d])
    X.local().wait()
    W1.arrived()
    X.ready(0)
    project(0)
    X.step(1, 1)
    X.ready(2)
    project(2)
    X.step(2, 1)
    attend(0)
    X.step(3, 1)
    C.send_own(1)
    C.local().start()
    X.ready(1)
    project(1)
    W2.forward()
    X.ready(3)
    project(3)
    C.step(1, 1)
    attend(1)
    W2.arrived()
    out_part(0)
    A.wait_stage(0, stage)
    out_part(1)
    C.step(2, 1)
    attend(2)
    A.slot(0, 0)
    A.slot(0, 1)
    out_part(2)
    C.step(3, 1)
    C.send_own(0)
    A.slot(1, 0)
    attend(3)
    A.slot(1, 1)
    A.wait_stage(2, stage)
    out_part(3)

    def turn(i, _):
        at = span(i * BT, BT)
        tr_v[:, at] = k_v[at, :].astype(F32).T.astype(BF)
        return 0

    lax.fori_loop(0, toks // BT, turn, 0)
    C.local().wait()
    C.ready(3)
    joined_back(3)
    C.step(1, 0)
    A.slot(2, 0)
    attend_back(3, 0, 3)
    A.slot(2, 1)
    attend_back(3, 3, 6)
    C.step(2, 0)
    A.slot(3, 0)
    attend_back(3, 6, 8)
    finish_back(3)
    A.slot(3, 1)
    A.wait_stage(1, stage)
    A.wait_stage(3, stage)
    norm_part(3)
    B.edge(3)
    C.step(3, 0)
    C.ready(1)
    joined_back(1)
    C.ready(2)
    joined_back(2)
    C.ready(0)
    joined_back(0)
    B.slot(3, 0)
    for b in range(4):
        go[b] = dot(att_v[...], cf[b], TN).astype(BF)
        gd[b] = dot(act_v[...], cf[b], TN).astype(BF)
    GO.start()
    GD.start()
    B.slot(3, 1)
    for b in range(4):
        gu[b] = dot(nrm[b], d1[:, 384:], TN).astype(BF)
    GU.start()
    attend_back(2, 0, 6)
    finish_back(2)
    B.wait_stage(3, stage)
    norm_part(2)
    B.edge(2)
    attend_back(1, 0, 4)
    finish_back(1)
    B.slot(2, 0)
    B.wait_stage(2, stage)
    norm_part(1)
    B.edge(1)
    GO.sum_and_spread()
    GD.sum_and_spread()
    B.slot(2, 1)
    attend_back(0, 0, 2)
    finish_back(0)
    B.wait_stage(1, stage)
    norm_part(0)
    B.edge(0)
    B.slot(1, 0)
    for b in range(4):
        gq[b] = dot(nrm[b], d1[:, 0:384], TN).astype(BF)
    GQ.start()
    B.slot(1, 1)
    sums[0] = dot(jnp.ones((8, toks), BF), d1[...])

    def sum_copy(e):
        return remote(sums.at[0], sums_in.at[e - 1], s_sum.at[e], r_sum.at[e], (dp ^ e, row, col))

    def row_copy(d):
        return remote(sums.at[1], cols_o.at[row], s_row.at[d], r_row.at[d], (dp, lax.rem(row + d, 4), col))

    for e in (3, 1, 2):
        sum_copy(e).start()
    GU.sum_and_spread()
    B.slot(0, 0)
    GO.share()
    GD.share()
    B.slot(0, 1)
    for e in (1, 2, 3):
        landed(sums_in.at[e - 1], r_sum.at[e])
    sums[1] = (sums[0] + sums_in[0]) + (sums_in[1] + sums_in[2])
    for d in (1, 2, 3):
        row_copy(d).start()
    own_cols = pltpu.make_async_copy(sums.at[1], cols_o.at[row], misc.at[4])
    own_cols.start()
    GQ.sum_and_spread()
    GU.share()

    x_copy.wait()
    at_obias = at_gain + 2 * depth

    def out_copy(k):
        at = pl.ds(k * BT, BT)
        return pltpu.make_async_copy(out_v.at[at], out_o.at[at], misc.at[1 + k])

    for k in range(2):
        at = pl.ds(k * BT, BT)
        A.final(k, total)
        out_v[at, :] = (
            x_v[at, :].astype(F32) + total[...] + vec[0:1, at_obias : at_obias + depth]
        ).astype(BF)
        out_copy(k).start()

    def stat_copy(d, k):
        return remote(
            send_st.at[k], st.at[d - 1, k], s_st.at[d, k], r_st.at[d, k], (dp, lax.rem(row + d, 4), col)
        )

    gain = vec[0:1, at_gain : at_gain + depth]
    small[...] = jnp.zeros_like(small)

    def centred(k):
        at = pl.ds(k * BT, BT)
        mine = span(col * half + k * BT, BT)
        mean, inv = stat[mine, 0:1], stat[mine, 1:2]
        return (x_v[at, :].astype(F32) - mean) * inv, inv, cf.at[row, mine][...].astype(F32)

    for k in (1, 0):
        B.final(k, total)
        at = pl.ds(k * BT, BT)
        dn = total[...]
        xh, inv, ct = centred(k)
        dc = dn * gain
        s0 = jnp.sum(dc, 1, keepdims=True)
        s1 = jnp.sum(dc * xh, 1, keepdims=True)
        lane = lax.broadcasted_iota(jnp.int32, (BT, 128), 1)
        send_st[k] = jnp.where(lane == 0, s0, jnp.where(lane == 1, s1, 0.0)).T[0:8, :]
        for d in (2, 1, 3):
            stat_copy(d, k).start()
        gin_v[at, :] = dc
        small[0, 0:1, :] += jnp.sum(dn * xh, 0, keepdims=True)
        small[0, 1:2, :] += jnp.sum(dn, 0, keepdims=True)
        small[0, 2:3, :] += jnp.sum(ct, 0, keepdims=True)

    sib_small = remote(small.at[0], small_sib, s_small.at[0], r_small.at[0], (dp, row, 1 - col))
    sib_small.start()

    def small_copy(e):
        return remote(small.at[1], small_in.at[e - 1], s_small.at[e], r_small.at[e], (dp ^ e, row, col))

    GQ.share()
    landed(small_sib, r_small.at[0])
    small[1] = small[0] + small_sib[...]
    for e in (3, 1, 2):
        small_copy(e).start()

    def gin_copy(k):
        at = pl.ds(k * BT, BT)
        return pltpu.make_async_copy(gin_v.at[at], gin_o.at[at], misc.at[5 + k])

    for k in (1, 0):
        at = pl.ds(k * BT, BT)
        acc = send_st[k]
        for d in (1, 2, 3):
            landed(st.at[d - 1, k], r_st.at[d, k])
            acc = acc + st[d - 1, k]
        both = jnp.concatenate([acc, jnp.zeros((120, BT), F32)], 0).T
        xh, inv, ct = centred(k)
        gin_v[at, :] = inv * (gin_v[at, :] - both[:, 0:1] * (1.0 / D) - xh * (both[:, 1:2] * (1.0 / D))) + ct
        gin_copy(k).start()
    for e in (1, 2, 3):
        landed(small_in.at[e - 1], r_small.at[e])
    small_o[...] = (small[1] + small_in[0]) + (small_in[1] + small_in[2])

    X.drain()
    C.drain()
    W1.drain()
    W2.drain()
    for d in (1, 2, 3):
        gain_copy(d).wait_send()
        for k in range(2):
            stat_copy(d, k).wait_send()
        row_copy(d).wait_send()
        sum_copy(d).wait_send()
        small_copy(d).wait_send()
        landed(sums.at[1], r_row.at[d])
    sib_small.wait_send()
    A.drain()
    B.wait_stage(0, stage)
    B.drain()
    own_cols.wait()
    for k in range(2):
        out_copy(k).wait()
        gin_copy(k).wait()
    GO.finish()
    GD.finish()
    GU.finish()
    GQ.finish()


def layer(x, cot, wq, wu, wo, wd, seg, vec):
    toks = seg.shape[1]
    half = toks // 2
    depth = wq.shape[0]
    hc, fc = wq.shape[1] // 12, wu.shape[1] // 4
    h3 = 3 * hc
    sd = jax.ShapeDtypeStruct
    V = pltpu.VMEM
    grads = []
    for r, c in ((depth, h3), (depth, fc), (hc, depth), (fc, depth)):
        grads += [V((4, r, c), BF), V((3, 4, r // 4, c), BF), V((4, r // 4, c), BF)]
    sems = (
        LineGather.SEMS * 2 + WeightGather.SEMS * 2 + LineReduce.SEMS * 2 + GradReduce.SEMS * 4
        + ((4,), (4,), (8,), (4, 2), (4, 2), (4,), (4,), (4,), (4,), (4,), (4,))
    )
    return pl.pallas_call(
        layer_kernel,
        name="layer",
        out_shape=(
            sd((half, depth), BF), sd((half, depth), F32), sd((8, depth), F32), sd((4, 8, h3 + fc), F32),
            sd((depth, 12 * hc), BF), sd((depth, 4 * fc), BF), sd((4, hc, depth), BF), sd((4, fc, depth), BF),
        ),
        in_specs=[hbm()] * 6 + [vmem()] * 2,
        out_specs=(hbm(), hbm(), vmem(), hbm(), hbm(), hbm(), hbm(), hbm()),
        scratch_shapes=[
            V((4, toks, depth), BF), V((4, toks, depth), BF), V((4, toks, depth), BF),
            V((4, depth, h3 + fc), BF), V((4, hc + fc, depth), BF),
            V((toks, hc), BF), V((toks, hc), BF), V((toks, hc), BF), V((hc, toks), BF),
            V((toks, hc), BF), V((toks, hc), BF), V((toks, fc), BF), V((toks, fc), BF),
            V((hc, toks), F32), V((hc, BT), F32), V((toks, hc), F32), V((toks, hc), F32),
            V((toks, 128), F32), V((8, toks), F32), V((8, toks), F32), V((16, toks), F32),
            V((8, toks), jnp.int32), V((4, 8, depth), F32), V((toks, h3 + fc), BF),
            V((4, half, depth), BF), V((4, half, depth), BF), V((5, half, depth), BF),
            V((4, half, depth), BF), V((4, half, depth), BF), V((5, half, depth), BF),
            V((4, BT, depth), BF), V((BT, depth), F32),
            *grads,
            V((half, depth), BF), V((half, depth), BF), V((half, depth), F32),
            V((2, 8, BT), F32), V((3, 2, 8, BT), F32), V((2, 8, h3 + fc), F32), V((3, 8, h3 + fc), F32),
            V((2, 8, depth), F32), V((8, depth), F32), V((3, 8, depth), F32),
            *dmas(*sems),
        ],
        compiler_params=pltpu.CompilerParams(
            collective_id=0, has_side_effects=True, vmem_limit_bytes=62 * 2**20
        ),
    )(x, cot, wq, wu, wo, wd, seg, vec)


def per_device_sliced(
    inputs, segments, ln_gain, ln_bias, w_qkv, b_qkv, w_out, w_up, b_up, w_down, out_bias, cotangent
):
    nrow = lax.axis_size("row")
    dpart = inputs.shape[1]
    hcols = w_qkv.shape[2] // nrow
    h3 = 3 * hcols
    vec = jnp.concatenate([b_qkv.reshape(-1), b_up, ln_gain, ln_bias, out_bias]).astype(F32)[None]
    layer_out, grad_inputs, small, cols, fq, fu, fo, fd = layer(
        inputs, cotangent, w_qkv.reshape(dpart, -1), w_up, w_out, w_down, segments, vec
    )
    cols = cols[:, 0]
    grad_b_qkv = cols[:, :h3].reshape(nrow, 3, hcols).transpose(1, 0, 2).reshape(3, -1)
    return (
        layer_out, grad_inputs, small[0], small[1],
        fq.astype(F32).reshape(w_qkv.shape), grad_b_qkv,
        fo.reshape(w_out.shape).astype(F32), fu.astype(F32), cols[:, h3:].reshape(-1),
        fd.reshape(w_down.shape).astype(F32), small[2],
    )


FLOOR_INIT = -1e30


def doc_positions(labels):
    token_index = jnp.arange(labels.shape[1], dtype=jnp.int32)
    flags = jnp.concatenate(
        [jnp.ones((labels.shape[0], 1), dtype=jnp.bool_), labels[:, 1:] != labels[:, :-1]], 1
    )
    starts = lax.cummax(jnp.where(flags, token_index[None, :], 0), axis=1)
    return token_index[None, :] - starts


def rotate(tensor_in, positions):
    half_rot = ROT // 2
    inverse = 10000.0 ** (-(jnp.arange(half_rot, dtype=jnp.float32) * 2.0 / ROT))
    angles = positions.astype(jnp.float32)[:, None] * inverse[None, :]
    cosines = jnp.cos(angles)[:, None, :]
    sine_vals = jnp.sin(angles)[:, None, :]
    first_half = tensor_in[..., :half_rot]
    second_half = tensor_in[..., half_rot:ROT]
    rest_dims = tensor_in[..., ROT:]
    return jnp.concatenate(
        [
            first_half * cosines - second_half * sine_vals,
            second_half * cosines + first_half * sine_vals,
            rest_dims,
        ],
        -1,
    )


def slice_rows(array_in, first_row, row_count, axis_num=0):
    return lax.dynamic_slice_in_dim(array_in, first_row, row_count, axis_num)


def put_rows(array_in, update, first_row, axis_num=0):
    return lax.dynamic_update_slice_in_dim(array_in, update, first_row, axis_num)


def block_pairs(query_blocks, key_blocks):
    q_list = jnp.repeat(jnp.arange(query_blocks, dtype=jnp.int32), key_blocks)
    k_list = jnp.tile(jnp.arange(key_blocks, dtype=jnp.int32), query_blocks)
    return (q_list, k_list)


def per_device_general(
    inputs, segments, ln_gain, ln_bias, w_qkv, b_qkv, w_out, w_up, b_up, w_down, out_bias, cotangent
):
    local_rows, feature_cols = inputs.shape
    part_count = lax.axis_size("row")
    row_index = lax.axis_index("row")
    head_cols = w_qkv.shape[2]
    head_count = head_cols // HD
    group_seqs = segments.shape[0]
    all_rows = group_seqs * SEQ_LEN
    span = all_rows // part_count
    query_blocks = span // span
    score_scale = 1.0 / math.sqrt(HD)
    labels = (segments + (jnp.arange(group_seqs, dtype=jnp.int32) * SEQ_LEN)[:, None]).reshape(-1)
    positions = doc_positions(segments).reshape(-1)
    token_index = jnp.arange(all_rows, dtype=jnp.int32)
    my_labels = slice_rows(labels, row_index * span, span)
    my_index = slice_rows(token_index, row_index * span, span)
    my_positions = slice_rows(positions, row_index * span, span)
    float_in = inputs.astype(jnp.float32)
    ln_sums = lax.psum((jnp.sum(float_in, 1), jnp.sum(float_in * float_in, 1)), "row")
    row_mean = ln_sums[0] / D
    row_var = ln_sums[1] / D - row_mean * row_mean
    inv_std = lax.rsqrt(row_var + EPSILON)
    centred = (float_in - row_mean[:, None]) * inv_std[:, None]
    normed = (centred * ln_gain.astype(jnp.float32) + ln_bias.astype(jnp.float32)).astype(
        jnp.bfloat16
    )
    gathered_hidden = lax.all_gather(normed, "col", axis=0, tiled=True)
    first_weights = jnp.concatenate([w_qkv.reshape(feature_cols, 3 * head_cols), w_up], 1)
    first_bias = jnp.concatenate(
        [b_qkv.reshape(3 * head_cols).astype(jnp.float32), b_up.astype(jnp.float32)]
    )
    first_out = (
        lax.psum_scatter(
            jnp.dot(
                slice_rows(gathered_hidden, jnp.int32(0), lax.axis_size("row") * span),
                first_weights,
                preferred_element_type=jnp.float32,
            ).astype(jnp.bfloat16),
            "row",
            scatter_dimension=0,
            tiled=True,
        ).astype(jnp.float32)
        + first_bias
    )

    def rotate_mine(tensor_in):
        return rotate(tensor_in, my_positions)

    query_lin = first_out[:, :head_cols].reshape(span, head_count, HD)
    key_lin = first_out[:, head_cols : 2 * head_cols].reshape(span, head_count, HD)
    query = rotate_mine(query_lin).astype(jnp.bfloat16)
    key_rows = rotate_mine(key_lin).astype(jnp.bfloat16)
    value_rows = (
        first_out[:, 2 * head_cols : 3 * head_cols]
        .reshape(span, head_count, HD)
        .astype(jnp.bfloat16)
    )
    up_lin = first_out[:, 3 * head_cols :]
    activated = jax.nn.gelu(up_lin, approximate=False).astype(jnp.bfloat16)

    def over_keys(fold_step, initial):
        return fold_step(
            initial,
            (
                lax.all_gather(key_rows, "row", axis=0, tiled=True),
                lax.all_gather(value_rows, "row", axis=0, tiled=True),
            ),
            jnp.int32(0),
        )

    def key_setup(pieces, first_row):
        row_count = pieces[0].shape[0]
        piece_labels = slice_rows(labels, first_row, row_count)
        piece_index = slice_rows(token_index, first_row, row_count)
        return (row_count, span, piece_labels, piece_index)

    def block_live(piece_labels, piece_index, key_size, q_block, k_block):
        q_labels = slice_rows(my_labels, q_block * span, span)
        q_index = slice_rows(my_index, q_block * span, span)
        k_labels = slice_rows(piece_labels, k_block * key_size, key_size)
        k_index = slice_rows(piece_index, k_block * key_size, key_size)
        return (
            (jnp.max(q_index) >= jnp.min(k_index))
            & (jnp.min(q_labels) <= jnp.max(k_labels))
            & (jnp.min(k_labels) <= jnp.max(q_labels))
        )

    def block_scores(pieces, piece_labels, piece_index, key_size, q_block, k_block):
        q_start = q_block * span
        k_start = k_block * key_size
        q_labels = slice_rows(my_labels, q_start, span)
        q_index = slice_rows(my_index, q_start, span)
        k_labels = slice_rows(piece_labels, k_start, key_size)
        k_index = slice_rows(piece_index, k_start, key_size)
        q_block_rows = slice_rows(query, q_start, span)
        k_block_rows = slice_rows(pieces[0], k_start, key_size)
        v_block_rows = slice_rows(pieces[1], k_start, key_size)
        scores = (
            jnp.einsum(
                "qhd,khd->hqk", q_block_rows, k_block_rows, preferred_element_type=jnp.float32
            )
            * score_scale
        )
        allowed = (q_labels[:, None] == k_labels[None, :]) & (k_index[None, :] <= q_index[:, None])
        scores = jnp.where(allowed[None], scores, MASKED)
        return (q_start, k_start, scores, q_block_rows, k_block_rows, v_block_rows)

    def forward_piece(running, pieces, first_row):
        row_count, key_size, piece_labels, piece_index = key_setup(pieces, first_row)
        q_list, k_list = block_pairs(query_blocks, row_count // key_size)

        def forward_pair_step(current, pair_ids):
            q_block, k_block = pair_ids

            def update(inner_state):
                row_max, row_sum, row_acc = inner_state
                q_start, k_start, scores, q_block_rows, k_block_rows, v_block_rows = block_scores(
                    pieces, piece_labels, piece_index, key_size, q_block, k_block
                )
                old_max = slice_rows(row_max, q_start, span, 1)
                new_max = jnp.maximum(old_max, jnp.max(scores, -1))
                weights = jnp.exp(scores - new_max[..., None])
                keep_part = jnp.exp(old_max - new_max)
                new_sum = slice_rows(row_sum, q_start, span, 1) * keep_part + jnp.sum(weights, -1)
                added = jnp.einsum(
                    "hqk,khd->hqd",
                    weights.astype(jnp.bfloat16),
                    v_block_rows,
                    preferred_element_type=jnp.float32,
                )
                new_acc = slice_rows(row_acc, q_start, span, 1) * keep_part[..., None] + added
                return (
                    put_rows(row_max, new_max, q_start, 1),
                    put_rows(row_sum, new_sum, q_start, 1),
                    put_rows(row_acc, new_acc, q_start, 1),
                )

            def forward_unchanged(inner_state):
                return inner_state

            is_live = block_live(piece_labels, piece_index, key_size, q_block, k_block)
            return (lax.cond(is_live, update, forward_unchanged, current), None)

        result, _ = lax.scan(forward_pair_step, running, (q_list, k_list))
        return result

    forward_init = (
        jnp.full((head_count, span), FLOOR_INIT, jnp.float32),
        jnp.zeros((head_count, span), jnp.float32),
        jnp.zeros((head_count, span, HD), jnp.float32),
    )
    row_max, row_sum, row_acc = over_keys(forward_piece, forward_init)
    log_total = row_max + jnp.log(row_sum)
    attention_raw = jnp.transpose(row_acc / row_sum[..., None], (1, 0, 2)).reshape(span, head_cols)
    attended = attention_raw.astype(jnp.bfloat16)
    joined = jnp.concatenate(
        (
            lax.all_gather(attended, "row", axis=0, tiled=True),
            lax.all_gather(activated, "row", axis=0, tiled=True),
        ),
        1,
    )
    second_weights = jnp.concatenate([w_out, w_down], 0)
    partial_out = lax.psum_scatter(
        jnp.dot(
            slice_rows(joined, jnp.int32(0), lax.axis_size("col") * local_rows),
            second_weights,
            preferred_element_type=jnp.float32,
        ).astype(jnp.bfloat16),
        "col",
        scatter_dimension=0,
        tiled=True,
    ).astype(jnp.float32)
    layer_out = (float_in + partial_out + out_bias.astype(jnp.float32)).astype(jnp.bfloat16)
    grad_full = lax.all_gather(cotangent, "col", axis=0, tiled=True)
    grad_out_bias = jnp.sum(grad_full, 0, dtype=jnp.float32)
    grad_second = lax.dot_general(
        joined, grad_full, (((0,), (0,)), ((), ())), preferred_element_type=jnp.float32
    )
    branch_back = lax.psum_scatter(
        lax.dot_general(
            slice_rows(grad_full, jnp.int32(0), lax.axis_size("row") * span),
            second_weights,
            (((1,), (1,)), ((), ())),
            preferred_element_type=jnp.float32,
        ).astype(jnp.bfloat16),
        "row",
        scatter_dimension=0,
        tiled=True,
    ).astype(jnp.float32)
    d_attended = branch_back[:, :head_cols].astype(jnp.bfloat16)
    d_activated = branch_back[:, head_cols:]
    _, gelu_back = jax.vjp(lambda tensor_in: jax.nn.gelu(tensor_in, approximate=False), up_lin)
    d_up = gelu_back(d_activated)[0].astype(jnp.bfloat16)
    d_out_heads = d_attended.reshape(span, head_count, HD)
    row_delta = jnp.transpose(
        jnp.sum((d_attended.astype(jnp.float32) * attention_raw).reshape(span, head_count, HD), -1)
    )

    def backward_piece(running, pieces, first_row):
        d_query_acc, d_key_all, d_value_all = running
        row_count, key_size, piece_labels, piece_index = key_setup(pieces, first_row)
        q_list, k_list = block_pairs(query_blocks, row_count // key_size)
        zero_keys = jnp.zeros((row_count, head_count, HD), jnp.float32)

        def backward_pair_step(current, pair_ids):
            q_block, k_block = pair_ids

            def update(inner_state):
                d_query_run, d_key_run, d_value_run = inner_state
                q_start, k_start, scores, q_block_rows, k_block_rows, v_block_rows = block_scores(
                    pieces, piece_labels, piece_index, key_size, q_block, k_block
                )
                probs_full = jnp.exp(scores - slice_rows(log_total, q_start, span, 1)[..., None])
                d_out_block = slice_rows(d_out_heads, q_start, span)
                d_probs = jnp.einsum(
                    "qhd,khd->hqk", d_out_block, v_block_rows, preferred_element_type=jnp.float32
                )
                d_scores = (
                    probs_full * (d_probs - slice_rows(row_delta, q_start, span, 1)[..., None])
                ).astype(jnp.bfloat16)
                q_added = (
                    jnp.einsum(
                        "hqk,khd->qhd", d_scores, k_block_rows, preferred_element_type=jnp.float32
                    )
                    * score_scale
                )
                k_added = (
                    jnp.einsum(
                        "hqk,qhd->khd", d_scores, q_block_rows, preferred_element_type=jnp.float32
                    )
                    * score_scale
                )
                v_added = jnp.einsum(
                    "hqk,qhd->khd",
                    probs_full.astype(jnp.bfloat16),
                    d_out_block,
                    preferred_element_type=jnp.float32,
                )
                return (
                    put_rows(
                        d_query_run, slice_rows(d_query_run, q_start, span) + q_added, q_start
                    ),
                    put_rows(
                        d_key_run, slice_rows(d_key_run, k_start, key_size) + k_added, k_start
                    ),
                    put_rows(
                        d_value_run, slice_rows(d_value_run, k_start, key_size) + v_added, k_start
                    ),
                )

            def backward_unchanged(inner_state):
                return inner_state

            is_live = block_live(piece_labels, piece_index, key_size, q_block, k_block)
            return (lax.cond(is_live, update, backward_unchanged, current), None)

        scanned, _ = lax.scan(
            backward_pair_step, (d_query_acc, zero_keys, zero_keys), (q_list, k_list)
        )
        d_query_acc, key_part, value_part = scanned
        d_key_all = put_rows(d_key_all, key_part, first_row)
        d_value_all = put_rows(d_value_all, value_part, first_row)
        return (d_query_acc, d_key_all, d_value_all)

    backward_init = (
        jnp.zeros((span, head_count, HD), jnp.float32),
        jnp.zeros((all_rows, head_count, HD), jnp.float32),
        jnp.zeros((all_rows, head_count, HD), jnp.float32),
    )
    d_query_rot, d_key_total, d_value_total = over_keys(backward_piece, backward_init)
    d_key_rot, d_value_mine = (
        lax.psum_scatter(
            d_key_total.reshape(all_rows, head_cols).astype(jnp.bfloat16),
            "row",
            scatter_dimension=0,
            tiled=True,
        ).astype(jnp.float32),
        lax.psum_scatter(
            d_value_total.reshape(all_rows, head_cols).astype(jnp.bfloat16),
            "row",
            scatter_dimension=0,
            tiled=True,
        ).astype(jnp.float32),
    )
    _, query_back = jax.vjp(rotate_mine, query_lin)
    _, key_back = jax.vjp(rotate_mine, key_lin)
    d_query_lin = query_back(d_query_rot)[0].reshape(span, head_cols).astype(jnp.bfloat16)
    d_key_lin = (
        key_back(d_key_rot.reshape(span, head_count, HD))[0]
        .reshape(span, head_cols)
        .astype(jnp.bfloat16)
    )
    d_first = jnp.concatenate([d_query_lin, d_key_lin, d_value_mine.astype(jnp.bfloat16), d_up], 1)
    d_first_full = lax.all_gather(d_first, "row", axis=0, tiled=True)
    grad_first_bias = jnp.sum(d_first_full, 0, dtype=jnp.float32)
    grad_first = lax.dot_general(
        gathered_hidden, d_first_full, (((0,), (0,)), ((), ())), preferred_element_type=jnp.float32
    )
    d_normed = lax.psum_scatter(
        lax.dot_general(
            slice_rows(d_first_full, jnp.int32(0), lax.axis_size("col") * local_rows),
            first_weights,
            (((1,), (1,)), ((), ())),
            preferred_element_type=jnp.float32,
        ).astype(jnp.bfloat16),
        "col",
        scatter_dimension=0,
        tiled=True,
    ).astype(jnp.float32)
    d_centred = d_normed * ln_gain.astype(jnp.float32)
    grad_stats = lax.psum((jnp.sum(d_centred, 1), jnp.sum(d_centred * centred, 1)), "row")
    grad_inputs = inv_std[:, None] * (
        d_centred - grad_stats[0][:, None] / D - centred * grad_stats[1][:, None] / D
    ) + cotangent.astype(jnp.float32)
    summed = (
        lax.psum(grad_first.astype(jnp.bfloat16), "dp").astype(jnp.float32),
        lax.psum(grad_second.astype(jnp.bfloat16), "dp").astype(jnp.float32),
        lax.psum(grad_first_bias.astype(jnp.bfloat16), "dp").astype(jnp.float32),
        lax.psum(grad_out_bias.astype(jnp.bfloat16), "dp").astype(jnp.float32),
    )
    norm_grads = lax.psum((jnp.sum(d_normed * centred, 0), jnp.sum(d_normed, 0)), ("dp", "col"))
    grad_w_qkv = summed[0][:, : 3 * head_cols].reshape(feature_cols, 3, head_cols)
    grad_w_up = summed[0][:, 3 * head_cols :]
    grad_w_out = summed[1][:head_cols]
    grad_w_down = summed[1][head_cols:]
    grad_b_qkv = summed[2][: 3 * head_cols].reshape(3, head_cols)
    grad_b_up = summed[2][3 * head_cols :]
    return (
        layer_out,
        grad_inputs,
        norm_grads[0],
        norm_grads[1],
        grad_w_qkv,
        grad_b_qkv,
        grad_w_out,
        grad_w_up,
        grad_b_up,
        grad_w_down,
        summed[3],
    )


def solution(mesh):
    placed = (
        P(("dp", "col"), "row"),
        P("dp", None),
        P("row"),
        P("row"),
        P("row", None, "col"),
        P(None, "col"),
        P("col", "row"),
        P("row", "col"),
        P("col"),
        P("col", "row"),
        P("row"),
        P(("dp", "col"), "row"),
    )
    size = dict(mesh.shape)
    sliced = (size["dp"], size["row"], size["col"]) == (4, 4, 2)
    return jax.shard_map(
        per_device_sliced if sliced else per_device_general,
        mesh=mesh,
        in_specs=placed,
        out_specs=(
            P(("dp", "col"), "row"),
            P(("dp", "col"), "row"),
            P("row"),
            P("row"),
            P("row", None, "col"),
            P(None, "col"),
            P("col", "row"),
            P("row", "col"),
            P("col"),
            P("col", "row"),
            P("row"),
        ),
        check_vma=False,
    )
```

```python
import math

import jax
import jax.numpy as jnp
from jax import lax
from jax.experimental import pallas as pl
from jax.experimental.pallas import tpu as pltpu
from jax.sharding import PartitionSpec as P

D = 1024
HD = 64
ROT = 16
SEQ_LEN = 2048
EPSILON = 1e-05
MASKED = -1000000000.0
BF = jnp.bfloat16
F32 = jnp.float32
NT = (((1,), (1,)), ((), ()))
NN = (((1,), (0,)), ((), ()))
TN = (((0,), (0,)), ((), ()))


def dot(a, b, dims=NN):
    return lax.dot_general(a, b, dims, preferred_element_type=F32)


BK = 512


def lane_mask(head, rows):
    lane = lax.broadcasted_iota(jnp.int32, (rows, 128), 1)
    return (lane >= head * HD) & (lane < (head + 1) * HD)


MESH = pl.DeviceIdType.MESH
TC = 256
BT = 512
HT = BT // 2


def vmem():
    return pl.BlockSpec(memory_space=pltpu.VMEM)


def hbm():
    return pl.BlockSpec(memory_space=pl.ANY)


def span(first, count):
    if not isinstance(first, int):
        first = pl.multiple_of(first, count & -count)
    return pl.ds(first, count)


def remote(src, dst, send, recv, dev):
    return pltpu.make_async_remote_copy(
        src_ref=src, dst_ref=dst, send_sem=send, recv_sem=recv, device_id=dev, device_id_type=MESH
    )


def landed(ref, sem):
    pltpu.make_async_copy(ref, ref, sem).wait()


def left(ref, sem):
    pltpu.make_async_copy(ref, ref, sem).wait()


def where():
    return lax.axis_index("dp"), lax.axis_index("row"), lax.axis_index("col")


def greet(dp, row, col):
    bar = pltpu.get_barrier_semaphore()
    for d in range(1, 4):
        pl.semaphore_signal(bar, inc=1, device_id=(dp ^ d, row, col), device_id_type=MESH)
        pl.semaphore_signal(bar, inc=1, device_id=(dp, lax.rem(row + d, 4), col), device_id_type=MESH)
    pl.semaphore_signal(bar, inc=1, device_id=(dp, row, 1 - col), device_id_type=MESH)
    pl.semaphore_wait(bar, 7)


def dmas(*shapes):
    return [pltpu.SemaphoreType.DMA(s) for s in shapes]


class LineGather:
    SEMS = ((4, 4),) * 4 + ((7, 4),) * 2 + ((1,),)

    def __init__(self, own, full, sems, pos):
        self.own, self.full, self.pos = own, full, pos
        self.su, self.sd, self.ru, self.rd, self.ss, self.rs, self.loc = sems

    def at(self, block, t, other=False):
        dp, row, col = self.pos
        return self.full.at[block, span(t * BT + (1 - col if other else col) * HT, HT)]

    def up(self, step, t):
        dp, row, col = self.pos
        ref = self.at(row - step, t)
        return remote(ref, ref, self.su.at[step, t], self.ru.at[step, t], (dp, row + 1, col))

    def down(self, step, t):
        dp, row, col = self.pos
        ref = self.at(row + step, t)
        return remote(ref, ref, self.sd.at[step, t], self.rd.at[step, t], (dp, row - 1, col))

    def sib(self, step, sign, t):
        dp, row, col = self.pos
        i = step + 3 * (sign < 0)
        ref = self.at(row - sign * step, t)
        return remote(ref, ref, self.ss.at[i, t], self.rs.at[i, t], (dp, row, 1 - col))

    def half_at(self, k, other=False):
        dp, row, col = self.pos
        return self.full.at[row, span((1 - col if other else col) * 2 * BT + k * BT, BT)]

    def give(self, k):
        dp, row, col = self.pos
        return remote(
            self.own.at[pl.ds(k * BT, BT)], self.half_at(k), self.ss.at[0, k], self.rs.at[0, k], (dp, row, 1 - col)
        )

    def local(self):
        dp, row, col = self.pos
        return pltpu.make_async_copy(self.own, self.full.at[row, span(col * 2 * BT, 2 * BT)], self.loc.at[0])

    def start(self, order):
        for k in order:
            self.give(k).start()
        self.local().start()

    def send_own(self, t):
        dp, row, col = self.pos

        @pl.when(col != t // 2)
        def _():
            landed(self.half_at(t % 2, True), self.rs.at[0, t % 2])

        @pl.when(row < 3)
        def _():
            self.up(0, t).start()

        @pl.when(row > 0)
        def _():
            self.down(0, t).start()

    def step(self, s, t):
        dp, row, col = self.pos

        @pl.when(row >= s)
        def _():
            landed(self.at(row - s, t), self.ru.at[s - 1, t])

            @pl.when(row < 3)
            def _():
                self.up(s, t).start()

            self.sib(s, 1, t).start()

        @pl.when(row + s <= 3)
        def _():
            landed(self.at(row + s, t), self.rd.at[s - 1, t])

            @pl.when(row > 0)
            def _():
                self.down(s, t).start()

            self.sib(s, -1, t).start()

    def ready(self, t):
        dp, row, col = self.pos
        for s in range(1, 4):
            @pl.when(row >= s)
            def _():
                landed(self.at(row - s, t, True), self.rs.at[s, t])

            @pl.when(row + s <= 3)
            def _():
                landed(self.at(row + s, t, True), self.rs.at[s + 3, t])

    def drain(self):
        dp, row, col = self.pos
        for k in range(2):
            self.give(k).wait_send()
        for t in range(4):
            for s in range(0, 3):
                @pl.when((row >= s) & (row < 3))
                def _():
                    self.up(s, t).wait_send()

                @pl.when((row + s <= 3) & (row > 0))
                def _():
                    self.down(s, t).wait_send()
            for s in range(1, 4):
                @pl.when(row >= s)
                def _():
                    self.sib(s, 1, t).wait_send()

                @pl.when(row + s <= 3)
                def _():
                    self.sib(s, -1, t).wait_send()


class WeightGather:
    SEMS = ((4,), (4,), (4, 4), (4, 4), (4,))

    def __init__(self, full, pieces, sems, pos):
        self.full, self.pieces, self.pos = full, pieces, pos
        self.sz, self.rz, self.sp, self.rp, self.loc = sems
        self.quarter = full.shape[1] // 4

    def parts(self, block, q):
        seen = []
        for src, r0, rows, c0, cols, d0, e0 in self.pieces(0):
            seen.append((d0, rows))
        out = []
        for d0, rows in dict.fromkeys(seen):
            out.append(self.full.at[block, span(d0 + q * (rows // 4), rows // 4)])
        return out

    def bytes(self):
        return self.full.at[0, pl.ds(0, self.quarter)]

    def along(self, d):
        dp, row, col = self.pos
        target = lax.rem(row + d, 4)
        copies = []
        for src, r0, rows, c0, cols, d0, e0 in self.pieces(target):
            q = rows // 4
            copies.append(remote(
                src.at[span(r0 + dp * q, q), span(c0, cols)],
                self.full.at[row, span(d0 + dp * q, q), pl.ds(e0, cols)],
                self.sz.at[d], self.rz.at[d], (dp, target, col),
            ))
        return copies

    def across(self, d, e):
        dp, row, col = self.pos
        block = lax.rem(row + 4 - d, 4)
        return [
            remote(p, p, self.sp.at[d, e], self.rp.at[d, e], (dp ^ e, row, col)) for p in self.parts(block, dp)
        ]

    def local(self):
        dp, row, col = self.pos
        return [
            pltpu.make_async_copy(
                src.at[span(r0, rows), span(c0, cols)],
                self.full.at[row, pl.ds(d0, rows), pl.ds(e0, cols)], self.loc.at[i],
            )
            for i, (src, r0, rows, c0, cols, d0, e0) in enumerate(self.pieces(row))
        ]

    def start(self):
        for d in (2, 1, 3):
            for c in self.along(d):
                c.start()
        for c in self.local():
            c.start()

    def forward(self):
        for d in (1, 3, 2):
            landed(self.bytes(), self.rz.at[d])
            for e in (3, 1, 2):
                for c in self.across(d, e):
                    c.start()

    def arrived(self):
        for c in self.local():
            c.wait()
        for d in (1, 3, 2):
            for e in (1, 2, 3):
                landed(self.bytes(), self.rp.at[d, e])

    def drain(self):
        for d in (1, 2, 3):
            left(self.bytes(), self.sz.at[d])
            for e in (1, 2, 3):
                left(self.bytes(), self.sp.at[d, e])


class LineReduce:
    SEMS = ((4, 4),) * 3 + ((5, 4),)

    def __init__(self, own, sib, line, sems, pos):
        self.own, self.sib_in, self.line_in = own, sib, line
        self.s_sib, self.r_sib, self.s_line, self.r_line = sems
        self.pos = pos

    def sib(self, stage, b, t):
        dp, row, col = self.pos
        return remote(
            stage.at[t % 2, b], self.sib_in.at[b, t], self.s_sib.at[b, t], self.r_sib.at[b, t], (dp, row, 1 - col)
        )

    def up(self, b, t):
        dp, row, col = self.pos
        return remote(
            self.own.at[b, t], self.line_in.at[b, t], self.s_line.at[b, t], self.r_line.at[b, t], (dp, row + 1, col)
        )

    def down(self, b, t):
        dp, row, col = self.pos
        slot = jnp.where(b == row - 1, 4, b)
        return remote(
            self.own.at[b, t], self.line_in.at[slot, t], self.s_line.at[b, t], self.r_line.at[slot, t],
            (dp, row - 1, col),
        )

    def produce(self, t, stage, rows, fn):
        dp, row, col = self.pos

        there = rows(span(t * BT + (1 - col) * HT, HT))
        for b in (3, 0, 2, 1):
            stage[t % 2, b] = fn(there, b).astype(BF)
            self.sib(stage, b, t).start()
        here = rows(span(t * BT + col * HT, HT))
        for b in (3, 0, 2, 1):
            self.own[b, t] = fn(here, b).astype(BF)

    def wait_stage(self, t, stage):
        for b in range(4):
            self.sib(stage, b, t).wait_send()

    def hop(self, b, t, take):
        dp, row, col = self.pos
        landed(self.sib_in.at[b, t], self.r_sib.at[b, t])
        total = self.own[b, t].astype(F32) + self.sib_in[b, t].astype(F32)
        if take:
            landed(self.line_in.at[b, t], self.r_line.at[b, t])
            total = total + self.line_in[b, t].astype(F32)
        self.own[b, t] = total.astype(BF)

        @pl.when(row < b)
        def _():
            self.up(b, t).start()

        @pl.when(row > b)
        def _():
            self.down(b, t).start()

    def edge(self, t):
        dp, row, col = self.pos

        @pl.when((row == 0) | (row == 3))
        def _():
            for i in range(3):
                self.hop(jnp.where(row == 0, 3 - i, i), t, False)

    def slot(self, t, j):
        dp, row, col = self.pos

        @pl.when((row == 1) | (row == 2))
        def _():
            self.hop(jnp.where(row == 1, 3 - j, j), t, True)
            if j == 1:
                self.hop(jnp.where(row == 1, 0, 3), t, True)

    def final(self, t, total):
        dp, row, col = self.pos
        landed(self.sib_in.at[row, t], self.r_sib.at[row, t])
        total[...] = self.own[row, t].astype(F32) + self.sib_in[row, t].astype(F32)

        @pl.when(row > 0)
        def _():
            landed(self.line_in.at[row, t], self.r_line.at[row, t])
            total[...] += self.line_in[row, t].astype(F32)

        @pl.when(row < 3)
        def _():
            landed(self.line_in.at[4, t], self.r_line.at[4, t])
            total[...] += self.line_in[4, t].astype(F32)

    def drain(self):
        dp, row, col = self.pos
        for b in range(4):
            for t in range(4):
                @pl.when(row < b)
                def _():
                    self.up(b, t).wait_send()

                @pl.when(row > b)
                def _():
                    self.down(b, t).wait_send()


class GradReduce:
    SEMS = ((4,), (4,), (2,), (2,), (4,), (4,), (2,), (2,), (4,), (4,))

    def __init__(self, grad, near, far, mid, part, place, shared, sems, pos):
        self.grad, self.near, self.far, self.mid, self.part = grad, near, far, mid, part
        self.place, self.shared = place, shared
        self.s1, self.r1, self.sm, self.rm, self.s2, self.r2, self.s3, self.r3, self.s4, self.r4 = sems
        self.pos = pos
        self.rows = grad.shape[1] // 4
        self.n = self.rows // 2

    def cut(self, q, h):
        return self.grad.at[:, span(q * self.rows + h * self.n, self.n)]

    def peer(self, e):
        dp, row, col = self.pos
        return (dp ^ e, row, col)

    def first(self, i):
        dp, row, col = self.pos
        e = 1 + i // 2
        q = dp ^ (3 if i % 2 else e)
        return remote(self.cut(q, i // 2), self.near.at[i], self.s1.at[i], self.r1.at[i], self.peer(e))

    def middle(self, h):
        return remote(self.mid.at[h], self.far.at[h], self.sm.at[h], self.rm.at[h], self.peer(2 - h))

    def second(self, d):
        dp, row, col = self.pos
        target = lax.rem(row + d, 4)
        return [
            remote(
                self.part.at[target, :, pl.ds(c0, cols)], dst, self.s2.at[d], self.r2.at[d], (dp, target, col)
            )
            for dst, c0, cols in self.place(row, dp)
        ]

    def third(self, h):
        dp, row, col = self.pos
        ref = self.shared(dp, h)
        return remote(ref, ref, self.s3.at[h], self.r3.at[h], self.peer(2 - h))

    def fourth(self, i):
        dp, row, col = self.pos
        h = i // 2
        ref = self.shared(dp ^ (2 - h) if i % 2 else dp, h)
        return remote(ref, ref, self.s4.at[i], self.r4.at[i], self.peer(1 + h))

    def start(self):
        for i in (1, 3, 0, 2):
            self.first(i).start()

    def middle_sum(self):
        dp, row, col = self.pos
        for h in range(2):
            i = 2 * h + 1
            landed(self.near.at[i], self.r1.at[i])
            self.mid[h] = (self.cut(dp ^ (2 - h), h)[...].astype(F32) + self.near[i].astype(F32)).astype(BF)
            self.middle(h).start()

    def own(self):
        dp, row, col = self.pos
        return [
            pltpu.make_async_copy(self.part.at[row, :, pl.ds(c0, cols)], dst, self.s2.at[0])
            for dst, c0, cols in self.place(row, dp)
        ]

    def sum_and_spread(self):
        dp, row, col = self.pos
        for h in range(2):
            landed(self.near.at[2 * h], self.r1.at[2 * h])
            landed(self.far.at[h], self.rm.at[h])
        for d in (2, 1, 3, 0):
            b = lax.rem(row + d, 4)
            for h in range(2):
                total = self.grad.at[b, span(dp * self.rows + h * self.n, self.n)][...].astype(F32)
                total = total + self.near[2 * h, b].astype(F32) + self.far[h, b].astype(F32)
                self.part[b, h * self.n : (h + 1) * self.n, :] = total.astype(BF)
            for c in self.own() if d == 0 else self.second(d):
                c.start()

    def share(self):
        pltpu.make_async_copy(self.part.at[0], self.part.at[0], self.s2.at[0]).wait()
        for d in (1, 2, 3):
            landed(self.part.at[0], self.r2.at[d])
        self.third(0).start()
        self.third(1).start()
        self.fourth(0).start()
        self.fourth(2).start()

    def relay(self):
        dp, row, col = self.pos
        for h in range(2):
            landed(self.shared(dp, h), self.r3.at[h])
            self.fourth(2 * h + 1).start()

    def finish(self):
        dp, row, col = self.pos
        for i in range(4):
            landed(self.shared(dp, i // 2), self.r4.at[i])
            self.first(i).wait_send()
            self.fourth(i).wait_send()
        for h in range(2):
            self.middle(h).wait_send()
            self.third(h).wait_send()
        for d in (1, 2, 3):
            left(self.part.at[0], self.s2.at[d])


def unrope(gt, cosv, sinv):
    rows = []
    for h in range(2):
        o = h * HD
        a, b = gt[o : o + 8], gt[o + 8 : o + 16]
        rows += [a * cosv + b * sinv, b * cosv - a * sinv, gt[o + 16 : o + HD]]
    return jnp.concatenate(rows, 0)


def layer_kernel(
    x, cot, wq, wu, wo, wd, seg, vec,
    out_o, gin_o, small_o, cols_o, fq_o, fu_o, fo_o, fd_o,
    xf, nrm, cf, w1, w2, q_v, k_v, v_v, tr_v, att_v, da, act_v, gp_v, raw, dqt, dka, dva,
    stat, lse, delta, cs, rng, gbs, d1,
    own_a, sib_a, line_a, own_b, sib_b, line_b, stage, total,
    gq, nq, rq, mq, tq, gu, nu, ru, mu, tu, go, no, ro, mo, to, gd, nd, rd, md, td,
    out_v, gin_v, send_st, st, sums, sums_in, small, small_sib, small_in,
    *sems,
):
    pos = where()
    dp, row, col = pos
    toks = seg.shape[1]
    half = toks // 2
    hc = wq.shape[2] // 4
    fc = wu.shape[1] // 4
    h3 = 3 * hc
    depth = wq.shape[1]
    scale = 1.0 / math.sqrt(HD)
    taken = [0]

    def take(cls):
        first = taken[0]
        taken[0] = first + len(cls.SEMS)
        return sems[first : taken[0]]

    X = LineGather(x, xf, take(LineGather), pos)
    C = LineGather(cot, cf, take(LineGather), pos)

    def pieces1(t):
        return [(wq.at[j], 0, depth, t * hc, hc, 0, j * hc) for j in range(3)] + [
            (wu, 0, depth, t * fc, fc, 0, h3)
        ]

    def pieces2(t):
        return [(wo, t * hc, hc, 0, depth, 0, 0), (wd, t * fc, fc, 0, depth, hc, 0)]

    W1 = WeightGather(w1, pieces1, take(WeightGather), pos)
    W2 = WeightGather(w2, pieces2, take(WeightGather), pos)
    A = LineReduce(own_a, sib_a, line_a, take(LineReduce), pos)
    B = LineReduce(own_b, sib_b, line_b, take(LineReduce), pos)

    def rows_of(q):
        return span(q * (depth // 4), depth // 4)

    def rows_half(q, h):
        return span(q * (depth // 4) + h * (depth // 8), depth // 8)

    def place_q(s, q):
        return [(fq_o.at[j, rows_of(q), span(s * hc, hc)], j * hc, hc) for j in range(3)]

    def place_u(s, q):
        return [(fu_o.at[rows_of(q), span(s * fc, fc)], 0, fc)]

    def tall(ref):
        n = ref.shape[1] // 4
        return lambda s, q: [(ref.at[s, span(q * n, n)], 0, depth)]

    def tall_share(ref):
        n = ref.shape[1] // 4
        return lambda q, h: ref.at[:, span(q * n + h * (n // 2), n // 2)]

    GQ = GradReduce(gq, nq, rq, mq, tq, place_q, lambda q, h: fq_o.at[:, rows_half(q, h)], take(GradReduce), pos)
    GU = GradReduce(gu, nu, ru, mu, tu, place_u, lambda q, h: fu_o.at[rows_half(q, h)], take(GradReduce), pos)
    GO = GradReduce(go, no, ro, mo, to, tall(fo_o), tall_share(fo_o), take(GradReduce), pos)
    GD = GradReduce(gd, nd, rd, md, td, tall(fd_o), tall_share(fd_o), take(GradReduce), pos)
    gs, gr, misc, s_st, r_st, s_sum, r_sum, s_row, r_row, s_small, r_small, s_own, r_own = sems[taken[0] :]

    greet(dp, row, col)
    X.start((0, 1))
    at_gain = h3 * 4 + fc * 4
    gbs[pl.ds(row, 1)] = jnp.zeros((1, 8, depth), F32)
    gbs[pl.ds(row, 1), 0:1, :] = vec[0:1, at_gain : at_gain + depth][None]
    gbs[pl.ds(row, 1), 1:2, :] = vec[0:1, at_gain + depth : at_gain + 2 * depth][None]

    def gain_copy(d):
        return remote(gbs.at[row], gbs.at[row], gs.at[d], gr.at[d], (dp, lax.rem(row + d, 4), col))

    for d in (1, 2, 3):
        gain_copy(d).start()
    X.local().wait()

    bias = jnp.concatenate(
        [vec[0:1, span((4 * j + row) * hc, hc)] for j in range(3)] + [vec[0:1, span(12 * hc + row * fc, fc)]], 1
    )
    weights = w1.reshape(w1.shape[0] * w1.shape[1], w1.shape[2])

    def project(t):
        def token_step(i, _):
            at = span(t * BT + i * TC, TC)
            blocks = [xf[b, at, :].astype(F32) for b in range(4)]
            one = (blocks[0] + blocks[1]) + (blocks[2] + blocks[3])
            two = (blocks[0] * blocks[0] + blocks[1] * blocks[1]) + (
                blocks[2] * blocks[2] + blocks[3] * blocks[3]
            )
            mean = jnp.sum(one, 1, keepdims=True) * (1.0 / D)
            var = jnp.sum(two, 1, keepdims=True) * (1.0 / D) - mean * mean
            inv = lax.rsqrt(var + EPSILON)
            lane = lax.broadcasted_iota(jnp.int32, (TC, 128), 1)
            stat[at, :] = jnp.where(lane == 0, mean, inv)
            parts = []
            for b in range(4):
                n = ((blocks[b] - mean) * inv * gbs[b, 0:1, :] + gbs[b, 1:2, :]).astype(BF)
                nrm[b, at, :] = n
                parts.append(n)
            acc = dot(jnp.concatenate(parts, 1), weights[...]) + bias
            cosv, sinv = cs[0:8, at], cs[8:16, at]
            q_v[at, :] = unrope(acc[:, 0:128].T, cosv, -sinv).T.astype(BF)
            k_v[at, :] = unrope(acc[:, 128:256].T, cosv, -sinv).T.astype(BF)
            v_v[at, :] = acc[:, 256:384].astype(BF)
            tr_v[:, at] = acc[:, 256:384].T.astype(BF)
            up = acc[:, 384:]
            phi = 0.5 * (1.0 + lax.erf(up * (1.0 / math.sqrt(2.0))))
            act_v[at, :] = (up * phi).astype(BF)
            gp_v[at, :] = (phi + up * jnp.exp(-0.5 * up * up) * (1.0 / math.sqrt(2.0 * math.pi))).astype(BF)
            return 0

        lax.fori_loop(0, BT // TC, token_step, 0)

    def allowed(k0, at):
        kidx = lax.broadcasted_iota(jnp.int32, (BK, BT), 0) + k0 - rng[0:1, at]
        return (kidx >= 0) & (kidx <= rng[1:2, at])

    def attend(t):
        at = pl.ds(t * BT, BT)
        qs = q_v[at, :] * BF(scale)
        heads = [jnp.where(lane_mask(h, BT), qs, BF(0)) for h in range(2)]

        def k_step(kb, carry):
            k0 = pl.multiple_of(kb * BK, BK)
            kk = k_v[pl.ds(k0, BK), :]
            ok = allowed(k0, at)
            new = []
            for h in range(2):
                m, l, acc = carry[h]
                s = jnp.where(ok, dot(kk, heads[h], NT), MASKED)
                m2 = jnp.maximum(m, jnp.max(s, 0, keepdims=True))
                p = jnp.exp(s - m2)
                c = jnp.exp(m - m2)
                l = l * c + jnp.sum(p, 0, keepdims=True)
                vt = tr_v[h * HD : (h + 1) * HD, pl.ds(k0, BK)]
                acc = acc * c + dot(vt, p.astype(BF))
                new.append((m2, l, acc))
            return tuple(new)

        init = tuple(
            (jnp.full((1, BT), -1e30, F32), jnp.zeros((1, BT), F32), jnp.zeros((HD, BT), F32))
            for _ in range(2)
        )
        res = lax.fori_loop(0, (t + 1) * (BT // BK), k_step, init)
        for h in range(2):
            m, l, acc = res[h]
            raw[h * HD : (h + 1) * HD, at] = acc / l
            lse[h : h + 1, at] = m + jnp.log(l)
        att_v[at, :] = raw[:, at].T.astype(BF)

    def out_part(t):
        def rows(at):
            return jnp.concatenate([att_v[at, :], act_v[at, :]], 1)

        if t >= 2:
            A.wait_stage(t - 2, stage)
        A.produce(t, stage, rows, lambda joined, b: dot(joined, w2[b]))
        A.edge(t)

    def joined_back(t):
        def chunk(i, _):
            at = span(t * BT + i * TC, TC)
            dj = dot(
                jnp.concatenate([cf[b, at, :] for b in range(4)], 1),
                jnp.concatenate([w2[b] for b in range(4)], 1),
                NT,
            )
            d_att = dj[:, 0:128].astype(BF)
            da[at, :] = d_att
            d1[at, 384:] = (dj[:, 128:] * gp_v[at, :].astype(F32)).astype(BF)
            prod = d_att.astype(F32).T * raw[:, at]
            for h in range(2):
                delta[h : h + 1, at] = jnp.sum(prod[h * HD : (h + 1) * HD], 0, keepdims=True)
            return 0

        lax.fori_loop(0, BT // TC, chunk, 0)

    def attend_back(t, lo, hi):
        at = pl.ds(t * BT, BT)
        qs = q_v[at, :] * BF(scale)
        do = da[at, :]
        qh = [jnp.where(lane_mask(h, BT), qs, BF(0)) for h in range(2)]
        doh = [jnp.where(lane_mask(h, BT), do, BF(0)) for h in range(2)]
        if lo == 0:
            dqt[...] = jnp.zeros_like(dqt)

        def k_step(kb, _):
            k0 = pl.multiple_of(kb * BK, BK)
            ka = pl.ds(k0, BK)
            kk = k_v[ka, :]
            vv = v_v[ka, :]
            ok = allowed(k0, at)
            dk, dv = dka[ka, :], dva[ka, :]
            for h in range(2):
                s = jnp.where(ok, dot(kk, qh[h], NT), MASKED)
                p = jnp.exp(s - lse[h : h + 1, at])
                ds = (p * (dot(vv, doh[h], NT) - delta[h : h + 1, at])).astype(BF)
                dv = dv + dot(p.astype(BF), doh[h])
                dk = dk + dot(ds, qh[h])
                rows = slice(h * HD, (h + 1) * HD)
                dqt[rows, :] += dot(tr_v[rows, ka], ds)
            dka[ka, :] = dk
            dva[ka, :] = dv
            return 0

        lax.fori_loop(lo * 256 // BK, hi * 256 // BK, k_step, 0)

    def finish_back(t):
        at = pl.ds(t * BT, BT)
        cosv, sinv = cs[0:8, at], cs[8:16, at]
        d1[at, 0:128] = unrope(dqt[...] * scale, cosv, sinv).T.astype(BF)
        d1[at, 128:256] = unrope(dka[at, :].T, cosv, sinv).T.astype(BF)
        d1[at, 256:384] = dva[at, :].astype(BF)

    def norm_part(t):
        (A if t >= 2 else B).wait_stage(t if t >= 2 else t + 2, stage)
        B.produce(t, stage, lambda at: d1[at, :], lambda rows, b: dot(rows, w1[b], NT))
        B.edge(t)

    def gains():
        for d in (1, 2, 3):
            landed(gbs.at[0], gr.at[d])

    def prep():
        labels = seg[...]
        start = jnp.zeros_like(labels)
        for d in range(1, 8):
            below = jnp.sum((labels == d - 1).astype(F32), 1, keepdims=True).astype(jnp.int32)
            start = start + jnp.where(labels >= d, below, 0)
        index = lax.broadcasted_iota(jnp.int32, labels.shape, 1)
        place = index - start
        rng[0:1, :] = start
        rng[1:2, :] = place
        power = lax.broadcasted_iota(jnp.int32, (8, 1), 0).astype(F32) * (-2.0 * math.log(10000.0) / ROT)
        ang = place.astype(F32) * jnp.exp(power)
        cs[0:8, :] = jnp.cos(ang)
        cs[8:16, :] = jnp.sin(ang)
        dka[...] = jnp.zeros_like(dka)
        dva[...] = jnp.zeros_like(dva)

    def turn():
        def step(i, _):
            at = span(i * BT, BT)
            tr_v[:, at] = k_v[at, :].astype(F32).T.astype(BF)
            return 0

        lax.fori_loop(0, toks // BT, step, 0)

    def grads2():
        for b in range(4):
            go[b] = dot(att_v[...], cf[b], TN).astype(BF)
            gd[b] = dot(act_v[...], cf[b], TN).astype(BF)

    def gradsu():
        for b in range(4):
            gu[b] = dot(nrm[b], d1[:, 384:], TN).astype(BF)

    def gradsq():
        for b in range(4):
            gq[b] = dot(nrm[b], d1[:, 0:384], TN).astype(BF)

    def sum_copy(e):
        return remote(sums.at[0], sums_in.at[e - 1], s_sum.at[e], r_sum.at[e], (dp ^ e, row, col))

    def row_copy(d):
        return remote(sums.at[1], cols_o.at[row], s_row.at[d], r_row.at[d], (dp, lax.rem(row + d, 4), col))

    own_cols = pltpu.make_async_copy(sums.at[1], cols_o.at[row], misc.at[0])

    def colsum():
        sums[0] = dot(jnp.ones((8, toks), BF), d1[...])
        for e in (3, 1, 2):
            sum_copy(e).start()

    def sums_on():
        for e in (1, 2, 3):
            landed(sums_in.at[e - 1], r_sum.at[e])
        sums[1] = (sums[0] + sums_in[0]) + (sums_in[1] + sums_in[2])
        for d in (1, 2, 3):
            row_copy(d).start()
        own_cols.start()

    at_obias = at_gain + 2 * depth

    def deliver(src, dst, i, t):
        at = span((t % 2) * BT + col * HT, HT)
        here = pltpu.make_async_copy(src.at[t], dst.at[at], s_own.at[i, t])
        there = remote(src.at[t], dst.at[at], s_own.at[i, t], r_own.at[i, t], (dp, row, 1 - col))
        return here, there

    def send_result(src, dst, i, t):
        here, there = deliver(src, dst, i, t)

        @pl.when(col == t // 2)
        def _():
            here.start()

        @pl.when(col != t // 2)
        def _():
            there.start()

    def end_result(src, dst, i, t):
        here, there = deliver(src, dst, i, t)

        @pl.when(col == t // 2)
        def _():
            here.wait()
            landed(dst.at[span((t % 2) * BT + (1 - col) * HT, HT)], r_own.at[i, t])

        @pl.when(col != t // 2)
        def _():
            there.wait_send()

    def mine(t):
        return span(t * BT + col * HT, HT)

    def out_final(t):
        A.final(t, total)
        out_v[t] = (
            xf[row, mine(t), :].astype(F32) + total[...] + vec[0:1, at_obias : at_obias + depth]
        ).astype(BF)
        send_result(out_v, out_o, 0, t)

    def stat_copy(d, k):
        return remote(
            send_st.at[k], st.at[d - 1, k], s_st.at[d, k], r_st.at[d, k], (dp, lax.rem(row + d, 4), col)
        )

    gain = vec[0:1, at_gain : at_gain + depth]
    small[...] = jnp.zeros_like(small)

    def centred(t):
        mean, inv = stat[mine(t), 0:1], stat[mine(t), 1:2]
        return (xf[row, mine(t), :].astype(F32) - mean) * inv, inv, cf[row, mine(t), :].astype(F32)

    def norm_final(t):
        B.final(t, total)
        dn = total[...]
        xh, inv, ct = centred(t)
        dc = dn * gain
        s0 = jnp.sum(dc, 1, keepdims=True)
        s1 = jnp.sum(dc * xh, 1, keepdims=True)
        lane = lax.broadcasted_iota(jnp.int32, (HT, 128), 1)
        send_st[t // 2, :, (t % 2) * HT : (t % 2 + 1) * HT] = jnp.where(
            lane == 0, s0, jnp.where(lane == 1, s1, 0.0)
        ).T[0:8, :]
        if t % 2 == 0:
            for d in (2, 1, 3):
                stat_copy(d, t // 2).start()
        gin_v[t] = dc
        small[0, 0:1, :] += jnp.sum(dn * xh, 0, keepdims=True)
        small[0, 1:2, :] += jnp.sum(dn, 0, keepdims=True)
        small[0, 2:3, :] += jnp.sum(ct, 0, keepdims=True)
        if t == 0:
            sib_small.start()

    sib_small = remote(small.at[0], small_sib, s_small.at[0], r_small.at[0], (dp, row, 1 - col))

    def small_copy(e):
        return remote(small.at[1], small_in.at[e - 1], s_small.at[e], r_small.at[e], (dp ^ e, row, col))

    def small_on():
        landed(small_sib, r_small.at[0])
        small[1] = small[0] + small_sib[...]
        for e in (3, 1, 2):
            small_copy(e).start()

    def grad_final(k):
        acc = send_st[k]
        for d in (1, 2, 3):
            landed(st.at[d - 1, k], r_st.at[d, k])
            acc = acc + st[d - 1, k]
        both = jnp.concatenate([acc, jnp.zeros((120, BT), F32)], 0).T
        for t in (2 * k + 1, 2 * k):
            xh, inv, ct = centred(t)
            r = slice((t % 2) * HT, (t % 2 + 1) * HT)
            gin_v[t] = inv * (gin_v[t] - both[r, 0:1] * (1.0 / D) - xh * (both[r, 1:2] * (1.0 / D))) + ct
            send_result(gin_v, gin_o, 1, t)
    X.send_own(0)
    W2.start()
    gains()
    X.step(1,0)
    X.send_own(1)
    W1.start()
    W2.forward()
    X.step(1,1)
    X.step(2,0)
    C.start((1, 0))
    X.send_own(2)
    W1.forward()
    X.step(3,0)
    X.step(2,1)
    X.step(1,2)
    C.local().wait()
    prep()
    X.step(3,1)
    X.ready(0)
    X.send_own(3)
    X.step(2,2)
    W1.arrived()
    C.send_own(3)
    project(0)
    C.send_own(2)
    X.ready(1)
    W2.arrived()
    C.send_own(1)
    attend(0)
    C.send_own(0)
    project(1)
    attend(1)
    C.step(1,3)
    out_part(0)
    X.step(1,3)
    X.step(3,2)
    out_part(1)
    X.ready(2)
    project(2)
    attend(2)
    X.step(2,3)
    out_part(2)
    C.step(2,3)
    C.step(1,1)
    A.slot(0, 0)
    X.step(3,3)
    X.ready(3)
    C.step(1,2)
    project(3)
    attend(3)
    C.step(3,3)
    C.step(2,1)
    C.step(2,2)
    out_part(3)
    C.step(3,1)
    C.step(3,2)
    C.step(1,0)
    C.ready(3)
    turn()
    joined_back(3)
    A.slot(0, 1)
    attend_back(3, 0, 2)
    attend_back(3, 2, 4)
    attend_back(3, 4, 6)
    A.slot(1, 0)
    C.step(2,0)
    C.step(3,0)
    attend_back(3, 6, 8)
    C.ready(0)
    finish_back(3)
    C.ready(2)
    A.slot(1, 1)
    C.ready(1)
    grads2()
    GD.start()
    A.slot(2, 0)
    joined_back(2)
    GO.start()
    norm_part(3)
    attend_back(2, 0, 2)
    GD.middle_sum()
    joined_back(0)
    A.slot(2, 1)
    A.slot(3, 0)
    joined_back(1)
    gradsu()
    attend_back(2, 2, 4)
    A.slot(3, 1)
    GD.sum_and_spread()
    attend_back(2, 4, 6)
    finish_back(2)
    norm_part(2)
    GO.middle_sum()
    GU.start()
    B.slot(3, 0)
    attend_back(1, 0, 2)
    attend_back(1, 2, 4)
    finish_back(1)
    GO.sum_and_spread()
    B.slot(3, 1)
    GU.middle_sum()
    norm_part(1)
    B.slot(2, 0)
    GD.share()
    attend_back(0, 0, 2)
    finish_back(0)
    B.slot(2, 1)
    gradsq()
    GQ.start()
    GU.sum_and_spread()
    B.slot(1, 0)
    GD.relay()
    norm_part(0)
    GQ.middle_sum()
    B.slot(1, 1)
    GO.share()
    out_final(3)
    GU.share()
    out_final(0)
    out_final(2)
    B.slot(0, 0)
    out_final(1)
    GQ.sum_and_spread()
    GU.relay()
    norm_final(3)
    GO.relay()
    colsum()
    B.slot(0, 1)
    norm_final(2)
    norm_final(1)
    GQ.share()
    norm_final(0)
    small_on()
    GD.finish()
    GO.finish()
    GQ.relay()
    sums_on()
    GU.finish()
    grad_final(1)
    grad_final(0)
    GQ.finish()

    for e in (1, 2, 3):
        landed(small_in.at[e - 1], r_small.at[e])
    small_o[...] = (small[1] + small_in[0]) + (small_in[1] + small_in[2])

    X.drain()
    C.drain()
    W1.drain()
    W2.drain()
    for d in (1, 2, 3):
        gain_copy(d).wait_send()
        for k in range(2):
            stat_copy(d, k).wait_send()
        row_copy(d).wait_send()
        sum_copy(d).wait_send()
        small_copy(d).wait_send()
        landed(sums.at[1], r_row.at[d])
    sib_small.wait_send()
    A.drain()
    B.wait_stage(1, stage)
    B.wait_stage(0, stage)
    B.drain()
    own_cols.wait()
    for t in range(4):
        end_result(out_v, out_o, 0, t)
        end_result(gin_v, gin_o, 1, t)


def layer(x, cot, wq, wu, wo, wd, seg, vec):
    toks = seg.shape[1]
    half = toks // 2
    depth = wq.shape[1]
    hc, fc = wq.shape[2] // 4, wu.shape[1] // 4
    h3 = 3 * hc
    sd = jax.ShapeDtypeStruct
    V = pltpu.VMEM
    grads = []
    for r, c in ((depth, h3), (depth, fc), (hc, depth), (fc, depth)):
        grads += [
            V((4, r, c), BF), V((4, 4, r // 8, c), BF), V((2, 4, r // 8, c), BF), V((2, 4, r // 8, c), BF),
            V((4, r // 4, c), BF),
        ]
    sems = (
        LineGather.SEMS * 2 + WeightGather.SEMS * 2 + LineReduce.SEMS * 2 + GradReduce.SEMS * 4
        + ((4,), (4,), (8,), (4, 2), (4, 2), (4,), (4,), (4,), (4,), (4,), (4,), (2, 4), (2, 4))
    )
    return pl.pallas_call(
        layer_kernel,
        name="layer",
        out_shape=(
            sd((half, depth), BF), sd((half, depth), F32), sd((8, depth), F32), sd((4, 8, h3 + fc), F32),
            sd((3, depth, 4 * hc), BF), sd((depth, 4 * fc), BF), sd((4, hc, depth), BF), sd((4, fc, depth), BF),
        ),
        in_specs=[hbm()] * 6 + [vmem()] * 2,
        out_specs=(hbm(), hbm(), vmem(), hbm(), hbm(), hbm(), hbm(), hbm()),
        scratch_shapes=[
            V((4, toks, depth), BF), V((4, toks, depth), BF), V((4, toks, depth), BF),
            V((4, depth, h3 + fc), BF), V((4, hc + fc, depth), BF),
            V((toks, hc), BF), V((toks, hc), BF), V((toks, hc), BF), V((hc, toks), BF),
            V((toks, hc), BF), V((toks, hc), BF), V((toks, fc), BF), V((toks, fc), BF),
            V((hc, toks), F32), V((hc, BT), F32), V((toks, hc), F32), V((toks, hc), F32),
            V((toks, 128), F32), V((8, toks), F32), V((8, toks), F32), V((16, toks), F32),
            V((8, toks), jnp.int32), V((4, 8, depth), F32), V((toks, h3 + fc), BF),
            V((4, 4, HT, depth), BF), V((4, 4, HT, depth), BF), V((5, 4, HT, depth), BF),
            V((4, 4, HT, depth), BF), V((4, 4, HT, depth), BF), V((5, 4, HT, depth), BF),
            V((2, 4, HT, depth), BF), V((HT, depth), F32),
            *grads,
            V((4, HT, depth), BF), V((4, HT, depth), F32),
            V((2, 8, BT), F32), V((3, 2, 8, BT), F32), V((2, 8, h3 + fc), F32), V((3, 8, h3 + fc), F32),
            V((2, 8, depth), F32), V((8, depth), F32), V((3, 8, depth), F32),
            *dmas(*sems),
        ],
        compiler_params=pltpu.CompilerParams(
            collective_id=0, has_side_effects=True, vmem_limit_bytes=62 * 2**20
        ),
    )(x, cot, wq, wu, wo, wd, seg, vec)


def per_device_sliced(
    inputs, segments, ln_gain, ln_bias, w_qkv, b_qkv, w_out, w_up, b_up, w_down, out_bias, cotangent
):
    nrow = lax.axis_size("row")
    dpart = inputs.shape[1]
    hcols = w_qkv.shape[2] // nrow
    h3 = 3 * hcols
    vec = jnp.concatenate([b_qkv.reshape(-1), b_up, ln_gain, ln_bias, out_bias]).astype(F32)[None]
    layer_out, grad_inputs, small, cols, fq, fu, fo, fd = layer(
        inputs, cotangent, w_qkv.transpose(1, 0, 2), w_up, w_out, w_down, segments, vec
    )
    cols = cols[:, 0]
    grad_b_qkv = cols[:, :h3].reshape(nrow, 3, hcols).transpose(1, 0, 2).reshape(3, -1)
    return (
        layer_out, grad_inputs, small[0], small[1],
        fq.astype(F32).transpose(1, 0, 2), grad_b_qkv,
        fo.reshape(w_out.shape).astype(F32), fu.astype(F32), cols[:, h3:].reshape(-1),
        fd.reshape(w_down.shape).astype(F32), small[2],
    )


FLOOR_INIT = -1e30


def doc_positions(labels):
    token_index = jnp.arange(labels.shape[1], dtype=jnp.int32)
    flags = jnp.concatenate(
        [jnp.ones((labels.shape[0], 1), dtype=jnp.bool_), labels[:, 1:] != labels[:, :-1]], 1
    )
    starts = lax.cummax(jnp.where(flags, token_index[None, :], 0), axis=1)
    return token_index[None, :] - starts


def rotate(tensor_in, positions):
    half_rot = ROT // 2
    inverse = 10000.0 ** (-(jnp.arange(half_rot, dtype=jnp.float32) * 2.0 / ROT))
    angles = positions.astype(jnp.float32)[:, None] * inverse[None, :]
    cosines = jnp.cos(angles)[:, None, :]
    sine_vals = jnp.sin(angles)[:, None, :]
    first_half = tensor_in[..., :half_rot]
    second_half = tensor_in[..., half_rot:ROT]
    rest_dims = tensor_in[..., ROT:]
    return jnp.concatenate(
        [
            first_half * cosines - second_half * sine_vals,
            second_half * cosines + first_half * sine_vals,
            rest_dims,
        ],
        -1,
    )


def slice_rows(array_in, first_row, row_count, axis_num=0):
    return lax.dynamic_slice_in_dim(array_in, first_row, row_count, axis_num)


def put_rows(array_in, update, first_row, axis_num=0):
    return lax.dynamic_update_slice_in_dim(array_in, update, first_row, axis_num)


def block_pairs(query_blocks, key_blocks):
    q_list = jnp.repeat(jnp.arange(query_blocks, dtype=jnp.int32), key_blocks)
    k_list = jnp.tile(jnp.arange(key_blocks, dtype=jnp.int32), query_blocks)
    return (q_list, k_list)


def per_device_general(
    inputs, segments, ln_gain, ln_bias, w_qkv, b_qkv, w_out, w_up, b_up, w_down, out_bias, cotangent
):
    local_rows, feature_cols = inputs.shape
    part_count = lax.axis_size("row")
    row_index = lax.axis_index("row")
    head_cols = w_qkv.shape[2]
    head_count = head_cols // HD
    group_seqs = segments.shape[0]
    all_rows = group_seqs * SEQ_LEN
    span = all_rows // part_count
    query_blocks = span // span
    score_scale = 1.0 / math.sqrt(HD)
    labels = (segments + (jnp.arange(group_seqs, dtype=jnp.int32) * SEQ_LEN)[:, None]).reshape(-1)
    positions = doc_positions(segments).reshape(-1)
    token_index = jnp.arange(all_rows, dtype=jnp.int32)
    my_labels = slice_rows(labels, row_index * span, span)
    my_index = slice_rows(token_index, row_index * span, span)
    my_positions = slice_rows(positions, row_index * span, span)
    float_in = inputs.astype(jnp.float32)
    ln_sums = lax.psum((jnp.sum(float_in, 1), jnp.sum(float_in * float_in, 1)), "row")
    row_mean = ln_sums[0] / D
    row_var = ln_sums[1] / D - row_mean * row_mean
    inv_std = lax.rsqrt(row_var + EPSILON)
    centred = (float_in - row_mean[:, None]) * inv_std[:, None]
    normed = (centred * ln_gain.astype(jnp.float32) + ln_bias.astype(jnp.float32)).astype(
        jnp.bfloat16
    )
    gathered_hidden = lax.all_gather(normed, "col", axis=0, tiled=True)
    first_weights = jnp.concatenate([w_qkv.reshape(feature_cols, 3 * head_cols), w_up], 1)
    first_bias = jnp.concatenate(
        [b_qkv.reshape(3 * head_cols).astype(jnp.float32), b_up.astype(jnp.float32)]
    )
    first_out = (
        lax.psum_scatter(
            jnp.dot(
                slice_rows(gathered_hidden, jnp.int32(0), lax.axis_size("row") * span),
                first_weights,
                preferred_element_type=jnp.float32,
            ).astype(jnp.bfloat16),
            "row",
            scatter_dimension=0,
            tiled=True,
        ).astype(jnp.float32)
        + first_bias
    )

    def rotate_mine(tensor_in):
        return rotate(tensor_in, my_positions)

    query_lin = first_out[:, :head_cols].reshape(span, head_count, HD)
    key_lin = first_out[:, head_cols : 2 * head_cols].reshape(span, head_count, HD)
    query = rotate_mine(query_lin).astype(jnp.bfloat16)
    key_rows = rotate_mine(key_lin).astype(jnp.bfloat16)
    value_rows = (
        first_out[:, 2 * head_cols : 3 * head_cols]
        .reshape(span, head_count, HD)
        .astype(jnp.bfloat16)
    )
    up_lin = first_out[:, 3 * head_cols :]
    activated = jax.nn.gelu(up_lin, approximate=False).astype(jnp.bfloat16)

    def over_keys(fold_step, initial):
        return fold_step(
            initial,
            (
                lax.all_gather(key_rows, "row", axis=0, tiled=True),
                lax.all_gather(value_rows, "row", axis=0, tiled=True),
            ),
            jnp.int32(0),
        )

    def key_setup(pieces, first_row):
        row_count = pieces[0].shape[0]
        piece_labels = slice_rows(labels, first_row, row_count)
        piece_index = slice_rows(token_index, first_row, row_count)
        return (row_count, span, piece_labels, piece_index)

    def block_live(piece_labels, piece_index, key_size, q_block, k_block):
        q_labels = slice_rows(my_labels, q_block * span, span)
        q_index = slice_rows(my_index, q_block * span, span)
        k_labels = slice_rows(piece_labels, k_block * key_size, key_size)
        k_index = slice_rows(piece_index, k_block * key_size, key_size)
        return (
            (jnp.max(q_index) >= jnp.min(k_index))
            & (jnp.min(q_labels) <= jnp.max(k_labels))
            & (jnp.min(k_labels) <= jnp.max(q_labels))
        )

    def block_scores(pieces, piece_labels, piece_index, key_size, q_block, k_block):
        q_start = q_block * span
        k_start = k_block * key_size
        q_labels = slice_rows(my_labels, q_start, span)
        q_index = slice_rows(my_index, q_start, span)
        k_labels = slice_rows(piece_labels, k_start, key_size)
        k_index = slice_rows(piece_index, k_start, key_size)
        q_block_rows = slice_rows(query, q_start, span)
        k_block_rows = slice_rows(pieces[0], k_start, key_size)
        v_block_rows = slice_rows(pieces[1], k_start, key_size)
        scores = (
            jnp.einsum(
                "qhd,khd->hqk", q_block_rows, k_block_rows, preferred_element_type=jnp.float32
            )
            * score_scale
        )
        allowed = (q_labels[:, None] == k_labels[None, :]) & (k_index[None, :] <= q_index[:, None])
        scores = jnp.where(allowed[None], scores, MASKED)
        return (q_start, k_start, scores, q_block_rows, k_block_rows, v_block_rows)

    def forward_piece(running, pieces, first_row):
        row_count, key_size, piece_labels, piece_index = key_setup(pieces, first_row)
        q_list, k_list = block_pairs(query_blocks, row_count // key_size)

        def forward_pair_step(current, pair_ids):
            q_block, k_block = pair_ids

            def update(inner_state):
                row_max, row_sum, row_acc = inner_state
                q_start, k_start, scores, q_block_rows, k_block_rows, v_block_rows = block_scores(
                    pieces, piece_labels, piece_index, key_size, q_block, k_block
                )
                old_max = slice_rows(row_max, q_start, span, 1)
                new_max = jnp.maximum(old_max, jnp.max(scores, -1))
                weights = jnp.exp(scores - new_max[..., None])
                keep_part = jnp.exp(old_max - new_max)
                new_sum = slice_rows(row_sum, q_start, span, 1) * keep_part + jnp.sum(weights, -1)
                added = jnp.einsum(
                    "hqk,khd->hqd",
                    weights.astype(jnp.bfloat16),
                    v_block_rows,
                    preferred_element_type=jnp.float32,
                )
                new_acc = slice_rows(row_acc, q_start, span, 1) * keep_part[..., None] + added
                return (
                    put_rows(row_max, new_max, q_start, 1),
                    put_rows(row_sum, new_sum, q_start, 1),
                    put_rows(row_acc, new_acc, q_start, 1),
                )

            def forward_unchanged(inner_state):
                return inner_state

            is_live = block_live(piece_labels, piece_index, key_size, q_block, k_block)
            return (lax.cond(is_live, update, forward_unchanged, current), None)

        result, _ = lax.scan(forward_pair_step, running, (q_list, k_list))
        return result

    forward_init = (
        jnp.full((head_count, span), FLOOR_INIT, jnp.float32),
        jnp.zeros((head_count, span), jnp.float32),
        jnp.zeros((head_count, span, HD), jnp.float32),
    )
    row_max, row_sum, row_acc = over_keys(forward_piece, forward_init)
    log_total = row_max + jnp.log(row_sum)
    attention_raw = jnp.transpose(row_acc / row_sum[..., None], (1, 0, 2)).reshape(span, head_cols)
    attended = attention_raw.astype(jnp.bfloat16)
    joined = jnp.concatenate(
        (
            lax.all_gather(attended, "row", axis=0, tiled=True),
            lax.all_gather(activated, "row", axis=0, tiled=True),
        ),
        1,
    )
    second_weights = jnp.concatenate([w_out, w_down], 0)
    partial_out = lax.psum_scatter(
        jnp.dot(
            slice_rows(joined, jnp.int32(0), lax.axis_size("col") * local_rows),
            second_weights,
            preferred_element_type=jnp.float32,
        ).astype(jnp.bfloat16),
        "col",
        scatter_dimension=0,
        tiled=True,
    ).astype(jnp.float32)
    layer_out = (float_in + partial_out + out_bias.astype(jnp.float32)).astype(jnp.bfloat16)
    grad_full = lax.all_gather(cotangent, "col", axis=0, tiled=True)
    grad_out_bias = jnp.sum(grad_full, 0, dtype=jnp.float32)
    grad_second = lax.dot_general(
        joined, grad_full, (((0,), (0,)), ((), ())), preferred_element_type=jnp.float32
    )
    branch_back = lax.psum_scatter(
        lax.dot_general(
            slice_rows(grad_full, jnp.int32(0), lax.axis_size("row") * span),
            second_weights,
            (((1,), (1,)), ((), ())),
            preferred_element_type=jnp.float32,
        ).astype(jnp.bfloat16),
        "row",
        scatter_dimension=0,
        tiled=True,
    ).astype(jnp.float32)
    d_attended = branch_back[:, :head_cols].astype(jnp.bfloat16)
    d_activated = branch_back[:, head_cols:]
    _, gelu_back = jax.vjp(lambda tensor_in: jax.nn.gelu(tensor_in, approximate=False), up_lin)
    d_up = gelu_back(d_activated)[0].astype(jnp.bfloat16)
    d_out_heads = d_attended.reshape(span, head_count, HD)
    row_delta = jnp.transpose(
        jnp.sum((d_attended.astype(jnp.float32) * attention_raw).reshape(span, head_count, HD), -1)
    )

    def backward_piece(running, pieces, first_row):
        d_query_acc, d_key_all, d_value_all = running
        row_count, key_size, piece_labels, piece_index = key_setup(pieces, first_row)
        q_list, k_list = block_pairs(query_blocks, row_count // key_size)
        zero_keys = jnp.zeros((row_count, head_count, HD), jnp.float32)

        def backward_pair_step(current, pair_ids):
            q_block, k_block = pair_ids

            def update(inner_state):
                d_query_run, d_key_run, d_value_run = inner_state
                q_start, k_start, scores, q_block_rows, k_block_rows, v_block_rows = block_scores(
                    pieces, piece_labels, piece_index, key_size, q_block, k_block
                )
                probs_full = jnp.exp(scores - slice_rows(log_total, q_start, span, 1)[..., None])
                d_out_block = slice_rows(d_out_heads, q_start, span)
                d_probs = jnp.einsum(
                    "qhd,khd->hqk", d_out_block, v_block_rows, preferred_element_type=jnp.float32
                )
                d_scores = (
                    probs_full * (d_probs - slice_rows(row_delta, q_start, span, 1)[..., None])
                ).astype(jnp.bfloat16)
                q_added = (
                    jnp.einsum(
                        "hqk,khd->qhd", d_scores, k_block_rows, preferred_element_type=jnp.float32
                    )
                    * score_scale
                )
                k_added = (
                    jnp.einsum(
                        "hqk,qhd->khd", d_scores, q_block_rows, preferred_element_type=jnp.float32
                    )
                    * score_scale
                )
                v_added = jnp.einsum(
                    "hqk,qhd->khd",
                    probs_full.astype(jnp.bfloat16),
                    d_out_block,
                    preferred_element_type=jnp.float32,
                )
                return (
                    put_rows(
                        d_query_run, slice_rows(d_query_run, q_start, span) + q_added, q_start
                    ),
                    put_rows(
                        d_key_run, slice_rows(d_key_run, k_start, key_size) + k_added, k_start
                    ),
                    put_rows(
                        d_value_run, slice_rows(d_value_run, k_start, key_size) + v_added, k_start
                    ),
                )

            def backward_unchanged(inner_state):
                return inner_state

            is_live = block_live(piece_labels, piece_index, key_size, q_block, k_block)
            return (lax.cond(is_live, update, backward_unchanged, current), None)

        scanned, _ = lax.scan(
            backward_pair_step, (d_query_acc, zero_keys, zero_keys), (q_list, k_list)
        )
        d_query_acc, key_part, value_part = scanned
        d_key_all = put_rows(d_key_all, key_part, first_row)
        d_value_all = put_rows(d_value_all, value_part, first_row)
        return (d_query_acc, d_key_all, d_value_all)

    backward_init = (
        jnp.zeros((span, head_count, HD), jnp.float32),
        jnp.zeros((all_rows, head_count, HD), jnp.float32),
        jnp.zeros((all_rows, head_count, HD), jnp.float32),
    )
    d_query_rot, d_key_total, d_value_total = over_keys(backward_piece, backward_init)
    d_key_rot, d_value_mine = (
        lax.psum_scatter(
            d_key_total.reshape(all_rows, head_cols).astype(jnp.bfloat16),
            "row",
            scatter_dimension=0,
            tiled=True,
        ).astype(jnp.float32),
        lax.psum_scatter(
            d_value_total.reshape(all_rows, head_cols).astype(jnp.bfloat16),
            "row",
            scatter_dimension=0,
            tiled=True,
        ).astype(jnp.float32),
    )
    _, query_back = jax.vjp(rotate_mine, query_lin)
    _, key_back = jax.vjp(rotate_mine, key_lin)
    d_query_lin = query_back(d_query_rot)[0].reshape(span, head_cols).astype(jnp.bfloat16)
    d_key_lin = (
        key_back(d_key_rot.reshape(span, head_count, HD))[0]
        .reshape(span, head_cols)
        .astype(jnp.bfloat16)
    )
    d_first = jnp.concatenate([d_query_lin, d_key_lin, d_value_mine.astype(jnp.bfloat16), d_up], 1)
    d_first_full = lax.all_gather(d_first, "row", axis=0, tiled=True)
    grad_first_bias = jnp.sum(d_first_full, 0, dtype=jnp.float32)
    grad_first = lax.dot_general(
        gathered_hidden, d_first_full, (((0,), (0,)), ((), ())), preferred_element_type=jnp.float32
    )
    d_normed = lax.psum_scatter(
        lax.dot_general(
            slice_rows(d_first_full, jnp.int32(0), lax.axis_size("col") * local_rows),
            first_weights,
            (((1,), (1,)), ((), ())),
            preferred_element_type=jnp.float32,
        ).astype(jnp.bfloat16),
        "col",
        scatter_dimension=0,
        tiled=True,
    ).astype(jnp.float32)
    d_centred = d_normed * ln_gain.astype(jnp.float32)
    grad_stats = lax.psum((jnp.sum(d_centred, 1), jnp.sum(d_centred * centred, 1)), "row")
    grad_inputs = inv_std[:, None] * (
        d_centred - grad_stats[0][:, None] / D - centred * grad_stats[1][:, None] / D
    ) + cotangent.astype(jnp.float32)
    summed = (
        lax.psum(grad_first.astype(jnp.bfloat16), "dp").astype(jnp.float32),
        lax.psum(grad_second.astype(jnp.bfloat16), "dp").astype(jnp.float32),
        lax.psum(grad_first_bias.astype(jnp.bfloat16), "dp").astype(jnp.float32),
        lax.psum(grad_out_bias.astype(jnp.bfloat16), "dp").astype(jnp.float32),
    )
    norm_grads = lax.psum((jnp.sum(d_normed * centred, 0), jnp.sum(d_normed, 0)), ("dp", "col"))
    grad_w_qkv = summed[0][:, : 3 * head_cols].reshape(feature_cols, 3, head_cols)
    grad_w_up = summed[0][:, 3 * head_cols :]
    grad_w_out = summed[1][:head_cols]
    grad_w_down = summed[1][head_cols:]
    grad_b_qkv = summed[2][: 3 * head_cols].reshape(3, head_cols)
    grad_b_up = summed[2][3 * head_cols :]
    return (
        layer_out,
        grad_inputs,
        norm_grads[0],
        norm_grads[1],
        grad_w_qkv,
        grad_b_qkv,
        grad_w_out,
        grad_w_up,
        grad_b_up,
        grad_w_down,
        summed[3],
    )


def solution(mesh):
    placed = (
        P(("dp", "col"), "row"),
        P("dp", None),
        P("row"),
        P("row"),
        P("row", None, "col"),
        P(None, "col"),
        P("col", "row"),
        P("row", "col"),
        P("col"),
        P("col", "row"),
        P("row"),
        P(("dp", "col"), "row"),
    )
    size = dict(mesh.shape)
    sliced = (size["dp"], size["row"], size["col"]) == (4, 4, 2)
    return jax.shard_map(
        per_device_sliced if sliced else per_device_general,
        mesh=mesh,
        in_specs=placed,
        out_specs=(
            P(("dp", "col"), "row"),
            P(("dp", "col"), "row"),
            P("row"),
            P("row"),
            P("row", None, "col"),
            P(None, "col"),
            P("col", "row"),
            P("row", "col"),
            P("col"),
            P("col", "row"),
            P("row"),
        ),
        check_vma=False,
    )
```

```python
import math

import jax
import jax.numpy as jnp
from jax import lax
from jax.experimental import pallas as pl
from jax.experimental.pallas import tpu as pltpu
from jax.sharding import PartitionSpec as P

D = 1024
HD = 64
ROT = 16
SEQ_LEN = 2048
EPSILON = 1e-05
MASKED = -1000000000.0
BF = jnp.bfloat16
F32 = jnp.float32
NT = (((1,), (1,)), ((), ()))
NN = (((1,), (0,)), ((), ()))
TN = (((0,), (0,)), ((), ()))


def dot(a, b, dims=NN):
    return lax.dot_general(a, b, dims, preferred_element_type=F32)


BK = 512


def lane_mask(head, rows):
    lane = lax.broadcasted_iota(jnp.int32, (rows, 128), 1)
    return (lane >= head * HD) & (lane < (head + 1) * HD)


MESH = pl.DeviceIdType.MESH
TC = 256
BT = 512
HT = BT // 2


def vmem():
    return pl.BlockSpec(memory_space=pltpu.VMEM)


def hbm():
    return pl.BlockSpec(memory_space=pl.ANY)


def span(first, count):
    if not isinstance(first, int):
        first = pl.multiple_of(first, count & -count)
    return pl.ds(first, count)


def remote(src, dst, send, recv, dev):
    return pltpu.make_async_remote_copy(
        src_ref=src, dst_ref=dst, send_sem=send, recv_sem=recv, device_id=dev, device_id_type=MESH
    )


def landed(ref, sem):
    pltpu.make_async_copy(ref, ref, sem).wait()


def left(ref, sem):
    pltpu.make_async_copy(ref, ref, sem).wait()


def where():
    return lax.axis_index("dp"), lax.axis_index("row"), lax.axis_index("col")


def greet(dp, row, col):
    bar = pltpu.get_barrier_semaphore()
    for d in range(1, 4):
        pl.semaphore_signal(bar, inc=1, device_id=(dp ^ d, row, col), device_id_type=MESH)
        pl.semaphore_signal(bar, inc=1, device_id=(dp, lax.rem(row + d, 4), col), device_id_type=MESH)
    pl.semaphore_signal(bar, inc=1, device_id=(dp, row, 1 - col), device_id_type=MESH)
    pl.semaphore_wait(bar, 7)


def dmas(*shapes):
    return [pltpu.SemaphoreType.DMA(s) for s in shapes]


class LineGather:
    SEMS = ((4, 4),) * 4 + ((7, 4),) * 2 + ((1,),)

    def __init__(self, own, full, sems, pos):
        self.own, self.full, self.pos = own, full, pos
        self.su, self.sd, self.ru, self.rd, self.ss, self.rs, self.loc = sems

    def at(self, block, t, other=False):
        dp, row, col = self.pos
        return self.full.at[block, span(t * BT + (1 - col if other else col) * HT, HT)]

    def up(self, step, t):
        dp, row, col = self.pos
        ref = self.at(row - step, t)
        return remote(ref, ref, self.su.at[step, t], self.ru.at[step, t], (dp, row + 1, col))

    def down(self, step, t):
        dp, row, col = self.pos
        ref = self.at(row + step, t)
        return remote(ref, ref, self.sd.at[step, t], self.rd.at[step, t], (dp, row - 1, col))

    def sib(self, step, sign, t):
        dp, row, col = self.pos
        i = step + 3 * (sign < 0)
        ref = self.at(row - sign * step, t)
        return remote(ref, ref, self.ss.at[i, t], self.rs.at[i, t], (dp, row, 1 - col))

    def half_at(self, k, other=False):
        dp, row, col = self.pos
        return self.full.at[row, span((1 - col if other else col) * 2 * BT + k * BT, BT)]

    def give(self, k):
        dp, row, col = self.pos
        return remote(
            self.own.at[pl.ds(k * BT, BT)], self.half_at(k), self.ss.at[0, k], self.rs.at[0, k], (dp, row, 1 - col)
        )

    def local(self):
        dp, row, col = self.pos
        return pltpu.make_async_copy(self.own, self.full.at[row, span(col * 2 * BT, 2 * BT)], self.loc.at[0])

    def start(self, order):
        for k in order:
            self.give(k).start()
        self.local().start()

    def send_own(self, t):
        dp, row, col = self.pos

        @pl.when(col != t // 2)
        def _():
            landed(self.half_at(t % 2, True), self.rs.at[0, t % 2])

        @pl.when(row < 3)
        def _():
            self.up(0, t).start()

        @pl.when(row > 0)
        def _():
            self.down(0, t).start()

    def step(self, s, t):
        dp, row, col = self.pos

        @pl.when(row >= s)
        def _():
            landed(self.at(row - s, t), self.ru.at[s - 1, t])

            @pl.when(row < 3)
            def _():
                self.up(s, t).start()

            self.sib(s, 1, t).start()

        @pl.when(row + s <= 3)
        def _():
            landed(self.at(row + s, t), self.rd.at[s - 1, t])

            @pl.when(row > 0)
            def _():
                self.down(s, t).start()

            self.sib(s, -1, t).start()

    def ready(self, t):
        dp, row, col = self.pos
        for s in range(1, 4):
            @pl.when(row >= s)
            def _():
                landed(self.at(row - s, t, True), self.rs.at[s, t])

            @pl.when(row + s <= 3)
            def _():
                landed(self.at(row + s, t, True), self.rs.at[s + 3, t])

    def drain(self):
        dp, row, col = self.pos
        for k in range(2):
            self.give(k).wait_send()
        for t in range(4):
            for s in range(0, 3):
                @pl.when((row >= s) & (row < 3))
                def _():
                    self.up(s, t).wait_send()

                @pl.when((row + s <= 3) & (row > 0))
                def _():
                    self.down(s, t).wait_send()
            for s in range(1, 4):
                @pl.when(row >= s)
                def _():
                    self.sib(s, 1, t).wait_send()

                @pl.when(row + s <= 3)
                def _():
                    self.sib(s, -1, t).wait_send()


class WeightGather:
    SEMS = ((4,), (4,), (4, 4), (4, 4), (4,))

    def __init__(self, full, pieces, sems, pos):
        self.full, self.pieces, self.pos = full, pieces, pos
        self.sz, self.rz, self.sp, self.rp, self.loc = sems
        self.quarter = full.shape[1] // 4

    def parts(self, block, q):
        seen = []
        for src, r0, rows, c0, cols, d0, e0 in self.pieces(0):
            seen.append((d0, rows))
        out = []
        for d0, rows in dict.fromkeys(seen):
            out.append(self.full.at[block, span(d0 + q * (rows // 4), rows // 4)])
        return out

    def bytes(self):
        return self.full.at[0, pl.ds(0, self.quarter)]

    def along(self, d):
        dp, row, col = self.pos
        target = lax.rem(row + d, 4)
        copies = []
        for src, r0, rows, c0, cols, d0, e0 in self.pieces(target):
            q = rows // 4
            copies.append(remote(
                src.at[span(r0 + dp * q, q), span(c0, cols)],
                self.full.at[row, span(d0 + dp * q, q), pl.ds(e0, cols)],
                self.sz.at[d], self.rz.at[d], (dp, target, col),
            ))
        return copies

    def across(self, d, e):
        dp, row, col = self.pos
        block = lax.rem(row + 4 - d, 4)
        return [
            remote(p, p, self.sp.at[d, e], self.rp.at[d, e], (dp ^ e, row, col)) for p in self.parts(block, dp)
        ]

    def local(self):
        dp, row, col = self.pos
        return [
            pltpu.make_async_copy(
                src.at[span(r0, rows), span(c0, cols)],
                self.full.at[row, pl.ds(d0, rows), pl.ds(e0, cols)], self.loc.at[i],
            )
            for i, (src, r0, rows, c0, cols, d0, e0) in enumerate(self.pieces(row))
        ]

    def start(self):
        for d in (2, 1, 3):
            for c in self.along(d):
                c.start()
        for c in self.local():
            c.start()

    def forward(self):
        for d in (1, 3, 2):
            landed(self.bytes(), self.rz.at[d])
            for e in (3, 1, 2):
                for c in self.across(d, e):
                    c.start()

    def arrived(self):
        for c in self.local():
            c.wait()
        for d in (1, 3, 2):
            for e in (1, 2, 3):
                landed(self.bytes(), self.rp.at[d, e])

    def drain(self):
        for d in (1, 2, 3):
            left(self.bytes(), self.sz.at[d])
            for e in (1, 2, 3):
                left(self.bytes(), self.sp.at[d, e])


class LineReduce:
    SEMS = ((4, 4),) * 3 + ((5, 4),)

    def __init__(self, own, sib, line, sems, pos):
        self.own, self.sib_in, self.line_in = own, sib, line
        self.s_sib, self.r_sib, self.s_line, self.r_line = sems
        self.pos = pos

    def sib(self, stage, b, t):
        dp, row, col = self.pos
        return remote(
            stage.at[t % 2, b], self.sib_in.at[b, t], self.s_sib.at[b, t], self.r_sib.at[b, t], (dp, row, 1 - col)
        )

    def up(self, b, t):
        dp, row, col = self.pos
        return remote(
            self.own.at[b, t], self.line_in.at[b, t], self.s_line.at[b, t], self.r_line.at[b, t], (dp, row + 1, col)
        )

    def down(self, b, t):
        dp, row, col = self.pos
        slot = jnp.where(b == row - 1, 4, b)
        return remote(
            self.own.at[b, t], self.line_in.at[slot, t], self.s_line.at[b, t], self.r_line.at[slot, t],
            (dp, row - 1, col),
        )

    def produce(self, t, stage, rows, fn):
        dp, row, col = self.pos

        there = rows(span(t * BT + (1 - col) * HT, HT))
        for b in (3, 0, 2, 1):
            stage[t % 2, b] = fn(there, b).astype(BF)
            self.sib(stage, b, t).start()
        here = rows(span(t * BT + col * HT, HT))
        for b in (3, 0, 2, 1):
            self.own[b, t] = fn(here, b).astype(BF)

    def wait_stage(self, t, stage):
        for b in range(4):
            self.sib(stage, b, t).wait_send()

    def hop(self, b, t, take):
        dp, row, col = self.pos
        landed(self.sib_in.at[b, t], self.r_sib.at[b, t])
        total = self.own[b, t].astype(F32) + self.sib_in[b, t].astype(F32)
        if take:
            landed(self.line_in.at[b, t], self.r_line.at[b, t])
            total = total + self.line_in[b, t].astype(F32)
        self.own[b, t] = total.astype(BF)

        @pl.when(row < b)
        def _():
            self.up(b, t).start()

        @pl.when(row > b)
        def _():
            self.down(b, t).start()

    def edge(self, t):
        dp, row, col = self.pos

        @pl.when((row == 0) | (row == 3))
        def _():
            for i in range(3):
                self.hop(jnp.where(row == 0, 3 - i, i), t, False)

    def slot(self, t, j):
        dp, row, col = self.pos

        @pl.when((row == 1) | (row == 2))
        def _():
            self.hop(jnp.where(row == 1, 3 - j, j), t, True)
            if j == 1:
                self.hop(jnp.where(row == 1, 0, 3), t, True)

    def final(self, t, total):
        dp, row, col = self.pos
        landed(self.sib_in.at[row, t], self.r_sib.at[row, t])
        total[...] = self.own[row, t].astype(F32) + self.sib_in[row, t].astype(F32)

        @pl.when(row > 0)
        def _():
            landed(self.line_in.at[row, t], self.r_line.at[row, t])
            total[...] += self.line_in[row, t].astype(F32)

        @pl.when(row < 3)
        def _():
            landed(self.line_in.at[4, t], self.r_line.at[4, t])
            total[...] += self.line_in[4, t].astype(F32)

    def drain(self):
        dp, row, col = self.pos
        for b in range(4):
            for t in range(4):
                @pl.when(row < b)
                def _():
                    self.up(b, t).wait_send()

                @pl.when(row > b)
                def _():
                    self.down(b, t).wait_send()


class GradReduce:
    SEMS = ((4,), (4,), (2,), (2,), (4,), (4,), (2,), (2,), (4,), (4,))

    def __init__(self, grad, near, far, mid, part, place, shared, sems, pos):
        self.grad, self.near, self.far, self.mid, self.part = grad, near, far, mid, part
        self.place, self.shared = place, shared
        self.s1, self.r1, self.sm, self.rm, self.s2, self.r2, self.s3, self.r3, self.s4, self.r4 = sems
        self.pos = pos
        self.rows = grad.shape[1] // 4
        self.n = self.rows // 2

    def cut(self, q, h):
        return self.grad.at[:, span(q * self.rows + h * self.n, self.n)]

    def peer(self, e):
        dp, row, col = self.pos
        return (dp ^ e, row, col)

    def first(self, i):
        dp, row, col = self.pos
        e = 1 + i // 2
        q = dp ^ (3 if i % 2 else e)
        return remote(self.cut(q, i // 2), self.near.at[i], self.s1.at[i], self.r1.at[i], self.peer(e))

    def middle(self, h):
        return remote(self.mid.at[h], self.far.at[h], self.sm.at[h], self.rm.at[h], self.peer(2 - h))

    def second(self, d):
        dp, row, col = self.pos
        target = lax.rem(row + d, 4)
        return [
            remote(
                self.part.at[target, :, pl.ds(c0, cols)], dst, self.s2.at[d], self.r2.at[d], (dp, target, col)
            )
            for dst, c0, cols in self.place(row, dp)
        ]

    def third(self, h):
        dp, row, col = self.pos
        ref = self.shared(dp, h)
        return remote(ref, ref, self.s3.at[h], self.r3.at[h], self.peer(2 - h))

    def fourth(self, i):
        dp, row, col = self.pos
        h = i // 2
        ref = self.shared(dp ^ (2 - h) if i % 2 else dp, h)
        return remote(ref, ref, self.s4.at[i], self.r4.at[i], self.peer(1 + h))

    def start(self):
        for i in (1, 3, 0, 2):
            self.first(i).start()

    def middle_sum(self):
        dp, row, col = self.pos
        for h in range(2):
            i = 2 * h + 1
            landed(self.near.at[i], self.r1.at[i])
            self.mid[h] = (self.cut(dp ^ (2 - h), h)[...].astype(F32) + self.near[i].astype(F32)).astype(BF)
            self.middle(h).start()

    def own(self):
        dp, row, col = self.pos
        return [
            pltpu.make_async_copy(self.part.at[row, :, pl.ds(c0, cols)], dst, self.s2.at[0])
            for dst, c0, cols in self.place(row, dp)
        ]

    def sum_and_spread(self):
        dp, row, col = self.pos
        for h in range(2):
            landed(self.near.at[2 * h], self.r1.at[2 * h])
            landed(self.far.at[h], self.rm.at[h])
        for d in (2, 1, 3, 0):
            b = lax.rem(row + d, 4)
            for h in range(2):
                total = self.grad.at[b, span(dp * self.rows + h * self.n, self.n)][...].astype(F32)
                total = total + self.near[2 * h, b].astype(F32) + self.far[h, b].astype(F32)
                self.part[b, h * self.n : (h + 1) * self.n, :] = total.astype(BF)
            for c in self.own() if d == 0 else self.second(d):
                c.start()

    def share(self):
        pltpu.make_async_copy(self.part.at[0], self.part.at[0], self.s2.at[0]).wait()
        for d in (1, 2, 3):
            landed(self.part.at[0], self.r2.at[d])
        self.third(0).start()
        self.third(1).start()
        self.fourth(0).start()
        self.fourth(2).start()

    def relay(self):
        dp, row, col = self.pos
        for h in range(2):
            landed(self.shared(dp, h), self.r3.at[h])
            self.fourth(2 * h + 1).start()

    def finish(self):
        dp, row, col = self.pos
        for i in range(4):
            landed(self.shared(dp, i // 2), self.r4.at[i])
            self.first(i).wait_send()
            self.fourth(i).wait_send()
        for h in range(2):
            self.middle(h).wait_send()
            self.third(h).wait_send()
        for d in (1, 2, 3):
            left(self.part.at[0], self.s2.at[d])


def unrope(gt, cosv, sinv):
    rows = []
    for h in range(2):
        o = h * HD
        a, b = gt[o : o + 8], gt[o + 8 : o + 16]
        rows += [a * cosv + b * sinv, b * cosv - a * sinv, gt[o + 16 : o + HD]]
    return jnp.concatenate(rows, 0)


def layer_kernel(
    x, cot, wq, wu, wo, wd, seg, vec,
    out_o, gin_o, small_o, cols_o, fq_o, fu_o, fo_o, fd_o,
    xf, nrm, cf, w1, w2, q_v, k_v, v_v, tr_v, att_v, da, act_v, gp_v, raw, dqt, dka, dva,
    stat, lse, delta, cs, rng, gbs, d1,
    own_a, sib_a, line_a, own_b, sib_b, line_b, stage, total,
    gq, nq, rq, mq, tq, gu, nu, ru, mu, tu, go, no, ro, mo, to, gd, nd, rd, md, td,
    out_v, gin_v, send_st, st, sums, sums_in, small, small_sib, small_in,
    *sems,
):
    pos = where()
    dp, row, col = pos
    toks = seg.shape[1]
    half = toks // 2
    hc = wq.shape[2] // 4
    fc = wu.shape[1] // 4
    h3 = 3 * hc
    depth = wq.shape[1]
    scale = 1.0 / math.sqrt(HD)
    taken = [0]

    def take(cls):
        first = taken[0]
        taken[0] = first + len(cls.SEMS)
        return sems[first : taken[0]]

    X = LineGather(x, xf, take(LineGather), pos)
    C = LineGather(cot, cf, take(LineGather), pos)

    def pieces1(t):
        return [(wq.at[j], 0, depth, t * hc, hc, 0, j * hc) for j in range(3)]

    def pieces3(t):
        return [(wu, 0, depth, t * fc, fc, 0, 0)]

    def pieces2(t):
        return [(wo, t * hc, hc, 0, depth, 0, 0), (wd, t * fc, fc, 0, depth, hc, 0)]

    W1 = WeightGather(w1.at[:, :, pl.ds(0, h3)], pieces1, take(WeightGather), pos)
    W3 = WeightGather(w1.at[:, :, pl.ds(h3, fc)], pieces3, take(WeightGather), pos)
    W2 = WeightGather(w2, pieces2, take(WeightGather), pos)
    A = LineReduce(own_a, sib_a, line_a, take(LineReduce), pos)
    B = LineReduce(own_b, sib_b, line_b, take(LineReduce), pos)

    def rows_of(q):
        return span(q * (depth // 4), depth // 4)

    def rows_half(q, h):
        return span(q * (depth // 4) + h * (depth // 8), depth // 8)

    def place_q(s, q):
        return [(fq_o.at[j, rows_of(q), span(s * hc, hc)], j * hc, hc) for j in range(3)]

    def place_u(s, q):
        return [(fu_o.at[rows_of(q), span(s * fc, fc)], 0, fc)]

    def tall(ref):
        n = ref.shape[1] // 4
        return lambda s, q: [(ref.at[s, span(q * n, n)], 0, depth)]

    def tall_share(ref):
        n = ref.shape[1] // 4
        return lambda q, h: ref.at[:, span(q * n + h * (n // 2), n // 2)]

    GQ = GradReduce(gq, nq, rq, mq, tq, place_q, lambda q, h: fq_o.at[:, rows_half(q, h)], take(GradReduce), pos)
    GU = GradReduce(gu, nu, ru, mu, tu, place_u, lambda q, h: fu_o.at[rows_half(q, h)], take(GradReduce), pos)
    GO = GradReduce(go, no, ro, mo, to, tall(fo_o), tall_share(fo_o), take(GradReduce), pos)
    GD = GradReduce(gd, nd, rd, md, td, tall(fd_o), tall_share(fd_o), take(GradReduce), pos)
    gs, gr, misc, s_st, r_st, s_sum, r_sum, s_row, r_row, s_small, r_small, s_own, r_own = sems[taken[0] :]

    greet(dp, row, col)
    X.start((0, 1))
    at_gain = h3 * 4 + fc * 4
    gbs[pl.ds(row, 1)] = jnp.zeros((1, 8, depth), F32)
    gbs[pl.ds(row, 1), 0:1, :] = vec[0:1, at_gain : at_gain + depth][None]
    gbs[pl.ds(row, 1), 1:2, :] = vec[0:1, at_gain + depth : at_gain + 2 * depth][None]

    def gain_copy(d):
        return remote(gbs.at[row], gbs.at[row], gs.at[d], gr.at[d], (dp, lax.rem(row + d, 4), col))

    for d in (1, 2, 3):
        gain_copy(d).start()
    X.local().wait()

    bias = jnp.concatenate(
        [vec[0:1, span((4 * j + row) * hc, hc)] for j in range(3)] + [vec[0:1, span(12 * hc + row * fc, fc)]], 1
    )
    weights = w1.reshape(w1.shape[0] * w1.shape[1], w1.shape[2])

    def project(t):
        def token_step(i, _):
            at = span(t * BT + i * TC, TC)
            blocks = [xf[b, at, :].astype(F32) for b in range(4)]
            one = (blocks[0] + blocks[1]) + (blocks[2] + blocks[3])
            two = (blocks[0] * blocks[0] + blocks[1] * blocks[1]) + (
                blocks[2] * blocks[2] + blocks[3] * blocks[3]
            )
            mean = jnp.sum(one, 1, keepdims=True) * (1.0 / D)
            var = jnp.sum(two, 1, keepdims=True) * (1.0 / D) - mean * mean
            inv = lax.rsqrt(var + EPSILON)
            lane = lax.broadcasted_iota(jnp.int32, (TC, 128), 1)
            stat[at, :] = jnp.where(lane == 0, mean, inv)
            parts = []
            for b in range(4):
                n = ((blocks[b] - mean) * inv * gbs[b, 0:1, :] + gbs[b, 1:2, :]).astype(BF)
                nrm[b, at, :] = n
                parts.append(n)
            acc = dot(jnp.concatenate(parts, 1), weights[:, 0:h3]) + bias[:, 0:h3]
            cosv, sinv = cs[0:8, at], cs[8:16, at]
            q_v[at, :] = unrope(acc[:, 0:128].T, cosv, -sinv).T.astype(BF)
            k_v[at, :] = unrope(acc[:, 128:256].T, cosv, -sinv).T.astype(BF)
            v_v[at, :] = acc[:, 256:384].astype(BF)
            tr_v[:, at] = acc[:, 256:384].T.astype(BF)
            return 0

        lax.fori_loop(0, BT // TC, token_step, 0)

    def hidden(t):
        def token_step(i, _):
            at = span(t * BT + i * TC, TC)
            rows = jnp.concatenate([nrm[b, at, :] for b in range(4)], 1)
            up = dot(rows, weights[:, h3:]) + bias[:, h3:]
            phi = 0.5 * (1.0 + lax.erf(up * (1.0 / math.sqrt(2.0))))
            act_v[at, :] = (up * phi).astype(BF)
            gp_v[at, :] = (phi + up * jnp.exp(-0.5 * up * up) * (1.0 / math.sqrt(2.0 * math.pi))).astype(BF)
            return 0

        lax.fori_loop(0, BT // TC, token_step, 0)

    def allowed(k0, at, diagonal):
        kidx = lax.broadcasted_iota(jnp.int32, (BK, BT), 0)
        if not diagonal:
            return kidx >= rng[0:1, at] - k0
        kidx = kidx + k0 - rng[0:1, at]
        return (kidx >= 0) & (kidx <= rng[1:2, at])

    def attend(t):
        at = pl.ds(t * BT, BT)
        qs = q_v[at, :] * BF(scale)
        heads = [jnp.where(lane_mask(h, BT), qs, BF(0)) for h in range(2)]

        def k_step(kb, carry, diagonal=False):
            k0 = kb * BK if diagonal else pl.multiple_of(kb * BK, BK)
            kk = k_v[pl.ds(k0, BK), :]
            ok = allowed(k0, at, diagonal)
            new = []
            for h in range(2):
                m, l, acc = carry[h]
                s = jnp.where(ok, dot(kk, heads[h], NT), MASKED)
                m2 = jnp.maximum(m, jnp.max(s, 0, keepdims=True))
                p = jnp.exp(s - m2)
                c = jnp.exp(m - m2)
                l = l * c + jnp.sum(p, 0, keepdims=True)
                vt = tr_v[h * HD : (h + 1) * HD, pl.ds(k0, BK)]
                acc = acc * c + dot(vt, p.astype(BF))
                new.append((m2, l, acc))
            return tuple(new)

        init = tuple(
            (jnp.full((1, BT), -1e30, F32), jnp.zeros((1, BT), F32), jnp.zeros((HD, BT), F32))
            for _ in range(2)
        )
        res = lax.fori_loop(0, t, k_step, init) if t else init
        res = k_step(t, res, True)
        for h in range(2):
            m, l, acc = res[h]
            raw[h * HD : (h + 1) * HD, at] = acc / l
            lse[h : h + 1, at] = m + jnp.log(l)
        att_v[at, :] = raw[:, at].T.astype(BF)

    def out_part(t):
        def rows(at):
            return jnp.concatenate([att_v[at, :], act_v[at, :]], 1)

        if t >= 2:
            A.wait_stage(t - 2, stage)
        A.produce(t, stage, rows, lambda joined, b: dot(joined, w2[b]))

    def joined_back(t):
        def chunk(i, _):
            at = span(t * BT + i * TC, TC)
            dj = dot(
                jnp.concatenate([cf[b, at, :] for b in range(4)], 1),
                jnp.concatenate([w2[b] for b in range(4)], 1),
                NT,
            )
            d_att = dj[:, 0:128].astype(BF)
            da[at, :] = d_att
            d1[at, 384:] = (dj[:, 128:] * gp_v[at, :].astype(F32)).astype(BF)
            prod = d_att.astype(F32).T * raw[:, at]
            for h in range(2):
                delta[h : h + 1, at] = jnp.sum(prod[h * HD : (h + 1) * HD], 0, keepdims=True)
            return 0

        lax.fori_loop(0, BT // TC, chunk, 0)

    def attend_back(t, lo, hi):
        at = pl.ds(t * BT, BT)
        qs = q_v[at, :] * BF(scale)
        do = da[at, :]
        qh = [jnp.where(lane_mask(h, BT), qs, BF(0)) for h in range(2)]
        doh = [jnp.where(lane_mask(h, BT), do, BF(0)) for h in range(2)]
        if lo == 0:
            dqt[...] = jnp.zeros_like(dqt)

        for kb in range(lo * 256 // BK, hi * 256 // BK):
            k0 = kb * BK
            ka = pl.ds(k0, BK)
            kk = k_v[ka, :]
            vv = v_v[ka, :]
            ok = allowed(k0, at, kb == t)
            dk, dv = dka[ka, :], dva[ka, :]
            for h in range(2):
                s = jnp.where(ok, dot(kk, qh[h], NT), MASKED)
                p = jnp.exp(s - lse[h : h + 1, at])
                ds = (p * (dot(vv, doh[h], NT) - delta[h : h + 1, at])).astype(BF)
                dv = dv + dot(p.astype(BF), doh[h])
                dk = dk + dot(ds, qh[h])
                rows = slice(h * HD, (h + 1) * HD)
                dqt[rows, :] += dot(tr_v[rows, ka], ds)
            dka[ka, :] = dk
            dva[ka, :] = dv

    def finish_back(t):
        at = pl.ds(t * BT, BT)
        cosv, sinv = cs[0:8, at], cs[8:16, at]
        d1[at, 0:128] = unrope(dqt[...] * scale, cosv, sinv).T.astype(BF)
        d1[at, 128:256] = unrope(dka[at, :].T, cosv, sinv).T.astype(BF)
        d1[at, 256:384] = dva[at, :].astype(BF)

    def norm_part(t):
        (A if t >= 2 else B).wait_stage(t if t >= 2 else t + 2, stage)
        B.produce(t, stage, lambda at: d1[at, :], lambda rows, b: dot(rows, w1[b], NT))

    def gains():
        for d in (1, 2, 3):
            landed(gbs.at[0], gr.at[d])

    def prep():
        labels = seg[...]
        start = jnp.zeros_like(labels)
        for d in range(1, 8):
            below = jnp.sum((labels == d - 1).astype(F32), 1, keepdims=True).astype(jnp.int32)
            start = start + jnp.where(labels >= d, below, 0)
        index = lax.broadcasted_iota(jnp.int32, labels.shape, 1)
        place = index - start
        rng[0:1, :] = start
        rng[1:2, :] = place
        power = lax.broadcasted_iota(jnp.int32, (8, 1), 0).astype(F32) * (-2.0 * math.log(10000.0) / ROT)
        ang = place.astype(F32) * jnp.exp(power)
        cs[0:8, :] = jnp.cos(ang)
        cs[8:16, :] = jnp.sin(ang)
        dka[...] = jnp.zeros_like(dka)
        dva[...] = jnp.zeros_like(dva)

    def turn():
        def step(i, _):
            at = span(i * BT, BT)
            tr_v[:, at] = k_v[at, :].astype(F32).T.astype(BF)
            return 0

        lax.fori_loop(0, toks // BT, step, 0)

    def grads2():
        for b in range(4):
            go[b] = dot(att_v[...], cf[b], TN).astype(BF)
            gd[b] = dot(act_v[...], cf[b], TN).astype(BF)

    def gradsu():
        for b in range(4):
            gu[b] = dot(nrm[b], d1[:, 384:], TN).astype(BF)

    def gradsq():
        for b in range(4):
            gq[b] = dot(nrm[b], d1[:, 0:384], TN).astype(BF)

    def sum_copy(e):
        return remote(sums.at[0], sums_in.at[e - 1], s_sum.at[e], r_sum.at[e], (dp ^ e, row, col))

    def row_copy(d):
        return remote(sums.at[1], cols_o.at[row], s_row.at[d], r_row.at[d], (dp, lax.rem(row + d, 4), col))

    own_cols = pltpu.make_async_copy(sums.at[1], cols_o.at[row], misc.at[0])

    def colsum():
        sums[0] = dot(jnp.ones((8, toks), BF), d1[...])
        for e in (3, 1, 2):
            sum_copy(e).start()

    def sums_on():
        for e in (1, 2, 3):
            landed(sums_in.at[e - 1], r_sum.at[e])
        sums[1] = (sums[0] + sums_in[0]) + (sums_in[1] + sums_in[2])
        for d in (1, 2, 3):
            row_copy(d).start()
        own_cols.start()

    at_obias = at_gain + 2 * depth

    def deliver(src, dst, i, t):
        at = span((t % 2) * BT + col * HT, HT)
        here = pltpu.make_async_copy(src.at[t], dst.at[at], s_own.at[i, t])
        there = remote(src.at[t], dst.at[at], s_own.at[i, t], r_own.at[i, t], (dp, row, 1 - col))
        return here, there

    def send_result(src, dst, i, t):
        here, there = deliver(src, dst, i, t)

        @pl.when(col == t // 2)
        def _():
            here.start()

        @pl.when(col != t // 2)
        def _():
            there.start()

    def end_result(src, dst, i, t):
        here, there = deliver(src, dst, i, t)

        @pl.when(col == t // 2)
        def _():
            here.wait()
            landed(dst.at[span((t % 2) * BT + (1 - col) * HT, HT)], r_own.at[i, t])

        @pl.when(col != t // 2)
        def _():
            there.wait_send()

    def mine(t):
        return span(t * BT + col * HT, HT)

    def out_final(t):
        A.final(t, total)
        out_v[t] = (
            xf[row, mine(t), :].astype(F32) + total[...] + vec[0:1, at_obias : at_obias + depth]
        ).astype(BF)
        send_result(out_v, out_o, 0, t)

    def stat_copy(d, k):
        return remote(
            send_st.at[k], st.at[d - 1, k], s_st.at[d, k], r_st.at[d, k], (dp, lax.rem(row + d, 4), col)
        )

    gain = vec[0:1, at_gain : at_gain + depth]
    small[...] = jnp.zeros_like(small)

    def centred(t):
        mean, inv = stat[mine(t), 0:1], stat[mine(t), 1:2]
        return (xf[row, mine(t), :].astype(F32) - mean) * inv, inv, cf[row, mine(t), :].astype(F32)

    def norm_final(t):
        B.final(t, total)
        dn = total[...]
        xh, inv, ct = centred(t)
        dc = dn * gain
        s0 = jnp.sum(dc, 1, keepdims=True)
        s1 = jnp.sum(dc * xh, 1, keepdims=True)
        lane = lax.broadcasted_iota(jnp.int32, (HT, 128), 1)
        send_st[t // 2, :, (t % 2) * HT : (t % 2 + 1) * HT] = jnp.where(
            lane == 0, s0, jnp.where(lane == 1, s1, 0.0)
        ).T[0:8, :]
        if t % 2 == 0:
            for d in (2, 1, 3):
                stat_copy(d, t // 2).start()
        gin_v[t] = dc
        small[0, 0:1, :] += jnp.sum(dn * xh, 0, keepdims=True)
        small[0, 1:2, :] += jnp.sum(dn, 0, keepdims=True)
        small[0, 2:3, :] += jnp.sum(ct, 0, keepdims=True)
        if t == 0:
            sib_small.start()

    sib_small = remote(small.at[0], small_sib, s_small.at[0], r_small.at[0], (dp, row, 1 - col))

    def small_copy(e):
        return remote(small.at[1], small_in.at[e - 1], s_small.at[e], r_small.at[e], (dp ^ e, row, col))

    def small_on():
        landed(small_sib, r_small.at[0])
        small[1] = small[0] + small_sib[...]
        for e in (3, 1, 2):
            small_copy(e).start()

    def grad_final(k):
        acc = send_st[k]
        for d in (1, 2, 3):
            landed(st.at[d - 1, k], r_st.at[d, k])
            acc = acc + st[d - 1, k]
        both = jnp.concatenate([acc, jnp.zeros((120, BT), F32)], 0).T
        for t in (2 * k + 1, 2 * k):
            xh, inv, ct = centred(t)
            r = slice((t % 2) * HT, (t % 2 + 1) * HT)
            gin_v[t] = inv * (gin_v[t] - both[r, 0:1] * (1.0 / D) - xh * (both[r, 1:2] * (1.0 / D))) + ct
            send_result(gin_v, gin_o, 1, t)
    X.send_own(0)
    W2.start()
    gains()
    X.step(1,0)
    X.send_own(1)
    W1.start()
    W3.start()
    W2.forward()
    X.step(1,1)
    X.step(2,0)
    C.start((1, 0))
    X.send_own(2)
    W1.forward()
    W3.forward()
    X.step(3,0)
    X.step(2,1)
    X.step(1,2)
    C.local().wait()
    prep()
    X.step(3,1)
    X.ready(0)
    X.send_own(3)
    X.step(2,2)
    W1.arrived()
    W3.arrived()
    C.send_own(3)
    project(0)
    hidden(0)
    C.send_own(2)
    X.ready(1)
    W2.arrived()
    C.send_own(1)
    attend(0)
    C.send_own(0)
    project(1)
    hidden(1)
    attend(1)
    C.step(1,3)
    out_part(0)
    A.edge(0)
    X.step(1,3)
    X.step(3,2)
    out_part(1)
    A.edge(1)
    X.ready(2)
    project(2)
    hidden(2)
    attend(2)
    X.step(2,3)
    out_part(2)
    A.edge(2)
    C.step(2,3)
    C.step(1,1)
    A.slot(0, 0)
    X.step(3,3)
    X.ready(3)
    C.step(1,2)
    project(3)
    hidden(3)
    attend(3)
    C.step(3,3)
    C.step(2,1)
    C.step(2,2)
    out_part(3)
    A.edge(3)
    C.step(3,1)
    C.step(3,2)
    C.step(1,0)
    C.ready(3)
    turn()
    joined_back(3)
    A.slot(0, 1)
    attend_back(3, 0, 2)
    attend_back(3, 2, 4)
    attend_back(3, 4, 6)
    A.slot(1, 0)
    C.step(2,0)
    C.step(3,0)
    attend_back(3, 6, 8)
    C.ready(0)
    finish_back(3)
    C.ready(2)
    A.slot(1, 1)
    C.ready(1)
    grads2()
    GD.start()
    A.slot(2, 0)
    joined_back(2)
    GO.start()
    norm_part(3)
    B.edge(3)
    attend_back(2, 0, 2)
    GD.middle_sum()
    joined_back(0)
    A.slot(2, 1)
    A.slot(3, 0)
    joined_back(1)
    gradsu()
    attend_back(2, 2, 4)
    A.slot(3, 1)
    GD.sum_and_spread()
    attend_back(2, 4, 6)
    finish_back(2)
    norm_part(2)
    B.edge(2)
    GO.middle_sum()
    GU.start()
    B.slot(3, 0)
    attend_back(1, 0, 2)
    attend_back(1, 2, 4)
    finish_back(1)
    GO.sum_and_spread()
    B.slot(3, 1)
    GU.middle_sum()
    norm_part(1)
    B.edge(1)
    B.slot(2, 0)
    GD.share()
    attend_back(0, 0, 2)
    finish_back(0)
    B.slot(2, 1)
    gradsq()
    GQ.start()
    GU.sum_and_spread()
    B.slot(1, 0)
    GD.relay()
    norm_part(0)
    B.edge(0)
    GQ.middle_sum()
    B.slot(1, 1)
    GO.share()
    out_final(3)
    GU.share()
    out_final(0)
    out_final(2)
    B.slot(0, 0)
    out_final(1)
    GQ.sum_and_spread()
    GU.relay()
    norm_final(3)
    GO.relay()
    colsum()
    B.slot(0, 1)
    norm_final(2)
    norm_final(1)
    GQ.share()
    norm_final(0)
    small_on()
    GD.finish()
    GO.finish()
    GQ.relay()
    sums_on()
    GU.finish()
    grad_final(1)
    grad_final(0)
    GQ.finish()

    for e in (1, 2, 3):
        landed(small_in.at[e - 1], r_small.at[e])
    small_o[...] = (small[1] + small_in[0]) + (small_in[1] + small_in[2])

    X.drain()
    C.drain()
    W1.drain()
    W3.drain()
    W2.drain()
    for d in (1, 2, 3):
        gain_copy(d).wait_send()
        for k in range(2):
            stat_copy(d, k).wait_send()
        row_copy(d).wait_send()
        sum_copy(d).wait_send()
        small_copy(d).wait_send()
        landed(sums.at[1], r_row.at[d])
    sib_small.wait_send()
    A.drain()
    B.wait_stage(1, stage)
    B.wait_stage(0, stage)
    B.drain()
    own_cols.wait()
    for t in range(4):
        end_result(out_v, out_o, 0, t)
        end_result(gin_v, gin_o, 1, t)


def layer(x, cot, wq, wu, wo, wd, seg, vec):
    toks = seg.shape[1]
    half = toks // 2
    depth = wq.shape[1]
    hc, fc = wq.shape[2] // 4, wu.shape[1] // 4
    h3 = 3 * hc
    sd = jax.ShapeDtypeStruct
    V = pltpu.VMEM
    grads = []
    for r, c in ((depth, h3), (depth, fc), (hc, depth), (fc, depth)):
        grads += [
            V((4, r, c), BF), V((4, 4, r // 8, c), BF), V((2, 4, r // 8, c), BF), V((2, 4, r // 8, c), BF),
            V((4, r // 4, c), BF),
        ]
    sems = (
        LineGather.SEMS * 2 + WeightGather.SEMS * 3 + LineReduce.SEMS * 2 + GradReduce.SEMS * 4
        + ((4,), (4,), (8,), (4, 2), (4, 2), (4,), (4,), (4,), (4,), (4,), (4,), (2, 4), (2, 4))
    )
    return pl.pallas_call(
        layer_kernel,
        name="layer",
        out_shape=(
            sd((half, depth), BF), sd((half, depth), F32), sd((8, depth), F32), sd((4, 8, h3 + fc), F32),
            sd((3, depth, 4 * hc), BF), sd((depth, 4 * fc), BF), sd((4, hc, depth), BF), sd((4, fc, depth), BF),
        ),
        in_specs=[hbm()] * 6 + [vmem()] * 2,
        out_specs=(hbm(), hbm(), vmem(), hbm(), hbm(), hbm(), hbm(), hbm()),
        scratch_shapes=[
            V((4, toks, depth), BF), V((4, toks, depth), BF), V((4, toks, depth), BF),
            V((4, depth, h3 + fc), BF), V((4, hc + fc, depth), BF),
            V((toks, hc), BF), V((toks, hc), BF), V((toks, hc), BF), V((hc, toks), BF),
            V((toks, hc), BF), V((toks, hc), BF), V((toks, fc), BF), V((toks, fc), BF),
            V((hc, toks), F32), V((hc, BT), F32), V((toks, hc), F32), V((toks, hc), F32),
            V((toks, 128), F32), V((8, toks), F32), V((8, toks), F32), V((16, toks), F32),
            V((8, toks), jnp.int32), V((4, 8, depth), F32), V((toks, h3 + fc), BF),
            V((4, 4, HT, depth), BF), V((4, 4, HT, depth), BF), V((5, 4, HT, depth), BF),
            V((4, 4, HT, depth), BF), V((4, 4, HT, depth), BF), V((5, 4, HT, depth), BF),
            V((2, 4, HT, depth), BF), V((HT, depth), F32),
            *grads,
            V((4, HT, depth), BF), V((4, HT, depth), F32),
            V((2, 8, BT), F32), V((3, 2, 8, BT), F32), V((2, 8, h3 + fc), F32), V((3, 8, h3 + fc), F32),
            V((2, 8, depth), F32), V((8, depth), F32), V((3, 8, depth), F32),
            *dmas(*sems),
        ],
        compiler_params=pltpu.CompilerParams(
            collective_id=0, has_side_effects=True, vmem_limit_bytes=62 * 2**20
        ),
    )(x, cot, wq, wu, wo, wd, seg, vec)


def per_device_sliced(
    inputs, segments, ln_gain, ln_bias, w_qkv, b_qkv, w_out, w_up, b_up, w_down, out_bias, cotangent
):
    nrow = lax.axis_size("row")
    dpart = inputs.shape[1]
    hcols = w_qkv.shape[2] // nrow
    h3 = 3 * hcols
    vec = jnp.concatenate([b_qkv.reshape(-1), b_up, ln_gain, ln_bias, out_bias]).astype(F32)[None]
    layer_out, grad_inputs, small, cols, fq, fu, fo, fd = layer(
        inputs, cotangent, w_qkv.transpose(1, 0, 2), w_up, w_out, w_down, segments, vec
    )
    cols = cols[:, 0]
    grad_b_qkv = cols[:, :h3].reshape(nrow, 3, hcols).transpose(1, 0, 2).reshape(3, -1)
    return (
        layer_out, grad_inputs, small[0], small[1],
        fq.astype(F32).transpose(1, 0, 2), grad_b_qkv,
        fo.reshape(w_out.shape).astype(F32), fu.astype(F32), cols[:, h3:].reshape(-1),
        fd.reshape(w_down.shape).astype(F32), small[2],
    )


FLOOR_INIT = -1e30


def doc_positions(labels):
    token_index = jnp.arange(labels.shape[1], dtype=jnp.int32)
    flags = jnp.concatenate(
        [jnp.ones((labels.shape[0], 1), dtype=jnp.bool_), labels[:, 1:] != labels[:, :-1]], 1
    )
    starts = lax.cummax(jnp.where(flags, token_index[None, :], 0), axis=1)
    return token_index[None, :] - starts


def rotate(tensor_in, positions):
    half_rot = ROT // 2
    inverse = 10000.0 ** (-(jnp.arange(half_rot, dtype=jnp.float32) * 2.0 / ROT))
    angles = positions.astype(jnp.float32)[:, None] * inverse[None, :]
    cosines = jnp.cos(angles)[:, None, :]
    sine_vals = jnp.sin(angles)[:, None, :]
    first_half = tensor_in[..., :half_rot]
    second_half = tensor_in[..., half_rot:ROT]
    rest_dims = tensor_in[..., ROT:]
    return jnp.concatenate(
        [
            first_half * cosines - second_half * sine_vals,
            second_half * cosines + first_half * sine_vals,
            rest_dims,
        ],
        -1,
    )


def slice_rows(array_in, first_row, row_count, axis_num=0):
    return lax.dynamic_slice_in_dim(array_in, first_row, row_count, axis_num)


def put_rows(array_in, update, first_row, axis_num=0):
    return lax.dynamic_update_slice_in_dim(array_in, update, first_row, axis_num)


def block_pairs(query_blocks, key_blocks):
    q_list = jnp.repeat(jnp.arange(query_blocks, dtype=jnp.int32), key_blocks)
    k_list = jnp.tile(jnp.arange(key_blocks, dtype=jnp.int32), query_blocks)
    return (q_list, k_list)


def per_device_general(
    inputs, segments, ln_gain, ln_bias, w_qkv, b_qkv, w_out, w_up, b_up, w_down, out_bias, cotangent
):
    local_rows, feature_cols = inputs.shape
    part_count = lax.axis_size("row")
    row_index = lax.axis_index("row")
    head_cols = w_qkv.shape[2]
    head_count = head_cols // HD
    group_seqs = segments.shape[0]
    all_rows = group_seqs * SEQ_LEN
    span = all_rows // part_count
    query_blocks = span // span
    score_scale = 1.0 / math.sqrt(HD)
    labels = (segments + (jnp.arange(group_seqs, dtype=jnp.int32) * SEQ_LEN)[:, None]).reshape(-1)
    positions = doc_positions(segments).reshape(-1)
    token_index = jnp.arange(all_rows, dtype=jnp.int32)
    my_labels = slice_rows(labels, row_index * span, span)
    my_index = slice_rows(token_index, row_index * span, span)
    my_positions = slice_rows(positions, row_index * span, span)
    float_in = inputs.astype(jnp.float32)
    ln_sums = lax.psum((jnp.sum(float_in, 1), jnp.sum(float_in * float_in, 1)), "row")
    row_mean = ln_sums[0] / D
    row_var = ln_sums[1] / D - row_mean * row_mean
    inv_std = lax.rsqrt(row_var + EPSILON)
    centred = (float_in - row_mean[:, None]) * inv_std[:, None]
    normed = (centred * ln_gain.astype(jnp.float32) + ln_bias.astype(jnp.float32)).astype(
        jnp.bfloat16
    )
    gathered_hidden = lax.all_gather(normed, "col", axis=0, tiled=True)
    first_weights = jnp.concatenate([w_qkv.reshape(feature_cols, 3 * head_cols), w_up], 1)
    first_bias = jnp.concatenate(
        [b_qkv.reshape(3 * head_cols).astype(jnp.float32), b_up.astype(jnp.float32)]
    )
    first_out = (
        lax.psum_scatter(
            jnp.dot(
                slice_rows(gathered_hidden, jnp.int32(0), lax.axis_size("row") * span),
                first_weights,
                preferred_element_type=jnp.float32,
            ).astype(jnp.bfloat16),
            "row",
            scatter_dimension=0,
            tiled=True,
        ).astype(jnp.float32)
        + first_bias
    )

    def rotate_mine(tensor_in):
        return rotate(tensor_in, my_positions)

    query_lin = first_out[:, :head_cols].reshape(span, head_count, HD)
    key_lin = first_out[:, head_cols : 2 * head_cols].reshape(span, head_count, HD)
    query = rotate_mine(query_lin).astype(jnp.bfloat16)
    key_rows = rotate_mine(key_lin).astype(jnp.bfloat16)
    value_rows = (
        first_out[:, 2 * head_cols : 3 * head_cols]
        .reshape(span, head_count, HD)
        .astype(jnp.bfloat16)
    )
    up_lin = first_out[:, 3 * head_cols :]
    activated = jax.nn.gelu(up_lin, approximate=False).astype(jnp.bfloat16)

    def over_keys(fold_step, initial):
        return fold_step(
            initial,
            (
                lax.all_gather(key_rows, "row", axis=0, tiled=True),
                lax.all_gather(value_rows, "row", axis=0, tiled=True),
            ),
            jnp.int32(0),
        )

    def key_setup(pieces, first_row):
        row_count = pieces[0].shape[0]
        piece_labels = slice_rows(labels, first_row, row_count)
        piece_index = slice_rows(token_index, first_row, row_count)
        return (row_count, span, piece_labels, piece_index)

    def block_live(piece_labels, piece_index, key_size, q_block, k_block):
        q_labels = slice_rows(my_labels, q_block * span, span)
        q_index = slice_rows(my_index, q_block * span, span)
        k_labels = slice_rows(piece_labels, k_block * key_size, key_size)
        k_index = slice_rows(piece_index, k_block * key_size, key_size)
        return (
            (jnp.max(q_index) >= jnp.min(k_index))
            & (jnp.min(q_labels) <= jnp.max(k_labels))
            & (jnp.min(k_labels) <= jnp.max(q_labels))
        )

    def block_scores(pieces, piece_labels, piece_index, key_size, q_block, k_block):
        q_start = q_block * span
        k_start = k_block * key_size
        q_labels = slice_rows(my_labels, q_start, span)
        q_index = slice_rows(my_index, q_start, span)
        k_labels = slice_rows(piece_labels, k_start, key_size)
        k_index = slice_rows(piece_index, k_start, key_size)
        q_block_rows = slice_rows(query, q_start, span)
        k_block_rows = slice_rows(pieces[0], k_start, key_size)
        v_block_rows = slice_rows(pieces[1], k_start, key_size)
        scores = (
            jnp.einsum(
                "qhd,khd->hqk", q_block_rows, k_block_rows, preferred_element_type=jnp.float32
            )
            * score_scale
        )
        allowed = (q_labels[:, None] == k_labels[None, :]) & (k_index[None, :] <= q_index[:, None])
        scores = jnp.where(allowed[None], scores, MASKED)
        return (q_start, k_start, scores, q_block_rows, k_block_rows, v_block_rows)

    def forward_piece(running, pieces, first_row):
        row_count, key_size, piece_labels, piece_index = key_setup(pieces, first_row)
        q_list, k_list = block_pairs(query_blocks, row_count // key_size)

        def forward_pair_step(current, pair_ids):
            q_block, k_block = pair_ids

            def update(inner_state):
                row_max, row_sum, row_acc = inner_state
                q_start, k_start, scores, q_block_rows, k_block_rows, v_block_rows = block_scores(
                    pieces, piece_labels, piece_index, key_size, q_block, k_block
                )
                old_max = slice_rows(row_max, q_start, span, 1)
                new_max = jnp.maximum(old_max, jnp.max(scores, -1))
                weights = jnp.exp(scores - new_max[..., None])
                keep_part = jnp.exp(old_max - new_max)
                new_sum = slice_rows(row_sum, q_start, span, 1) * keep_part + jnp.sum(weights, -1)
                added = jnp.einsum(
                    "hqk,khd->hqd",
                    weights.astype(jnp.bfloat16),
                    v_block_rows,
                    preferred_element_type=jnp.float32,
                )
                new_acc = slice_rows(row_acc, q_start, span, 1) * keep_part[..., None] + added
                return (
                    put_rows(row_max, new_max, q_start, 1),
                    put_rows(row_sum, new_sum, q_start, 1),
                    put_rows(row_acc, new_acc, q_start, 1),
                )

            def forward_unchanged(inner_state):
                return inner_state

            is_live = block_live(piece_labels, piece_index, key_size, q_block, k_block)
            return (lax.cond(is_live, update, forward_unchanged, current), None)

        result, _ = lax.scan(forward_pair_step, running, (q_list, k_list))
        return result

    forward_init = (
        jnp.full((head_count, span), FLOOR_INIT, jnp.float32),
        jnp.zeros((head_count, span), jnp.float32),
        jnp.zeros((head_count, span, HD), jnp.float32),
    )
    row_max, row_sum, row_acc = over_keys(forward_piece, forward_init)
    log_total = row_max + jnp.log(row_sum)
    attention_raw = jnp.transpose(row_acc / row_sum[..., None], (1, 0, 2)).reshape(span, head_cols)
    attended = attention_raw.astype(jnp.bfloat16)
    joined = jnp.concatenate(
        (
            lax.all_gather(attended, "row", axis=0, tiled=True),
            lax.all_gather(activated, "row", axis=0, tiled=True),
        ),
        1,
    )
    second_weights = jnp.concatenate([w_out, w_down], 0)
    partial_out = lax.psum_scatter(
        jnp.dot(
            slice_rows(joined, jnp.int32(0), lax.axis_size("col") * local_rows),
            second_weights,
            preferred_element_type=jnp.float32,
        ).astype(jnp.bfloat16),
        "col",
        scatter_dimension=0,
        tiled=True,
    ).astype(jnp.float32)
    layer_out = (float_in + partial_out + out_bias.astype(jnp.float32)).astype(jnp.bfloat16)
    grad_full = lax.all_gather(cotangent, "col", axis=0, tiled=True)
    grad_out_bias = jnp.sum(grad_full, 0, dtype=jnp.float32)
    grad_second = lax.dot_general(
        joined, grad_full, (((0,), (0,)), ((), ())), preferred_element_type=jnp.float32
    )
    branch_back = lax.psum_scatter(
        lax.dot_general(
            slice_rows(grad_full, jnp.int32(0), lax.axis_size("row") * span),
            second_weights,
            (((1,), (1,)), ((), ())),
            preferred_element_type=jnp.float32,
        ).astype(jnp.bfloat16),
        "row",
        scatter_dimension=0,
        tiled=True,
    ).astype(jnp.float32)
    d_attended = branch_back[:, :head_cols].astype(jnp.bfloat16)
    d_activated = branch_back[:, head_cols:]
    _, gelu_back = jax.vjp(lambda tensor_in: jax.nn.gelu(tensor_in, approximate=False), up_lin)
    d_up = gelu_back(d_activated)[0].astype(jnp.bfloat16)
    d_out_heads = d_attended.reshape(span, head_count, HD)
    row_delta = jnp.transpose(
        jnp.sum((d_attended.astype(jnp.float32) * attention_raw).reshape(span, head_count, HD), -1)
    )

    def backward_piece(running, pieces, first_row):
        d_query_acc, d_key_all, d_value_all = running
        row_count, key_size, piece_labels, piece_index = key_setup(pieces, first_row)
        q_list, k_list = block_pairs(query_blocks, row_count // key_size)
        zero_keys = jnp.zeros((row_count, head_count, HD), jnp.float32)

        def backward_pair_step(current, pair_ids):
            q_block, k_block = pair_ids

            def update(inner_state):
                d_query_run, d_key_run, d_value_run = inner_state
                q_start, k_start, scores, q_block_rows, k_block_rows, v_block_rows = block_scores(
                    pieces, piece_labels, piece_index, key_size, q_block, k_block
                )
                probs_full = jnp.exp(scores - slice_rows(log_total, q_start, span, 1)[..., None])
                d_out_block = slice_rows(d_out_heads, q_start, span)
                d_probs = jnp.einsum(
                    "qhd,khd->hqk", d_out_block, v_block_rows, preferred_element_type=jnp.float32
                )
                d_scores = (
                    probs_full * (d_probs - slice_rows(row_delta, q_start, span, 1)[..., None])
                ).astype(jnp.bfloat16)
                q_added = (
                    jnp.einsum(
                        "hqk,khd->qhd", d_scores, k_block_rows, preferred_element_type=jnp.float32
                    )
                    * score_scale
                )
                k_added = (
                    jnp.einsum(
                        "hqk,qhd->khd", d_scores, q_block_rows, preferred_element_type=jnp.float32
                    )
                    * score_scale
                )
                v_added = jnp.einsum(
                    "hqk,qhd->khd",
                    probs_full.astype(jnp.bfloat16),
                    d_out_block,
                    preferred_element_type=jnp.float32,
                )
                return (
                    put_rows(
                        d_query_run, slice_rows(d_query_run, q_start, span) + q_added, q_start
                    ),
                    put_rows(
                        d_key_run, slice_rows(d_key_run, k_start, key_size) + k_added, k_start
                    ),
                    put_rows(
                        d_value_run, slice_rows(d_value_run, k_start, key_size) + v_added, k_start
                    ),
                )

            def backward_unchanged(inner_state):
                return inner_state

            is_live = block_live(piece_labels, piece_index, key_size, q_block, k_block)
            return (lax.cond(is_live, update, backward_unchanged, current), None)

        scanned, _ = lax.scan(
            backward_pair_step, (d_query_acc, zero_keys, zero_keys), (q_list, k_list)
        )
        d_query_acc, key_part, value_part = scanned
        d_key_all = put_rows(d_key_all, key_part, first_row)
        d_value_all = put_rows(d_value_all, value_part, first_row)
        return (d_query_acc, d_key_all, d_value_all)

    backward_init = (
        jnp.zeros((span, head_count, HD), jnp.float32),
        jnp.zeros((all_rows, head_count, HD), jnp.float32),
        jnp.zeros((all_rows, head_count, HD), jnp.float32),
    )
    d_query_rot, d_key_total, d_value_total = over_keys(backward_piece, backward_init)
    d_key_rot, d_value_mine = (
        lax.psum_scatter(
            d_key_total.reshape(all_rows, head_cols).astype(jnp.bfloat16),
            "row",
            scatter_dimension=0,
            tiled=True,
        ).astype(jnp.float32),
        lax.psum_scatter(
            d_value_total.reshape(all_rows, head_cols).astype(jnp.bfloat16),
            "row",
            scatter_dimension=0,
            tiled=True,
        ).astype(jnp.float32),
    )
    _, query_back = jax.vjp(rotate_mine, query_lin)
    _, key_back = jax.vjp(rotate_mine, key_lin)
    d_query_lin = query_back(d_query_rot)[0].reshape(span, head_cols).astype(jnp.bfloat16)
    d_key_lin = (
        key_back(d_key_rot.reshape(span, head_count, HD))[0]
        .reshape(span, head_cols)
        .astype(jnp.bfloat16)
    )
    d_first = jnp.concatenate([d_query_lin, d_key_lin, d_value_mine.astype(jnp.bfloat16), d_up], 1)
    d_first_full = lax.all_gather(d_first, "row", axis=0, tiled=True)
    grad_first_bias = jnp.sum(d_first_full, 0, dtype=jnp.float32)
    grad_first = lax.dot_general(
        gathered_hidden, d_first_full, (((0,), (0,)), ((), ())), preferred_element_type=jnp.float32
    )
    d_normed = lax.psum_scatter(
        lax.dot_general(
            slice_rows(d_first_full, jnp.int32(0), lax.axis_size("col") * local_rows),
            first_weights,
            (((1,), (1,)), ((), ())),
            preferred_element_type=jnp.float32,
        ).astype(jnp.bfloat16),
        "col",
        scatter_dimension=0,
        tiled=True,
    ).astype(jnp.float32)
    d_centred = d_normed * ln_gain.astype(jnp.float32)
    grad_stats = lax.psum((jnp.sum(d_centred, 1), jnp.sum(d_centred * centred, 1)), "row")
    grad_inputs = inv_std[:, None] * (
        d_centred - grad_stats[0][:, None] / D - centred * grad_stats[1][:, None] / D
    ) + cotangent.astype(jnp.float32)
    summed = (
        lax.psum(grad_first.astype(jnp.bfloat16), "dp").astype(jnp.float32),
        lax.psum(grad_second.astype(jnp.bfloat16), "dp").astype(jnp.float32),
        lax.psum(grad_first_bias.astype(jnp.bfloat16), "dp").astype(jnp.float32),
        lax.psum(grad_out_bias.astype(jnp.bfloat16), "dp").astype(jnp.float32),
    )
    norm_grads = lax.psum((jnp.sum(d_normed * centred, 0), jnp.sum(d_normed, 0)), ("dp", "col"))
    grad_w_qkv = summed[0][:, : 3 * head_cols].reshape(feature_cols, 3, head_cols)
    grad_w_up = summed[0][:, 3 * head_cols :]
    grad_w_out = summed[1][:head_cols]
    grad_w_down = summed[1][head_cols:]
    grad_b_qkv = summed[2][: 3 * head_cols].reshape(3, head_cols)
    grad_b_up = summed[2][3 * head_cols :]
    return (
        layer_out,
        grad_inputs,
        norm_grads[0],
        norm_grads[1],
        grad_w_qkv,
        grad_b_qkv,
        grad_w_out,
        grad_w_up,
        grad_b_up,
        grad_w_down,
        summed[3],
    )


def solution(mesh):
    placed = (
        P(("dp", "col"), "row"),
        P("dp", None),
        P("row"),
        P("row"),
        P("row", None, "col"),
        P(None, "col"),
        P("col", "row"),
        P("row", "col"),
        P("col"),
        P("col", "row"),
        P("row"),
        P(("dp", "col"), "row"),
    )
    size = dict(mesh.shape)
    sliced = (size["dp"], size["row"], size["col"]) == (4, 4, 2)
    return jax.shard_map(
        per_device_sliced if sliced else per_device_general,
        mesh=mesh,
        in_specs=placed,
        out_specs=(
            P(("dp", "col"), "row"),
            P(("dp", "col"), "row"),
            P("row"),
            P("row"),
            P("row", None, "col"),
            P(None, "col"),
            P("col", "row"),
            P("row", "col"),
            P("col"),
            P("col", "row"),
            P("row"),
        ),
        check_vma=False,
    )
```

```python
import math

import jax
import jax.numpy as jnp
from jax import lax
from jax.experimental import pallas as pl
from jax.experimental.pallas import tpu as pltpu
from jax.sharding import PartitionSpec as P

D = 1024
HD = 64
ROT = 16
SEQ_LEN = 2048
EPSILON = 1e-05
MASKED = -1000000000.0
BF = jnp.bfloat16
F32 = jnp.float32
NT = (((1,), (1,)), ((), ()))
NN = (((1,), (0,)), ((), ()))
TN = (((0,), (0,)), ((), ()))


def dot(a, b, dims=NN):
    return lax.dot_general(a, b, dims, preferred_element_type=F32)


BK = 512


def lane_mask(head, rows):
    lane = lax.broadcasted_iota(jnp.int32, (rows, 128), 1)
    return (lane >= head * HD) & (lane < (head + 1) * HD)


MESH = pl.DeviceIdType.MESH
TC = 256
BT = 512
HT = BT // 2


def vmem():
    return pl.BlockSpec(memory_space=pltpu.VMEM)


def hbm():
    return pl.BlockSpec(memory_space=pl.ANY)


def span(first, count):
    if not isinstance(first, int):
        first = pl.multiple_of(first, count & -count)
    return pl.ds(first, count)


def remote(src, dst, send, recv, dev):
    return pltpu.make_async_remote_copy(
        src_ref=src, dst_ref=dst, send_sem=send, recv_sem=recv, device_id=dev, device_id_type=MESH
    )


def landed(ref, sem):
    pltpu.make_async_copy(ref, ref, sem).wait()


def left(ref, sem):
    pltpu.make_async_copy(ref, ref, sem).wait()


def where():
    return lax.axis_index("dp"), lax.axis_index("row"), lax.axis_index("col")


def greet(dp, row, col):
    bar = pltpu.get_barrier_semaphore()
    for d in range(1, 4):
        pl.semaphore_signal(bar, inc=1, device_id=(dp ^ d, row, col), device_id_type=MESH)
        pl.semaphore_signal(bar, inc=1, device_id=(dp, lax.rem(row + d, 4), col), device_id_type=MESH)
    pl.semaphore_signal(bar, inc=1, device_id=(dp, row, 1 - col), device_id_type=MESH)
    pl.semaphore_wait(bar, 7)


def dmas(*shapes):
    return [pltpu.SemaphoreType.DMA(s) for s in shapes]


class LineGather:
    SEMS = ((4, 4),) * 4 + ((7, 4),) * 2 + ((1,),)

    def __init__(self, own, full, sems, pos):
        self.own, self.full, self.pos = own, full, pos
        self.su, self.sd, self.ru, self.rd, self.ss, self.rs, self.loc = sems

    def at(self, block, t, other=False):
        dp, row, col = self.pos
        return self.full.at[block, span(t * BT + (1 - col if other else col) * HT, HT)]

    def up(self, step, t):
        dp, row, col = self.pos
        ref = self.at(row - step, t)
        return remote(ref, ref, self.su.at[step, t], self.ru.at[step, t], (dp, row + 1, col))

    def down(self, step, t):
        dp, row, col = self.pos
        ref = self.at(row + step, t)
        return remote(ref, ref, self.sd.at[step, t], self.rd.at[step, t], (dp, row - 1, col))

    def sib(self, step, sign, t):
        dp, row, col = self.pos
        i = step + 3 * (sign < 0)
        ref = self.at(row - sign * step, t)
        return remote(ref, ref, self.ss.at[i, t], self.rs.at[i, t], (dp, row, 1 - col))

    def half_at(self, k, other=False):
        dp, row, col = self.pos
        return self.full.at[row, span((1 - col if other else col) * 2 * BT + k * BT, BT)]

    def give(self, k):
        dp, row, col = self.pos
        return remote(
            self.own.at[pl.ds(k * BT, BT)], self.half_at(k), self.ss.at[0, k], self.rs.at[0, k], (dp, row, 1 - col)
        )

    def local(self):
        dp, row, col = self.pos
        return pltpu.make_async_copy(self.own, self.full.at[row, span(col * 2 * BT, 2 * BT)], self.loc.at[0])

    def start(self, order):
        for k in order:
            self.give(k).start()
        self.local().start()

    def send_own(self, t):
        dp, row, col = self.pos

        @pl.when(col != t // 2)
        def _():
            landed(self.half_at(t % 2, True), self.rs.at[0, t % 2])

        @pl.when(row < 3)
        def _():
            self.up(0, t).start()

        @pl.when(row > 0)
        def _():
            self.down(0, t).start()

    def step(self, s, t):
        dp, row, col = self.pos

        @pl.when(row >= s)
        def _():
            landed(self.at(row - s, t), self.ru.at[s - 1, t])

            @pl.when(row < 3)
            def _():
                self.up(s, t).start()

            self.sib(s, 1, t).start()

        @pl.when(row + s <= 3)
        def _():
            landed(self.at(row + s, t), self.rd.at[s - 1, t])

            @pl.when(row > 0)
            def _():
                self.down(s, t).start()

            self.sib(s, -1, t).start()

    def ready(self, t):
        dp, row, col = self.pos
        for s in range(1, 4):
            @pl.when(row >= s)
            def _():
                landed(self.at(row - s, t, True), self.rs.at[s, t])

            @pl.when(row + s <= 3)
            def _():
                landed(self.at(row + s, t, True), self.rs.at[s + 3, t])

    def drain(self):
        dp, row, col = self.pos
        for k in range(2):
            self.give(k).wait_send()
        for t in range(4):
            for s in range(0, 3):
                @pl.when((row >= s) & (row < 3))
                def _():
                    self.up(s, t).wait_send()

                @pl.when((row + s <= 3) & (row > 0))
                def _():
                    self.down(s, t).wait_send()
            for s in range(1, 4):
                @pl.when(row >= s)
                def _():
                    self.sib(s, 1, t).wait_send()

                @pl.when(row + s <= 3)
                def _():
                    self.sib(s, -1, t).wait_send()


class WeightGather:
    SEMS = ((4,), (4,), (4, 4), (4, 4), (4,))

    def __init__(self, full, pieces, sems, pos):
        self.full, self.pieces, self.pos = full, pieces, pos
        self.sz, self.rz, self.sp, self.rp, self.loc = sems
        self.quarter = full.shape[1] // 4

    def parts(self, block, q):
        seen = []
        for src, r0, rows, c0, cols, d0, e0 in self.pieces(0):
            seen.append((d0, rows))
        out = []
        for d0, rows in dict.fromkeys(seen):
            out.append(self.full.at[block, span(d0 + q * (rows // 4), rows // 4)])
        return out

    def bytes(self):
        return self.full.at[0, pl.ds(0, self.quarter)]

    def along(self, d):
        dp, row, col = self.pos
        target = lax.rem(row + d, 4)
        copies = []
        for src, r0, rows, c0, cols, d0, e0 in self.pieces(target):
            q = rows // 4
            copies.append(remote(
                src.at[span(r0 + dp * q, q), span(c0, cols)],
                self.full.at[row, span(d0 + dp * q, q), pl.ds(e0, cols)],
                self.sz.at[d], self.rz.at[d], (dp, target, col),
            ))
        return copies

    def across(self, d, e):
        dp, row, col = self.pos
        block = lax.rem(row + 4 - d, 4)
        return [
            remote(p, p, self.sp.at[d, e], self.rp.at[d, e], (dp ^ e, row, col)) for p in self.parts(block, dp)
        ]

    def local(self):
        dp, row, col = self.pos
        return [
            pltpu.make_async_copy(
                src.at[span(r0, rows), span(c0, cols)],
                self.full.at[row, pl.ds(d0, rows), pl.ds(e0, cols)], self.loc.at[i],
            )
            for i, (src, r0, rows, c0, cols, d0, e0) in enumerate(self.pieces(row))
        ]

    def start(self):
        for d in (2, 1, 3):
            for c in self.along(d):
                c.start()
        for c in self.local():
            c.start()

    def forward(self):
        for d in (1, 3, 2):
            landed(self.bytes(), self.rz.at[d])
            for e in (3, 1, 2):
                for c in self.across(d, e):
                    c.start()

    def arrived(self):
        for c in self.local():
            c.wait()
        for d in (1, 3, 2):
            for e in (1, 2, 3):
                landed(self.bytes(), self.rp.at[d, e])

    def drain(self):
        for d in (1, 2, 3):
            left(self.bytes(), self.sz.at[d])
            for e in (1, 2, 3):
                left(self.bytes(), self.sp.at[d, e])


class LineReduce:
    SEMS = ((4, 4),) * 3 + ((5, 4),)

    def __init__(self, own, sib, line, sems, pos):
        self.own, self.sib_in, self.line_in = own, sib, line
        self.s_sib, self.r_sib, self.s_line, self.r_line = sems
        self.pos = pos

    def sib(self, stage, b, t):
        dp, row, col = self.pos
        return remote(
            stage.at[t % 2, b], self.sib_in.at[b, t], self.s_sib.at[b, t], self.r_sib.at[b, t], (dp, row, 1 - col)
        )

    def up(self, b, t):
        dp, row, col = self.pos
        return remote(
            self.own.at[b, t], self.line_in.at[b, t], self.s_line.at[b, t], self.r_line.at[b, t], (dp, row + 1, col)
        )

    def down(self, b, t):
        dp, row, col = self.pos
        slot = jnp.where(b == row - 1, 4, b)
        return remote(
            self.own.at[b, t], self.line_in.at[slot, t], self.s_line.at[b, t], self.r_line.at[slot, t],
            (dp, row - 1, col),
        )

    def produce(self, t, stage, rows, fn):
        dp, row, col = self.pos

        there = rows(span(t * BT + (1 - col) * HT, HT))
        for b in (3, 0, 2, 1):
            stage[t % 2, b] = fn(there, b).astype(BF)
            self.sib(stage, b, t).start()
        here = rows(span(t * BT + col * HT, HT))
        for b in (3, 0, 2, 1):
            self.own[b, t] = fn(here, b).astype(BF)

    def wait_stage(self, t, stage):
        for b in range(4):
            self.sib(stage, b, t).wait_send()

    def hop(self, b, t, take):
        dp, row, col = self.pos
        landed(self.sib_in.at[b, t], self.r_sib.at[b, t])
        total = self.own[b, t].astype(F32) + self.sib_in[b, t].astype(F32)
        if take:
            landed(self.line_in.at[b, t], self.r_line.at[b, t])
            total = total + self.line_in[b, t].astype(F32)
        self.own[b, t] = total.astype(BF)

        @pl.when(row < b)
        def _():
            self.up(b, t).start()

        @pl.when(row > b)
        def _():
            self.down(b, t).start()

    def edge(self, t):
        dp, row, col = self.pos

        @pl.when((row == 0) | (row == 3))
        def _():
            for i in range(3):
                self.hop(jnp.where(row == 0, 3 - i, i), t, False)

    def slot(self, t, j):
        dp, row, col = self.pos

        @pl.when((row == 1) | (row == 2))
        def _():
            self.hop(jnp.where(row == 1, 3 - j, j), t, True)
            if j == 1:
                self.hop(jnp.where(row == 1, 0, 3), t, True)

    def final(self, t, total):
        dp, row, col = self.pos
        landed(self.sib_in.at[row, t], self.r_sib.at[row, t])
        total[...] = self.own[row, t].astype(F32) + self.sib_in[row, t].astype(F32)

        @pl.when(row > 0)
        def _():
            landed(self.line_in.at[row, t], self.r_line.at[row, t])
            total[...] += self.line_in[row, t].astype(F32)

        @pl.when(row < 3)
        def _():
            landed(self.line_in.at[4, t], self.r_line.at[4, t])
            total[...] += self.line_in[4, t].astype(F32)

    def drain(self):
        dp, row, col = self.pos
        for b in range(4):
            for t in range(4):
                @pl.when(row < b)
                def _():
                    self.up(b, t).wait_send()

                @pl.when(row > b)
                def _():
                    self.down(b, t).wait_send()


class GradReduce:
    SEMS = ((4,), (4,), (2,), (2,), (4,), (4,), (2,), (2,), (4,), (4,))

    def __init__(self, grad, near, far, mid, part, place, shared, sems, pos):
        self.grad, self.near, self.far, self.mid, self.part = grad, near, far, mid, part
        self.place, self.shared = place, shared
        self.s1, self.r1, self.sm, self.rm, self.s2, self.r2, self.s3, self.r3, self.s4, self.r4 = sems
        self.pos = pos
        self.rows = grad.shape[1] // 4
        self.n = self.rows // 2

    def cut(self, q, h):
        return self.grad.at[:, span(q * self.rows + h * self.n, self.n)]

    def peer(self, e):
        dp, row, col = self.pos
        return (dp ^ e, row, col)

    def first(self, i):
        dp, row, col = self.pos
        e = 1 + i // 2
        q = dp ^ (3 if i % 2 else e)
        return remote(self.cut(q, i // 2), self.near.at[i], self.s1.at[i], self.r1.at[i], self.peer(e))

    def middle(self, h):
        return remote(self.mid.at[h], self.far.at[h], self.sm.at[h], self.rm.at[h], self.peer(2 - h))

    def second(self, d):
        dp, row, col = self.pos
        target = lax.rem(row + d, 4)
        return [
            remote(
                self.part.at[target, :, pl.ds(c0, cols)], dst, self.s2.at[d], self.r2.at[d], (dp, target, col)
            )
            for dst, c0, cols in self.place(row, dp)
        ]

    def third(self, h):
        dp, row, col = self.pos
        ref = self.shared(dp, h)
        return remote(ref, ref, self.s3.at[h], self.r3.at[h], self.peer(2 - h))

    def fourth(self, i):
        dp, row, col = self.pos
        h = i // 2
        ref = self.shared(dp ^ (2 - h) if i % 2 else dp, h)
        return remote(ref, ref, self.s4.at[i], self.r4.at[i], self.peer(1 + h))

    def start(self):
        for i in (1, 3, 0, 2):
            self.first(i).start()

    def middle_sum(self):
        dp, row, col = self.pos
        for h in range(2):
            i = 2 * h + 1
            landed(self.near.at[i], self.r1.at[i])
            self.mid[h] = (self.cut(dp ^ (2 - h), h)[...].astype(F32) + self.near[i].astype(F32)).astype(BF)
            self.middle(h).start()

    def own(self):
        dp, row, col = self.pos
        return [
            pltpu.make_async_copy(self.part.at[row, :, pl.ds(c0, cols)], dst, self.s2.at[0])
            for dst, c0, cols in self.place(row, dp)
        ]

    def sum_and_spread(self):
        dp, row, col = self.pos
        for h in range(2):
            landed(self.near.at[2 * h], self.r1.at[2 * h])
            landed(self.far.at[h], self.rm.at[h])
        for d in (2, 1, 3, 0):
            b = lax.rem(row + d, 4)
            for h in range(2):
                total = self.grad.at[b, span(dp * self.rows + h * self.n, self.n)][...].astype(F32)
                total = total + self.near[2 * h, b].astype(F32) + self.far[h, b].astype(F32)
                self.part[b, h * self.n : (h + 1) * self.n, :] = total.astype(BF)
            for c in self.own() if d == 0 else self.second(d):
                c.start()

    def share(self):
        pltpu.make_async_copy(self.part.at[0], self.part.at[0], self.s2.at[0]).wait()
        for d in (1, 2, 3):
            landed(self.part.at[0], self.r2.at[d])
        self.third(0).start()
        self.third(1).start()
        self.fourth(0).start()
        self.fourth(2).start()

    def relay(self):
        dp, row, col = self.pos
        for h in range(2):
            landed(self.shared(dp, h), self.r3.at[h])
            self.fourth(2 * h + 1).start()

    def finish(self):
        dp, row, col = self.pos
        for i in range(4):
            landed(self.shared(dp, i // 2), self.r4.at[i])
            self.first(i).wait_send()
            self.fourth(i).wait_send()
        for h in range(2):
            self.middle(h).wait_send()
            self.third(h).wait_send()
        for d in (1, 2, 3):
            left(self.part.at[0], self.s2.at[d])


def unrope(gt, cosv, sinv):
    rows = []
    for h in range(2):
        o = h * HD
        a, b = gt[o : o + 8], gt[o + 8 : o + 16]
        rows += [a * cosv + b * sinv, b * cosv - a * sinv, gt[o + 16 : o + HD]]
    return jnp.concatenate(rows, 0)


def layer_kernel(
    x, cot, wq, wu, wo, wd, seg, vec,
    out_o, gin_o, small_o, cols_o, fq_o, fu_o, fo_o, fd_o,
    xf, nrm, cf, w1, w2, q_v, k_v, v_v, tr_v, att_v, da, act_v, gp_v, raw, dqt, dka, dva,
    stat, lse, delta, cs, rng, gbs, d1,
    own_a, sib_a, line_a, own_b, sib_b, line_b, stage, total,
    gq, nq, rq, mq, tq, gu, nu, ru, mu, tu, go, no, ro, mo, to, gd, nd, rd, md, td,
    out_v, gin_v, send_st, st, sums, sums_in, small, small_sib, small_in,
    *sems,
):
    pos = where()
    dp, row, col = pos
    toks = seg.shape[1]
    half = toks // 2
    hc = wq.shape[2] // 4
    fc = wu.shape[1] // 4
    h3 = 3 * hc
    depth = wq.shape[1]
    scale = 1.0 / math.sqrt(HD)
    taken = [0]

    def take(cls):
        first = taken[0]
        taken[0] = first + len(cls.SEMS)
        return sems[first : taken[0]]

    X = LineGather(x, xf, take(LineGather), pos)
    C = LineGather(cot, cf, take(LineGather), pos)

    def pieces1(t):
        return [(wq.at[j], 0, depth, t * hc, hc, 0, j * hc) for j in range(3)]

    def pieces3(t):
        return [(wu, 0, depth, t * fc, fc, 0, 0)]

    def pieces2(t):
        return [(wo, t * hc, hc, 0, depth, 0, 0), (wd, t * fc, fc, 0, depth, hc, 0)]

    W1 = WeightGather(w1.at[:, :, pl.ds(0, h3)], pieces1, take(WeightGather), pos)
    W3 = WeightGather(w1.at[:, :, pl.ds(h3, fc)], pieces3, take(WeightGather), pos)
    W2 = WeightGather(w2, pieces2, take(WeightGather), pos)
    A = LineReduce(own_a, sib_a, line_a, take(LineReduce), pos)
    B = LineReduce(own_b, sib_b, line_b, take(LineReduce), pos)

    def rows_of(q):
        return span(q * (depth // 4), depth // 4)

    def rows_half(q, h):
        return span(q * (depth // 4) + h * (depth // 8), depth // 8)

    def place_q(s, q):
        return [(fq_o.at[j, rows_of(q), span(s * hc, hc)], j * hc, hc) for j in range(3)]

    def place_u(s, q):
        return [(fu_o.at[rows_of(q), span(s * fc, fc)], 0, fc)]

    def tall(ref):
        n = ref.shape[1] // 4
        return lambda s, q: [(ref.at[s, span(q * n, n)], 0, depth)]

    def tall_share(ref):
        n = ref.shape[1] // 4
        return lambda q, h: ref.at[:, span(q * n + h * (n // 2), n // 2)]

    GQ = GradReduce(gq, nq, rq, mq, tq, place_q, lambda q, h: fq_o.at[:, rows_half(q, h)], take(GradReduce), pos)
    GU = GradReduce(gu, nu, ru, mu, tu, place_u, lambda q, h: fu_o.at[rows_half(q, h)], take(GradReduce), pos)
    GO = GradReduce(go, no, ro, mo, to, tall(fo_o), tall_share(fo_o), take(GradReduce), pos)
    GD = GradReduce(gd, nd, rd, md, td, tall(fd_o), tall_share(fd_o), take(GradReduce), pos)
    gs, gr, misc, s_st, r_st, s_sum, r_sum, s_row, r_row, s_small, r_small, s_own, r_own = sems[taken[0] :]

    greet(dp, row, col)
    X.start((0, 1))
    at_gain = h3 * 4 + fc * 4
    gbs[pl.ds(row, 1)] = jnp.zeros((1, 8, depth), F32)
    gbs[pl.ds(row, 1), 0:1, :] = vec[0:1, at_gain : at_gain + depth][None]
    gbs[pl.ds(row, 1), 1:2, :] = vec[0:1, at_gain + depth : at_gain + 2 * depth][None]

    def gain_copy(d):
        return remote(gbs.at[row], gbs.at[row], gs.at[d], gr.at[d], (dp, lax.rem(row + d, 4), col))

    for d in (1, 2, 3):
        gain_copy(d).start()
    X.local().wait()

    bias = jnp.concatenate(
        [vec[0:1, span((4 * j + row) * hc, hc)] for j in range(3)] + [vec[0:1, span(12 * hc + row * fc, fc)]], 1
    )
    weights = w1.reshape(w1.shape[0] * w1.shape[1], w1.shape[2])

    def project(t):
        def token_step(i, _):
            at = span(t * BT + i * TC, TC)
            blocks = [xf[b, at, :].astype(F32) for b in range(4)]
            one = (blocks[0] + blocks[1]) + (blocks[2] + blocks[3])
            two = (blocks[0] * blocks[0] + blocks[1] * blocks[1]) + (
                blocks[2] * blocks[2] + blocks[3] * blocks[3]
            )
            mean = jnp.sum(one, 1, keepdims=True) * (1.0 / D)
            var = jnp.sum(two, 1, keepdims=True) * (1.0 / D) - mean * mean
            inv = lax.rsqrt(var + EPSILON)
            lane = lax.broadcasted_iota(jnp.int32, (TC, 128), 1)
            stat[at, :] = jnp.where(lane == 0, mean, inv)
            parts = []
            for b in range(4):
                n = ((blocks[b] - mean) * inv * gbs[b, 0:1, :] + gbs[b, 1:2, :]).astype(BF)
                nrm[b, at, :] = n
                parts.append(n)
            acc = dot(jnp.concatenate(parts, 1), weights[:, 0:h3]) + bias[:, 0:h3]
            cosv, sinv = cs[0:8, at], cs[8:16, at]
            q_v[at, :] = unrope(acc[:, 0:128].T, cosv, -sinv).T.astype(BF)
            k_v[at, :] = unrope(acc[:, 128:256].T, cosv, -sinv).T.astype(BF)
            v_v[at, :] = acc[:, 256:384].astype(BF)
            tr_v[:, at] = acc[:, 256:384].T.astype(BF)
            return 0

        lax.fori_loop(0, BT // TC, token_step, 0)

    def hidden(t):
        def token_step(i, _):
            at = span(t * BT + i * TC, TC)
            rows = jnp.concatenate([nrm[b, at, :] for b in range(4)], 1)
            up = dot(rows, weights[:, h3:]) + bias[:, h3:]
            phi = 0.5 * (1.0 + lax.erf(up * (1.0 / math.sqrt(2.0))))
            act_v[at, :] = (up * phi).astype(BF)
            gp_v[at, :] = (phi + up * jnp.exp(-0.5 * up * up) * (1.0 / math.sqrt(2.0 * math.pi))).astype(BF)
            return 0

        lax.fori_loop(0, BT // TC, token_step, 0)

    def allowed(k0, at, diagonal):
        kidx = lax.broadcasted_iota(jnp.int32, (BK, BT), 0)
        if not diagonal:
            return kidx >= rng[0:1, at] - k0
        kidx = kidx + k0 - rng[0:1, at]
        return (kidx >= 0) & (kidx <= rng[1:2, at])

    def attend(t):
        at = pl.ds(t * BT, BT)
        qs = q_v[at, :] * BF(scale)
        heads = [jnp.where(lane_mask(h, BT), qs, BF(0)) for h in range(2)]

        def k_step(kb, carry, diagonal=False):
            k0 = kb * BK if diagonal else pl.multiple_of(kb * BK, BK)
            kk = k_v[pl.ds(k0, BK), :]
            ok = allowed(k0, at, diagonal)
            new = []
            for h in range(2):
                m, l, acc = carry[h]
                s = jnp.where(ok, dot(kk, heads[h], NT), MASKED)
                m2 = jnp.maximum(m, jnp.max(s, 0, keepdims=True))
                p = jnp.exp(s - m2)
                c = jnp.exp(m - m2)
                l = l * c + jnp.sum(p, 0, keepdims=True)
                vt = tr_v[h * HD : (h + 1) * HD, pl.ds(k0, BK)]
                acc = acc * c + dot(vt, p.astype(BF))
                new.append((m2, l, acc))
            return tuple(new)

        init = tuple(
            (jnp.full((1, BT), -1e30, F32), jnp.zeros((1, BT), F32), jnp.zeros((HD, BT), F32))
            for _ in range(2)
        )
        res = lax.fori_loop(0, t, k_step, init) if t else init
        res = k_step(t, res, True)
        for h in range(2):
            m, l, acc = res[h]
            raw[h * HD : (h + 1) * HD, at] = acc / l
            lse[h : h + 1, at] = m + jnp.log(l)
        att_v[at, :] = raw[:, at].T.astype(BF)

    def out_part(t):
        def rows(at):
            return jnp.concatenate([att_v[at, :], act_v[at, :]], 1)

        if t >= 2:
            A.wait_stage(t - 2, stage)
        A.produce(t, stage, rows, lambda joined, b: dot(joined, w2[b]))

    def joined_back(t):
        def chunk(i, _):
            at = span(t * BT + i * TC, TC)
            dj = dot(
                jnp.concatenate([cf[b, at, :] for b in range(4)], 1),
                jnp.concatenate([w2[b] for b in range(4)], 1),
                NT,
            )
            d_att = dj[:, 0:128].astype(BF)
            da[at, :] = d_att
            d1[at, 384:] = (dj[:, 128:] * gp_v[at, :].astype(F32)).astype(BF)
            prod = d_att.astype(F32).T * raw[:, at]
            for h in range(2):
                delta[h : h + 1, at] = jnp.sum(prod[h * HD : (h + 1) * HD], 0, keepdims=True)
            return 0

        lax.fori_loop(0, BT // TC, chunk, 0)

    def attend_back(t, lo, hi):
        at = pl.ds(t * BT, BT)
        qs = q_v[at, :] * BF(scale)
        do = da[at, :]
        qh = [jnp.where(lane_mask(h, BT), qs, BF(0)) for h in range(2)]
        doh = [jnp.where(lane_mask(h, BT), do, BF(0)) for h in range(2)]
        if lo == 0:
            dqt[...] = jnp.zeros_like(dqt)

        for kb in range(lo * 256 // BK, hi * 256 // BK):
            k0 = kb * BK
            ka = pl.ds(k0, BK)
            kk = k_v[ka, :]
            vv = v_v[ka, :]
            ok = allowed(k0, at, kb == t)
            dk, dv = dka[ka, :], dva[ka, :]
            for h in range(2):
                s = jnp.where(ok, dot(kk, qh[h], NT), MASKED)
                p = jnp.exp(s - lse[h : h + 1, at])
                ds = (p * (dot(vv, doh[h], NT) - delta[h : h + 1, at])).astype(BF)
                dv = dv + dot(p.astype(BF), doh[h])
                dk = dk + dot(ds, qh[h])
                rows = slice(h * HD, (h + 1) * HD)
                dqt[rows, :] += dot(tr_v[rows, ka], ds)
            dka[ka, :] = dk
            dva[ka, :] = dv

    def finish_back(t):
        at = pl.ds(t * BT, BT)
        cosv, sinv = cs[0:8, at], cs[8:16, at]
        d1[at, 0:128] = unrope(dqt[...] * scale, cosv, sinv).T.astype(BF)
        d1[at, 128:256] = unrope(dka[at, :].T, cosv, sinv).T.astype(BF)
        d1[at, 256:384] = dva[at, :].astype(BF)

    def norm_part(t):
        (A if t >= 2 else B).wait_stage(t if t >= 2 else t + 2, stage)
        B.produce(t, stage, lambda at: d1[at, :], lambda rows, b: dot(rows, w1[b], NT))

    def gains():
        for d in (1, 2, 3):
            landed(gbs.at[0], gr.at[d])

    def prep():
        labels = seg[...]
        start = jnp.zeros_like(labels)
        for d in range(1, 8):
            below = jnp.sum((labels == d - 1).astype(F32), 1, keepdims=True).astype(jnp.int32)
            start = start + jnp.where(labels >= d, below, 0)
        index = lax.broadcasted_iota(jnp.int32, labels.shape, 1)
        place = index - start
        rng[0:1, :] = start
        rng[1:2, :] = place
        power = lax.broadcasted_iota(jnp.int32, (8, 1), 0).astype(F32) * (-2.0 * math.log(10000.0) / ROT)
        ang = place.astype(F32) * jnp.exp(power)
        cs[0:8, :] = jnp.cos(ang)
        cs[8:16, :] = jnp.sin(ang)
        dka[...] = jnp.zeros_like(dka)
        dva[...] = jnp.zeros_like(dva)

    def turn():
        def step(i, _):
            at = span(i * BT, BT)
            tr_v[:, at] = k_v[at, :].astype(F32).T.astype(BF)
            return 0

        lax.fori_loop(0, toks // BT, step, 0)

    def grads2():
        for b in range(4):
            go[b] = dot(att_v[...], cf[b], TN).astype(BF)
            gd[b] = dot(act_v[...], cf[b], TN).astype(BF)

    def gradsu():
        for b in range(4):
            gu[b] = dot(nrm[b], d1[:, 384:], TN).astype(BF)

    def gradsq():
        for b in range(4):
            gq[b] = dot(nrm[b], d1[:, 0:384], TN).astype(BF)

    def sum_copy(e):
        return remote(sums.at[0], sums_in.at[e - 1], s_sum.at[e], r_sum.at[e], (dp ^ e, row, col))

    def row_copy(d):
        return remote(sums.at[1], cols_o.at[row], s_row.at[d], r_row.at[d], (dp, lax.rem(row + d, 4), col))

    own_cols = pltpu.make_async_copy(sums.at[1], cols_o.at[row], misc.at[0])

    def colsum():
        sums[0] = dot(jnp.ones((8, toks), BF), d1[...])
        for e in (3, 1, 2):
            sum_copy(e).start()

    def sums_on():
        for e in (1, 2, 3):
            landed(sums_in.at[e - 1], r_sum.at[e])
        sums[1] = (sums[0] + sums_in[0]) + (sums_in[1] + sums_in[2])
        for d in (1, 2, 3):
            row_copy(d).start()
        own_cols.start()

    at_obias = at_gain + 2 * depth

    def deliver(src, dst, i, t):
        at = span((t % 2) * BT + col * HT, HT)
        here = pltpu.make_async_copy(src.at[t], dst.at[at], s_own.at[i, t])
        there = remote(src.at[t], dst.at[at], s_own.at[i, t], r_own.at[i, t], (dp, row, 1 - col))
        return here, there

    def send_result(src, dst, i, t):
        here, there = deliver(src, dst, i, t)

        @pl.when(col == t // 2)
        def _():
            here.start()

        @pl.when(col != t // 2)
        def _():
            there.start()

    def end_result(src, dst, i, t):
        here, there = deliver(src, dst, i, t)

        @pl.when(col == t // 2)
        def _():
            here.wait()
            landed(dst.at[span((t % 2) * BT + (1 - col) * HT, HT)], r_own.at[i, t])

        @pl.when(col != t // 2)
        def _():
            there.wait_send()

    def mine(t):
        return span(t * BT + col * HT, HT)

    def out_final(t):
        A.final(t, total)
        out_v[t] = (
            xf[row, mine(t), :].astype(F32) + total[...] + vec[0:1, at_obias : at_obias + depth]
        ).astype(BF)
        send_result(out_v, out_o, 0, t)

    def stat_copy(d, k):
        return remote(
            send_st.at[k], st.at[d - 1, k], s_st.at[d, k], r_st.at[d, k], (dp, lax.rem(row + d, 4), col)
        )

    gain = vec[0:1, at_gain : at_gain + depth]
    small[...] = jnp.zeros_like(small)

    def centred(t):
        mean, inv = stat[mine(t), 0:1], stat[mine(t), 1:2]
        return (xf[row, mine(t), :].astype(F32) - mean) * inv, inv, cf[row, mine(t), :].astype(F32)

    def norm_final(t):
        B.final(t, total)
        dn = total[...]
        xh, inv, ct = centred(t)
        dc = dn * gain
        s0 = jnp.sum(dc, 1, keepdims=True)
        s1 = jnp.sum(dc * xh, 1, keepdims=True)
        lane = lax.broadcasted_iota(jnp.int32, (HT, 128), 1)
        send_st[t // 2, :, (t % 2) * HT : (t % 2 + 1) * HT] = jnp.where(
            lane == 0, s0, jnp.where(lane == 1, s1, 0.0)
        ).T[0:8, :]
        if t % 2 == 0:
            for d in (2, 1, 3):
                stat_copy(d, t // 2).start()
        gin_v[t] = dc
        small[0, 0:1, :] += jnp.sum(dn * xh, 0, keepdims=True)
        small[0, 1:2, :] += jnp.sum(dn, 0, keepdims=True)
        small[0, 2:3, :] += jnp.sum(ct, 0, keepdims=True)
        if t == 0:
            sib_small.start()

    sib_small = remote(small.at[0], small_sib, s_small.at[0], r_small.at[0], (dp, row, 1 - col))

    def small_copy(e):
        return remote(small.at[1], small_in.at[e - 1], s_small.at[e], r_small.at[e], (dp ^ e, row, col))

    def small_on():
        landed(small_sib, r_small.at[0])
        small[1] = small[0] + small_sib[...]
        for e in (3, 1, 2):
            small_copy(e).start()

    def grad_final(k):
        acc = send_st[k]
        for d in (1, 2, 3):
            landed(st.at[d - 1, k], r_st.at[d, k])
            acc = acc + st[d - 1, k]
        both = jnp.concatenate([acc, jnp.zeros((120, BT), F32)], 0).T
        for t in (2 * k + 1, 2 * k):
            xh, inv, ct = centred(t)
            r = slice((t % 2) * HT, (t % 2 + 1) * HT)
            gin_v[t] = inv * (gin_v[t] - both[r, 0:1] * (1.0 / D) - xh * (both[r, 1:2] * (1.0 / D))) + ct
            send_result(gin_v, gin_o, 1, t)
    X.send_own(0)
    X.send_own(1)
    W1.start()
    W3.start()
    X.step(1,0)
    X.send_own(2)
    X.step(1,1)
    X.step(2,0)
    gains()
    X.send_own(3)
    W2.start()
    W1.forward()
    X.step(2,1)
    C.start((1, 0))
    W3.forward()
    W1.arrived()
    C.local().wait()
    prep()
    X.step(3,0)
    X.ready(0)
    X.step(1,2)
    X.step(3,1)
    project(0)
    W3.arrived()
    W2.forward()
    X.step(2,2)
    X.step(1,3)
    attend(0)
    C.send_own(3)
    X.ready(1)
    project(1)
    hidden(0)
    hidden(1)
    attend(1)
    C.send_own(2)
    C.step(1,3)
    W2.arrived()
    C.send_own(1)
    out_part(0)
    out_part(1)
    X.step(3,2)
    A.edge(0)
    X.step(2,3)
    X.ready(2)
    project(2)
    hidden(2)
    C.step(2,3)
    attend(2)
    C.send_own(0)
    A.slot(0, 0)
    C.step(1,2)
    X.step(3,3)
    A.edge(1)
    X.ready(3)
    C.step(1,1)
    C.step(3,3)
    project(3)
    hidden(3)
    C.ready(3)
    attend(3)
    joined_back(3)
    C.step(2,2)
    A.slot(0, 1)
    C.step(2,1)
    C.step(1,0)
    turn()
    out_part(2)
    attend_back(3, 0, 2)
    A.slot(1, 0)
    A.edge(2)
    out_part(3)
    attend_back(3, 2, 4)
    C.step(3,2)
    attend_back(3, 4, 6)
    C.step(3,1)
    A.edge(3)
    C.step(2,0)
    attend_back(3, 6, 8)
    A.slot(1, 1)
    C.ready(2)
    C.ready(1)
    finish_back(3)
    norm_part(3)
    C.step(3,0)
    B.edge(3)
    A.slot(2, 0)
    C.ready(0)
    grads2()
    GD.start()
    joined_back(2)
    joined_back(1)
    joined_back(0)
    gradsu()
    GD.middle_sum()
    GO.start()
    GU.start()
    A.slot(2, 1)
    A.slot(3, 0)
    attend_back(2, 0, 2)
    attend_back(2, 2, 4)
    attend_back(2, 4, 6)
    A.slot(3, 1)
    B.slot(3, 0)
    GO.middle_sum()
    GD.sum_and_spread()
    finish_back(2)
    norm_part(2)
    out_final(1)
    B.edge(2)
    GU.middle_sum()
    attend_back(1, 0, 2)
    attend_back(1, 2, 4)
    GO.sum_and_spread()
    GD.share()
    B.slot(3, 1)
    finish_back(1)
    attend_back(0, 0, 2)
    GU.sum_and_spread()
    finish_back(0)
    gradsq()
    GQ.start()
    B.slot(2, 0)
    norm_part(1)
    B.edge(1)
    out_final(2)
    GO.share()
    GQ.middle_sum()
    B.slot(2, 1)
    GQ.sum_and_spread()
    GU.share()
    norm_part(0)
    GO.relay()
    B.edge(0)
    out_final(3)
    GD.relay()
    B.slot(1, 0)
    GU.relay()
    B.slot(1, 1)
    B.slot(0, 0)
    out_final(0)
    colsum()
    norm_final(3)
    GQ.share()
    B.slot(0, 1)
    norm_final(2)
    norm_final(1)
    norm_final(0)
    GQ.relay()
    GU.finish()
    small_on()
    GO.finish()
    grad_final(1)
    GD.finish()
    GQ.finish()
    sums_on()
    grad_final(0)

    for e in (1, 2, 3):
        landed(small_in.at[e - 1], r_small.at[e])
    small_o[...] = (small[1] + small_in[0]) + (small_in[1] + small_in[2])

    X.drain()
    C.drain()
    W1.drain()
    W3.drain()
    W2.drain()
    for d in (1, 2, 3):
        gain_copy(d).wait_send()
        for k in range(2):
            stat_copy(d, k).wait_send()
        row_copy(d).wait_send()
        sum_copy(d).wait_send()
        small_copy(d).wait_send()
        landed(sums.at[1], r_row.at[d])
    sib_small.wait_send()
    A.drain()
    B.wait_stage(1, stage)
    B.wait_stage(0, stage)
    B.drain()
    own_cols.wait()
    for t in range(4):
        end_result(out_v, out_o, 0, t)
        end_result(gin_v, gin_o, 1, t)


def layer(x, cot, wq, wu, wo, wd, seg, vec):
    toks = seg.shape[1]
    half = toks // 2
    depth = wq.shape[1]
    hc, fc = wq.shape[2] // 4, wu.shape[1] // 4
    h3 = 3 * hc
    sd = jax.ShapeDtypeStruct
    V = pltpu.VMEM
    grads = []
    for r, c in ((depth, h3), (depth, fc), (hc, depth), (fc, depth)):
        grads += [
            V((4, r, c), BF), V((4, 4, r // 8, c), BF), V((2, 4, r // 8, c), BF), V((2, 4, r // 8, c), BF),
            V((4, r // 4, c), BF),
        ]
    sems = (
        LineGather.SEMS * 2 + WeightGather.SEMS * 3 + LineReduce.SEMS * 2 + GradReduce.SEMS * 4
        + ((4,), (4,), (8,), (4, 2), (4, 2), (4,), (4,), (4,), (4,), (4,), (4,), (2, 4), (2, 4))
    )
    return pl.pallas_call(
        layer_kernel,
        name="layer",
        out_shape=(
            sd((half, depth), BF), sd((half, depth), F32), sd((8, depth), F32), sd((4, 8, h3 + fc), F32),
            sd((3, depth, 4 * hc), BF), sd((depth, 4 * fc), BF), sd((4, hc, depth), BF), sd((4, fc, depth), BF),
        ),
        in_specs=[hbm()] * 6 + [vmem()] * 2,
        out_specs=(hbm(), hbm(), vmem(), hbm(), hbm(), hbm(), hbm(), hbm()),
        scratch_shapes=[
            V((4, toks, depth), BF), V((4, toks, depth), BF), V((4, toks, depth), BF),
            V((4, depth, h3 + fc), BF), V((4, hc + fc, depth), BF),
            V((toks, hc), BF), V((toks, hc), BF), V((toks, hc), BF), V((hc, toks), BF),
            V((toks, hc), BF), V((toks, hc), BF), V((toks, fc), BF), V((toks, fc), BF),
            V((hc, toks), F32), V((hc, BT), F32), V((toks, hc), F32), V((toks, hc), F32),
            V((toks, 128), F32), V((8, toks), F32), V((8, toks), F32), V((16, toks), F32),
            V((8, toks), jnp.int32), V((4, 8, depth), F32), V((toks, h3 + fc), BF),
            V((4, 4, HT, depth), BF), V((4, 4, HT, depth), BF), V((5, 4, HT, depth), BF),
            V((4, 4, HT, depth), BF), V((4, 4, HT, depth), BF), V((5, 4, HT, depth), BF),
            V((2, 4, HT, depth), BF), V((HT, depth), F32),
            *grads,
            V((4, HT, depth), BF), V((4, HT, depth), F32),
            V((2, 8, BT), F32), V((3, 2, 8, BT), F32), V((2, 8, h3 + fc), F32), V((3, 8, h3 + fc), F32),
            V((2, 8, depth), F32), V((8, depth), F32), V((3, 8, depth), F32),
            *dmas(*sems),
        ],
        compiler_params=pltpu.CompilerParams(
            collective_id=0, has_side_effects=True, vmem_limit_bytes=62 * 2**20
        ),
    )(x, cot, wq, wu, wo, wd, seg, vec)


def per_device_sliced(
    inputs, segments, ln_gain, ln_bias, w_qkv, b_qkv, w_out, w_up, b_up, w_down, out_bias, cotangent
):
    nrow = lax.axis_size("row")
    dpart = inputs.shape[1]
    hcols = w_qkv.shape[2] // nrow
    h3 = 3 * hcols
    vec = jnp.concatenate([b_qkv.reshape(-1), b_up, ln_gain, ln_bias, out_bias]).astype(F32)[None]
    layer_out, grad_inputs, small, cols, fq, fu, fo, fd = layer(
        inputs, cotangent, w_qkv.transpose(1, 0, 2), w_up, w_out, w_down, segments, vec
    )
    cols = cols[:, 0]
    grad_b_qkv = cols[:, :h3].reshape(nrow, 3, hcols).transpose(1, 0, 2).reshape(3, -1)
    return (
        layer_out, grad_inputs, small[0], small[1],
        fq.astype(F32).transpose(1, 0, 2), grad_b_qkv,
        fo.reshape(w_out.shape).astype(F32), fu.astype(F32), cols[:, h3:].reshape(-1),
        fd.reshape(w_down.shape).astype(F32), small[2],
    )


FLOOR_INIT = -1e30


def doc_positions(labels):
    token_index = jnp.arange(labels.shape[1], dtype=jnp.int32)
    flags = jnp.concatenate(
        [jnp.ones((labels.shape[0], 1), dtype=jnp.bool_), labels[:, 1:] != labels[:, :-1]], 1
    )
    starts = lax.cummax(jnp.where(flags, token_index[None, :], 0), axis=1)
    return token_index[None, :] - starts


def rotate(tensor_in, positions):
    half_rot = ROT // 2
    inverse = 10000.0 ** (-(jnp.arange(half_rot, dtype=jnp.float32) * 2.0 / ROT))
    angles = positions.astype(jnp.float32)[:, None] * inverse[None, :]
    cosines = jnp.cos(angles)[:, None, :]
    sine_vals = jnp.sin(angles)[:, None, :]
    first_half = tensor_in[..., :half_rot]
    second_half = tensor_in[..., half_rot:ROT]
    rest_dims = tensor_in[..., ROT:]
    return jnp.concatenate(
        [
            first_half * cosines - second_half * sine_vals,
            second_half * cosines + first_half * sine_vals,
            rest_dims,
        ],
        -1,
    )


def slice_rows(array_in, first_row, row_count, axis_num=0):
    return lax.dynamic_slice_in_dim(array_in, first_row, row_count, axis_num)


def put_rows(array_in, update, first_row, axis_num=0):
    return lax.dynamic_update_slice_in_dim(array_in, update, first_row, axis_num)


def block_pairs(query_blocks, key_blocks):
    q_list = jnp.repeat(jnp.arange(query_blocks, dtype=jnp.int32), key_blocks)
    k_list = jnp.tile(jnp.arange(key_blocks, dtype=jnp.int32), query_blocks)
    return (q_list, k_list)


def per_device_general(
    inputs, segments, ln_gain, ln_bias, w_qkv, b_qkv, w_out, w_up, b_up, w_down, out_bias, cotangent
):
    local_rows, feature_cols = inputs.shape
    part_count = lax.axis_size("row")
    row_index = lax.axis_index("row")
    head_cols = w_qkv.shape[2]
    head_count = head_cols // HD
    group_seqs = segments.shape[0]
    all_rows = group_seqs * SEQ_LEN
    span = all_rows // part_count
    query_blocks = span // span
    score_scale = 1.0 / math.sqrt(HD)
    labels = (segments + (jnp.arange(group_seqs, dtype=jnp.int32) * SEQ_LEN)[:, None]).reshape(-1)
    positions = doc_positions(segments).reshape(-1)
    token_index = jnp.arange(all_rows, dtype=jnp.int32)
    my_labels = slice_rows(labels, row_index * span, span)
    my_index = slice_rows(token_index, row_index * span, span)
    my_positions = slice_rows(positions, row_index * span, span)
    float_in = inputs.astype(jnp.float32)
    ln_sums = lax.psum((jnp.sum(float_in, 1), jnp.sum(float_in * float_in, 1)), "row")
    row_mean = ln_sums[0] / D
    row_var = ln_sums[1] / D - row_mean * row_mean
    inv_std = lax.rsqrt(row_var + EPSILON)
    centred = (float_in - row_mean[:, None]) * inv_std[:, None]
    normed = (centred * ln_gain.astype(jnp.float32) + ln_bias.astype(jnp.float32)).astype(
        jnp.bfloat16
    )
    gathered_hidden = lax.all_gather(normed, "col", axis=0, tiled=True)
    first_weights = jnp.concatenate([w_qkv.reshape(feature_cols, 3 * head_cols), w_up], 1)
    first_bias = jnp.concatenate(
        [b_qkv.reshape(3 * head_cols).astype(jnp.float32), b_up.astype(jnp.float32)]
    )
    first_out = (
        lax.psum_scatter(
            jnp.dot(
                slice_rows(gathered_hidden, jnp.int32(0), lax.axis_size("row") * span),
                first_weights,
                preferred_element_type=jnp.float32,
            ).astype(jnp.bfloat16),
            "row",
            scatter_dimension=0,
            tiled=True,
        ).astype(jnp.float32)
        + first_bias
    )

    def rotate_mine(tensor_in):
        return rotate(tensor_in, my_positions)

    query_lin = first_out[:, :head_cols].reshape(span, head_count, HD)
    key_lin = first_out[:, head_cols : 2 * head_cols].reshape(span, head_count, HD)
    query = rotate_mine(query_lin).astype(jnp.bfloat16)
    key_rows = rotate_mine(key_lin).astype(jnp.bfloat16)
    value_rows = (
        first_out[:, 2 * head_cols : 3 * head_cols]
        .reshape(span, head_count, HD)
        .astype(jnp.bfloat16)
    )
    up_lin = first_out[:, 3 * head_cols :]
    activated = jax.nn.gelu(up_lin, approximate=False).astype(jnp.bfloat16)

    def over_keys(fold_step, initial):
        return fold_step(
            initial,
            (
                lax.all_gather(key_rows, "row", axis=0, tiled=True),
                lax.all_gather(value_rows, "row", axis=0, tiled=True),
            ),
            jnp.int32(0),
        )

    def key_setup(pieces, first_row):
        row_count = pieces[0].shape[0]
        piece_labels = slice_rows(labels, first_row, row_count)
        piece_index = slice_rows(token_index, first_row, row_count)
        return (row_count, span, piece_labels, piece_index)

    def block_live(piece_labels, piece_index, key_size, q_block, k_block):
        q_labels = slice_rows(my_labels, q_block * span, span)
        q_index = slice_rows(my_index, q_block * span, span)
        k_labels = slice_rows(piece_labels, k_block * key_size, key_size)
        k_index = slice_rows(piece_index, k_block * key_size, key_size)
        return (
            (jnp.max(q_index) >= jnp.min(k_index))
            & (jnp.min(q_labels) <= jnp.max(k_labels))
            & (jnp.min(k_labels) <= jnp.max(q_labels))
        )

    def block_scores(pieces, piece_labels, piece_index, key_size, q_block, k_block):
        q_start = q_block * span
        k_start = k_block * key_size
        q_labels = slice_rows(my_labels, q_start, span)
        q_index = slice_rows(my_index, q_start, span)
        k_labels = slice_rows(piece_labels, k_start, key_size)
        k_index = slice_rows(piece_index, k_start, key_size)
        q_block_rows = slice_rows(query, q_start, span)
        k_block_rows = slice_rows(pieces[0], k_start, key_size)
        v_block_rows = slice_rows(pieces[1], k_start, key_size)
        scores = (
            jnp.einsum(
                "qhd,khd->hqk", q_block_rows, k_block_rows, preferred_element_type=jnp.float32
            )
            * score_scale
        )
        allowed = (q_labels[:, None] == k_labels[None, :]) & (k_index[None, :] <= q_index[:, None])
        scores = jnp.where(allowed[None], scores, MASKED)
        return (q_start, k_start, scores, q_block_rows, k_block_rows, v_block_rows)

    def forward_piece(running, pieces, first_row):
        row_count, key_size, piece_labels, piece_index = key_setup(pieces, first_row)
        q_list, k_list = block_pairs(query_blocks, row_count // key_size)

        def forward_pair_step(current, pair_ids):
            q_block, k_block = pair_ids

            def update(inner_state):
                row_max, row_sum, row_acc = inner_state
                q_start, k_start, scores, q_block_rows, k_block_rows, v_block_rows = block_scores(
                    pieces, piece_labels, piece_index, key_size, q_block, k_block
                )
                old_max = slice_rows(row_max, q_start, span, 1)
                new_max = jnp.maximum(old_max, jnp.max(scores, -1))
                weights = jnp.exp(scores - new_max[..., None])
                keep_part = jnp.exp(old_max - new_max)
                new_sum = slice_rows(row_sum, q_start, span, 1) * keep_part + jnp.sum(weights, -1)
                added = jnp.einsum(
                    "hqk,khd->hqd",
                    weights.astype(jnp.bfloat16),
                    v_block_rows,
                    preferred_element_type=jnp.float32,
                )
                new_acc = slice_rows(row_acc, q_start, span, 1) * keep_part[..., None] + added
                return (
                    put_rows(row_max, new_max, q_start, 1),
                    put_rows(row_sum, new_sum, q_start, 1),
                    put_rows(row_acc, new_acc, q_start, 1),
                )

            def forward_unchanged(inner_state):
                return inner_state

            is_live = block_live(piece_labels, piece_index, key_size, q_block, k_block)
            return (lax.cond(is_live, update, forward_unchanged, current), None)

        result, _ = lax.scan(forward_pair_step, running, (q_list, k_list))
        return result

    forward_init = (
        jnp.full((head_count, span), FLOOR_INIT, jnp.float32),
        jnp.zeros((head_count, span), jnp.float32),
        jnp.zeros((head_count, span, HD), jnp.float32),
    )
    row_max, row_sum, row_acc = over_keys(forward_piece, forward_init)
    log_total = row_max + jnp.log(row_sum)
    attention_raw = jnp.transpose(row_acc / row_sum[..., None], (1, 0, 2)).reshape(span, head_cols)
    attended = attention_raw.astype(jnp.bfloat16)
    joined = jnp.concatenate(
        (
            lax.all_gather(attended, "row", axis=0, tiled=True),
            lax.all_gather(activated, "row", axis=0, tiled=True),
        ),
        1,
    )
    second_weights = jnp.concatenate([w_out, w_down], 0)
    partial_out = lax.psum_scatter(
        jnp.dot(
            slice_rows(joined, jnp.int32(0), lax.axis_size("col") * local_rows),
            second_weights,
            preferred_element_type=jnp.float32,
        ).astype(jnp.bfloat16),
        "col",
        scatter_dimension=0,
        tiled=True,
    ).astype(jnp.float32)
    layer_out = (float_in + partial_out + out_bias.astype(jnp.float32)).astype(jnp.bfloat16)
    grad_full = lax.all_gather(cotangent, "col", axis=0, tiled=True)
    grad_out_bias = jnp.sum(grad_full, 0, dtype=jnp.float32)
    grad_second = lax.dot_general(
        joined, grad_full, (((0,), (0,)), ((), ())), preferred_element_type=jnp.float32
    )
    branch_back = lax.psum_scatter(
        lax.dot_general(
            slice_rows(grad_full, jnp.int32(0), lax.axis_size("row") * span),
            second_weights,
            (((1,), (1,)), ((), ())),
            preferred_element_type=jnp.float32,
        ).astype(jnp.bfloat16),
        "row",
        scatter_dimension=0,
        tiled=True,
    ).astype(jnp.float32)
    d_attended = branch_back[:, :head_cols].astype(jnp.bfloat16)
    d_activated = branch_back[:, head_cols:]
    _, gelu_back = jax.vjp(lambda tensor_in: jax.nn.gelu(tensor_in, approximate=False), up_lin)
    d_up = gelu_back(d_activated)[0].astype(jnp.bfloat16)
    d_out_heads = d_attended.reshape(span, head_count, HD)
    row_delta = jnp.transpose(
        jnp.sum((d_attended.astype(jnp.float32) * attention_raw).reshape(span, head_count, HD), -1)
    )

    def backward_piece(running, pieces, first_row):
        d_query_acc, d_key_all, d_value_all = running
        row_count, key_size, piece_labels, piece_index = key_setup(pieces, first_row)
        q_list, k_list = block_pairs(query_blocks, row_count // key_size)
        zero_keys = jnp.zeros((row_count, head_count, HD), jnp.float32)

        def backward_pair_step(current, pair_ids):
            q_block, k_block = pair_ids

            def update(inner_state):
                d_query_run, d_key_run, d_value_run = inner_state
                q_start, k_start, scores, q_block_rows, k_block_rows, v_block_rows = block_scores(
                    pieces, piece_labels, piece_index, key_size, q_block, k_block
                )
                probs_full = jnp.exp(scores - slice_rows(log_total, q_start, span, 1)[..., None])
                d_out_block = slice_rows(d_out_heads, q_start, span)
                d_probs = jnp.einsum(
                    "qhd,khd->hqk", d_out_block, v_block_rows, preferred_element_type=jnp.float32
                )
                d_scores = (
                    probs_full * (d_probs - slice_rows(row_delta, q_start, span, 1)[..., None])
                ).astype(jnp.bfloat16)
                q_added = (
                    jnp.einsum(
                        "hqk,khd->qhd", d_scores, k_block_rows, preferred_element_type=jnp.float32
                    )
                    * score_scale
                )
                k_added = (
                    jnp.einsum(
                        "hqk,qhd->khd", d_scores, q_block_rows, preferred_element_type=jnp.float32
                    )
                    * score_scale
                )
                v_added = jnp.einsum(
                    "hqk,qhd->khd",
                    probs_full.astype(jnp.bfloat16),
                    d_out_block,
                    preferred_element_type=jnp.float32,
                )
                return (
                    put_rows(
                        d_query_run, slice_rows(d_query_run, q_start, span) + q_added, q_start
                    ),
                    put_rows(
                        d_key_run, slice_rows(d_key_run, k_start, key_size) + k_added, k_start
                    ),
                    put_rows(
                        d_value_run, slice_rows(d_value_run, k_start, key_size) + v_added, k_start
                    ),
                )

            def backward_unchanged(inner_state):
                return inner_state

            is_live = block_live(piece_labels, piece_index, key_size, q_block, k_block)
            return (lax.cond(is_live, update, backward_unchanged, current), None)

        scanned, _ = lax.scan(
            backward_pair_step, (d_query_acc, zero_keys, zero_keys), (q_list, k_list)
        )
        d_query_acc, key_part, value_part = scanned
        d_key_all = put_rows(d_key_all, key_part, first_row)
        d_value_all = put_rows(d_value_all, value_part, first_row)
        return (d_query_acc, d_key_all, d_value_all)

    backward_init = (
        jnp.zeros((span, head_count, HD), jnp.float32),
        jnp.zeros((all_rows, head_count, HD), jnp.float32),
        jnp.zeros((all_rows, head_count, HD), jnp.float32),
    )
    d_query_rot, d_key_total, d_value_total = over_keys(backward_piece, backward_init)
    d_key_rot, d_value_mine = (
        lax.psum_scatter(
            d_key_total.reshape(all_rows, head_cols).astype(jnp.bfloat16),
            "row",
            scatter_dimension=0,
            tiled=True,
        ).astype(jnp.float32),
        lax.psum_scatter(
            d_value_total.reshape(all_rows, head_cols).astype(jnp.bfloat16),
            "row",
            scatter_dimension=0,
            tiled=True,
        ).astype(jnp.float32),
    )
    _, query_back = jax.vjp(rotate_mine, query_lin)
    _, key_back = jax.vjp(rotate_mine, key_lin)
    d_query_lin = query_back(d_query_rot)[0].reshape(span, head_cols).astype(jnp.bfloat16)
    d_key_lin = (
        key_back(d_key_rot.reshape(span, head_count, HD))[0]
        .reshape(span, head_cols)
        .astype(jnp.bfloat16)
    )
    d_first = jnp.concatenate([d_query_lin, d_key_lin, d_value_mine.astype(jnp.bfloat16), d_up], 1)
    d_first_full = lax.all_gather(d_first, "row", axis=0, tiled=True)
    grad_first_bias = jnp.sum(d_first_full, 0, dtype=jnp.float32)
    grad_first = lax.dot_general(
        gathered_hidden, d_first_full, (((0,), (0,)), ((), ())), preferred_element_type=jnp.float32
    )
    d_normed = lax.psum_scatter(
        lax.dot_general(
            slice_rows(d_first_full, jnp.int32(0), lax.axis_size("col") * local_rows),
            first_weights,
            (((1,), (1,)), ((), ())),
            preferred_element_type=jnp.float32,
        ).astype(jnp.bfloat16),
        "col",
        scatter_dimension=0,
        tiled=True,
    ).astype(jnp.float32)
    d_centred = d_normed * ln_gain.astype(jnp.float32)
    grad_stats = lax.psum((jnp.sum(d_centred, 1), jnp.sum(d_centred * centred, 1)), "row")
    grad_inputs = inv_std[:, None] * (
        d_centred - grad_stats[0][:, None] / D - centred * grad_stats[1][:, None] / D
    ) + cotangent.astype(jnp.float32)
    summed = (
        lax.psum(grad_first.astype(jnp.bfloat16), "dp").astype(jnp.float32),
        lax.psum(grad_second.astype(jnp.bfloat16), "dp").astype(jnp.float32),
        lax.psum(grad_first_bias.astype(jnp.bfloat16), "dp").astype(jnp.float32),
        lax.psum(grad_out_bias.astype(jnp.bfloat16), "dp").astype(jnp.float32),
    )
    norm_grads = lax.psum((jnp.sum(d_normed * centred, 0), jnp.sum(d_normed, 0)), ("dp", "col"))
    grad_w_qkv = summed[0][:, : 3 * head_cols].reshape(feature_cols, 3, head_cols)
    grad_w_up = summed[0][:, 3 * head_cols :]
    grad_w_out = summed[1][:head_cols]
    grad_w_down = summed[1][head_cols:]
    grad_b_qkv = summed[2][: 3 * head_cols].reshape(3, head_cols)
    grad_b_up = summed[2][3 * head_cols :]
    return (
        layer_out,
        grad_inputs,
        norm_grads[0],
        norm_grads[1],
        grad_w_qkv,
        grad_b_qkv,
        grad_w_out,
        grad_w_up,
        grad_b_up,
        grad_w_down,
        summed[3],
    )


def solution(mesh):
    placed = (
        P(("dp", "col"), "row"),
        P("dp", None),
        P("row"),
        P("row"),
        P("row", None, "col"),
        P(None, "col"),
        P("col", "row"),
        P("row", "col"),
        P("col"),
        P("col", "row"),
        P("row"),
        P(("dp", "col"), "row"),
    )
    size = dict(mesh.shape)
    sliced = (size["dp"], size["row"], size["col"]) == (4, 4, 2)
    return jax.shard_map(
        per_device_sliced if sliced else per_device_general,
        mesh=mesh,
        in_specs=placed,
        out_specs=(
            P(("dp", "col"), "row"),
            P(("dp", "col"), "row"),
            P("row"),
            P("row"),
            P("row", None, "col"),
            P(None, "col"),
            P("col", "row"),
            P("row", "col"),
            P("col"),
            P("col", "row"),
            P("row"),
        ),
        check_vma=False,
    )
```
